128 devices in a mesh: section: 2 (over core), dp: 64 (over y, z, x).
Axes of the slice: x: 4, y: 4, z: 4, core: 2. Of those that a mesh axis runs over, the one named last changes fastest.
Arguments:
- inputs: bfloat16 [2, 4096, 768], P(None, 'dp'), may hold values from -6 to 6
- cotangent: bfloat16 [2, 4096, 768], P(None, 'dp'), may hold values from -6 to 6
- segments: int32 [2, 4096], P(None, 'dp'), may hold values from 0 to 255, never falling along the last dimension, each value on 1 to 32 neighbouring positions
- routes: int32 [2, 2, 4096, 2], P('section', None, 'dp'), may hold values from 0 to 31, as said below
- slots: int32 [2, 2, 4096, 2], P('section', None, 'dp'), may hold values from 0 to 7, as said below
- qkv_weight: bfloat16 [2, 768, 2304], P('section', 'dp'), may hold values from -0.21875 to 0.21875
- out_weight: bfloat16 [2, 768, 768], P('section', 'dp'), may hold values from -0.4375 to 0.4375
- router_weight: bfloat16 [2, 768, 32], P('section', 'dp'), may hold values from -0.15625 to 0.15625
- gain_one: bfloat16 [2, 768], P('section', 'dp'), may hold values from 0.5 to 1.5
- gain_two: bfloat16 [2, 768], P('section', 'dp'), may hold values from 0.5 to 1.5
- bias_table: bfloat16 [2, 384], P('section', 'dp'), may hold values from -3 to 3
- w_in: bfloat16 [2, 64, 768, 1536], P('section', 'dp'), may hold values from -0.21875 to 0.21875
- w_out: bfloat16 [2, 64, 1536, 768], P('section', 'dp'), may hold values from -0.109375 to 0.109375
Outputs:
- layer_out: bfloat16 [2, 2, 4096, 768], P('section', None, 'dp')
- input_grad: bfloat16 [2, 2, 4096, 768], P('section', None, 'dp')
- grad_qkv: float32 [2, 768, 2304], P('section', 'dp')
- grad_out: float32 [2, 768, 768], P('section', 'dp')
- grad_router: float32 [2, 768, 32], P('section', 'dp')
- grad_gain_one: float32 [2, 768], P('section', 'dp')
- grad_gain_two: float32 [2, 768], P('section', 'dp')
- grad_bias: float32 [2, 384], P('section', 'dp')
- grad_w_in: float32 [2, 64, 768, 1536], P('section', 'dp')
- grad_w_out: float32 [2, 64, 1536, 768], P('section', 'dp')
The draws below stay inside these ranges and needn't reach their ends.
Inputs may be any that keep to these rules, and one draw needn't show every extreme that they name: `routes`: in every layer and micro-batch, each of the 64 rows of one device names two different experts; no expert is named by more than 8 of one device's rows, and one expert, the same for every device of that layer and micro-batch, by exactly 8. In every layer and micro-batch, the rows of one device that name one expert hold the slots 0 to their count less one, each once.
All inputs are finite; a program needn't handle non-finite values.
Results may differ from the reference program's by a relative error of at most 0.04.
Values may be sent and summed in bfloat16 or wider, within the bound.
No kernel may reach another device: no remote copies, remote signals or barrier semaphores. Data moves between devices by JAX's collectives and lax.ppermute only.
A program may use at most 192 MiB of HBM per device.

```python
import math
import jax
import jax.numpy as jnp
import numpy as np
from jax import lax

D = 768
HEADS = 12
HEAD_DIM = 64
FF = 3072
HALF_FF = 1536
BUCKETS = 32
SEQ = 64
MICRO = 2
LAYERS = 2
EXPERTS = 32
TOKENS = 4096
CAP = 8
N_DP = 64


def routing_plan(key):
    mean_load = 2 * SEQ // EXPERTS
    pair_count = EXPERTS // 2
    block_count = LAYERS * MICRO * N_DP
    order_keys = jax.random.split(jax.random.fold_in(key, 11), LAYERS * MICRO)
    orders = jax.vmap(lambda inner: jax.random.permutation(inner, EXPERTS))(order_keys)
    orders = jnp.repeat(orders, N_DP, axis=0)
    spread = jax.random.randint(jax.random.fold_in(key, 12), (block_count, pair_count), 0, mean_load + 1)
    spread = spread.at[:, 0].set(mean_load)
    loads = jnp.stack([mean_load + spread, mean_load - spread], axis=2).reshape(block_count, EXPERTS)
    load_ends = jnp.cumsum(loads, axis=1)
    starts = load_ends - loads
    positions = jnp.arange(2 * SEQ)
    ranks = jnp.sum((positions[None, :, None] >= load_ends[:, None, :]).astype(jnp.int32), axis=2)
    experts_at = jnp.take_along_axis(orders, ranks, axis=1)
    slots_at = positions[None, :] - jnp.take_along_axis(starts, ranks, axis=1)
    shuffle_keys = jax.random.split(jax.random.fold_in(key, 13), block_count)
    shuffles = jax.vmap(lambda inner: jax.random.permutation(inner, SEQ))(shuffle_keys)
    picked_order = jnp.stack([shuffles, shuffles + SEQ], axis=2).reshape(block_count, 2 * SEQ)
    route_ids = jnp.take_along_axis(experts_at, picked_order, axis=1).reshape(LAYERS, MICRO, TOKENS, 2)
    slot_ids = jnp.take_along_axis(slots_at, picked_order, axis=1).reshape(LAYERS, MICRO, TOKENS, 2)
    return (route_ids.astype(jnp.int32), slot_ids.astype(jnp.int32))


def draw_routes(key, part):
    route_ids, slot_ids = routing_plan(key)
    return route_ids


def draw_slots(key, part):
    route_ids, slot_ids = routing_plan(key)
    return slot_ids


def level_of(rng, extent, pieces, least, high):
    level = 1.0
    for dim, shards_of in pieces:
        heights = jax.random.uniform(jax.random.fold_in(jax.random.fold_in(rng, 6), dim), (shards_of,), jnp.float32, least / len(pieces), high / len(pieces))
        level = level * jnp.repeat(jnp.exp(heights), extent[dim] // shards_of).reshape((-1,) + (1,) * (len(extent) - 1 - dim))
    return level


def length_profile(number_of, total, bound, slope):
    weights = [(1 << 20) // math.isqrt(grade ** slope) + 1 for grade in range(2, number_of + 1)]
    rest, given = total - bound - (number_of - 1), [1] * (number_of - 1)
    while rest > 0:
        candidates = [i for i in range(number_of - 1) if given[i] < bound]
        mass, budget = sum([weights[i] for i in candidates]), rest
        for i in candidates:
            more = min(bound - given[i], max(1, budget * weights[i] // mass), rest)
            given[i] = given[i] + more
            rest = rest - more
    return np.array([bound] + given)


def ragged(stream_key, amount, total, reach, skew):
    if amount == 2:
        one = jax.random.randint(stream_key, (), max(1, total - reach), min(reach, total - 1) + 1)
        return jnp.stack([one, total - one])
    sizes = jnp.asarray(length_profile(amount, total, reach, skew), jnp.int32)
    twos = (amount - 1) // 2
    giver, sink = sizes[1:1 + 2 * twos:2], sizes[2:2 + 2 * twos:2]
    room = jnp.minimum(giver - 1, reach - sink)
    shifted = jax.random.randint(jax.random.fold_in(stream_key, 1), (twos,), 0, 1 << 20) % (room + 1)
    sizes = sizes.at[1:1 + 2 * twos:2].set(giver - shifted).at[2:2 + 2 * twos:2].set(sink + shifted)
    return sizes[jax.random.permutation(jax.random.fold_in(stream_key, 2), amount)]


def scatter_about(rng, dims, scale, reach, shards=(), held_as=jnp.bfloat16):
    array = jax.random.normal(rng, dims, jnp.float32) * scale
    if len(shards) > 0:
        array = level_of(rng, dims, shards, -0.22, 0.18) * array
    return jnp.clip(array, min=-reach, max=reach).astype(held_as)


def setup_inputs(seed: int = 0) -> dict:
    key_list = jax.random.split(jax.random.key(seed), 14)
    return {
        "inputs": scatter_about(key_list[0], (MICRO, TOKENS, D), 1.0, 6.0, ((1, 64),)),
        "cotangent": scatter_about(key_list[1], (MICRO, TOKENS, D), 1.0, 6.0, ((1, 64),)),
        "segments": jax.vmap(lambda own: jnp.searchsorted(jnp.cumsum(ragged(own, 4 * TOKENS // SEQ, TOKENS, SEQ // 2, 1)), jnp.arange(TOKENS), side="right"))(jax.random.split(key_list[2], MICRO)).reshape((MICRO, TOKENS)).astype(jnp.int32),
        "routes": draw_routes(jax.random.fold_in(key_list[13], 71), 0),
        "slots": draw_slots(jax.random.fold_in(key_list[13], 71), 0),
        "qkv_weight": scatter_about(key_list[5], (LAYERS, D, 3 * D), D ** -0.5, 0.21875, ((0, 2), (1, 64))),
        "out_weight": scatter_about(key_list[6], (LAYERS, D, D), (D // 4) ** -0.5, 0.4375, ((0, 2), (1, 64))),
        "router_weight": scatter_about(key_list[7], (LAYERS, D, EXPERTS), (2 * D) ** -0.5, 0.15625, ((0, 2), (1, 64))),
        "gain_one": jnp.clip(1.0 + 0.1 * jax.random.normal(key_list[8], (LAYERS, D), jnp.float32), 0.5, 1.5).astype(jnp.bfloat16),
        "gain_two": jnp.clip(1.0 + 0.1 * jax.random.normal(key_list[9], (LAYERS, D), jnp.float32), 0.5, 1.5).astype(jnp.bfloat16),
        "bias_table": scatter_about(key_list[10], (LAYERS, HEADS * BUCKETS), 0.5, 3.0, ((0, 2), (1, 64))),
        "w_in": scatter_about(key_list[11], (LAYERS, N_DP, D, HALF_FF), D ** -0.5, 0.21875, ((0, 2), (1, 64))),
        "w_out": scatter_about(key_list[12], (LAYERS, N_DP, HALF_FF, D), FF ** -0.5, 0.109375, ((0, 2), (1, 64))),
    }


EPS = 1e-06
HIGHEST_PRECISION = lax.Precision.HIGHEST

@jax.custom_vjp
def low(v):
    return lax.optimization_barrier(v.astype(jnp.bfloat16)).astype(jnp.float32)

@jax.custom_vjp
def low_back(v):
    return v

def low_keep(v):
    return (low(v), None)

def low_pass(kept, grad):
    return (grad,)

def back_keep(v):
    return (v, None)

def back_low(kept, grad):
    return (low(grad),)
low.defvjp(low_keep, low_pass)
low_back.defvjp(back_keep, back_low)

def bucket_table(length, count):
    places = np.arange(length)
    distance = np.maximum(places[:, None] - places[None, :], 0)
    safe_distance = np.maximum(distance, 1)
    near_count = count // 2
    far_bucket = near_count + np.floor(np.log(safe_distance / near_count) / np.log(128.0 / near_count) * near_count).astype(np.int32)
    return np.where(distance < near_count, distance, np.minimum(far_bucket, count - 1)).astype(np.int32)

def inverse_rms(value):
    return lax.rsqrt(lax.optimization_barrier(jnp.mean(value * value, axis=-1, keepdims=True)) + EPS)

def attention_branch(normed, segment_rows, qkv_matrix, out_matrix, bias_rows):
    lowered = low(normed)
    packed = low(low_back(jnp.einsum('nsd,de->nse', lowered, qkv_matrix, precision=HIGHEST_PRECISION)))
    packed = packed.reshape(N_DP, SEQ, 3, HEADS, HEAD_DIM)
    query_rows = packed[:, :, 0]
    key_rows = packed[:, :, 1]
    value_rows = packed[:, :, 2]
    buckets = jnp.asarray(bucket_table(SEQ, BUCKETS))
    bias_scores = bias_rows.reshape(HEADS, BUCKETS)[:, buckets]
    scores = jnp.einsum('nqhc,nkhc->nhqk', query_rows, key_rows, precision=HIGHEST_PRECISION) * HEAD_DIM ** (-0.5) + bias_scores[None]
    scores = low_back(scores)
    places = jnp.arange(SEQ)
    causal = places[:, None] >= places[None, :]
    same_document = segment_rows[:, :, None] == segment_rows[:, None, :]
    allowed = (causal[None] & same_document)[:, None]
    masked = jnp.where(allowed, scores, -1e+30)
    raised = jnp.exp(masked - lax.optimization_barrier(jnp.max(masked, axis=-1, keepdims=True)))
    weights = raised / lax.optimization_barrier(jnp.sum(raised, axis=-1, keepdims=True))
    mixed = jnp.einsum('nhqk,nkhc->nqhc', low(weights), value_rows, precision=HIGHEST_PRECISION).reshape(N_DP, SEQ, D)
    mixed = low(low_back(mixed))
    return low_back(jnp.einsum('nsd,de->nse', mixed, out_matrix, precision=HIGHEST_PRECISION))

def expert_branch(normed, route_ids, slot_ids, router_matrix, first_halves, second_halves):
    lowered = low(normed)
    logits = low_back(jnp.dot(lowered, router_matrix, precision=HIGHEST_PRECISION))
    chosen = jnp.take_along_axis(logits, route_ids, axis=1)
    raised = jnp.exp(chosen - lax.optimization_barrier(jnp.max(chosen, axis=1, keepdims=True)))
    gate_values = raised / lax.optimization_barrier(jnp.sum(raised, axis=1, keepdims=True))
    source = jnp.broadcast_to((jnp.arange(TOKENS) // SEQ).astype(jnp.int32)[:, None], route_ids.shape)
    buffer = jnp.zeros((EXPERTS, N_DP, CAP, D), jnp.float32)
    buffer = buffer.at[route_ids, source, slot_ids].set(jnp.broadcast_to(lowered[:, None, :], (TOKENS, 2, D)))
    slot_rows = low_back(buffer).reshape(EXPERTS, N_DP * CAP, D)
    first_matrix = first_halves.reshape(EXPERTS, 2, D, HALF_FF).transpose(0, 2, 1, 3).reshape(EXPERTS, D, FF)
    second_matrix = second_halves.reshape(EXPERTS, FF, D)
    pre_act = low_back(jnp.einsum('erd,edf->erf', slot_rows, first_matrix, precision=HIGHEST_PRECISION))
    hidden = low(jax.nn.gelu(pre_act, approximate=True))
    result = low(low_back(jnp.einsum('erf,efd->erd', hidden, second_matrix, precision=HIGHEST_PRECISION)))
    result = result.reshape(EXPERTS, N_DP, CAP, D)
    picked = result[route_ids, source, slot_ids]
    return lax.optimization_barrier(jnp.sum(gate_values[:, :, None] * picked, axis=1))

def residual_block(hidden_in, layer_index, segment_row, route_ids, slot_ids, weights):
    qkv_w, out_w, router_w, gain_first, gain_second, bias_w, first_w, second_w = weights
    normed = hidden_in * inverse_rms(hidden_in) * gain_first[layer_index]
    attended = attention_branch(normed.reshape(N_DP, SEQ, D), segment_row.reshape(N_DP, SEQ), qkv_w[layer_index], out_w[layer_index], bias_w[layer_index])
    middle = hidden_in + attended.reshape(TOKENS, D)
    second_normed = middle * inverse_rms(middle) * gain_second[layer_index]
    return middle + expert_branch(second_normed, route_ids, slot_ids, router_w[layer_index], first_w[layer_index], second_w[layer_index])

def reference(inputs, cotangent, segments, routes, slots, qkv_weight, out_weight, router_weight, gain_one, gain_two, bias_table, w_in, w_out):
    weights = tuple((member.astype(jnp.float32) for member in (qkv_weight, out_weight, router_weight, gain_one, gain_two, bias_table, w_in, w_out)))
    start_rows = inputs.astype(jnp.float32)
    passing = jnp.zeros(inputs.shape, jnp.float32)

    def forward(start_rows, passing, weights):
        outputs = []
        handed = []
        for micro_index in range(MICRO):
            first_out = residual_block(start_rows[micro_index], 0, segments[micro_index], routes[0, micro_index], slots[0, micro_index], weights)
            handoff = low(low_back(first_out + passing[micro_index]))
            handed.append(handoff)
            outputs.append(residual_block(handoff, 1, segments[micro_index], routes[1, micro_index], slots[1, micro_index], weights))
        return (jnp.stack(outputs), jnp.stack(handed))
    final, pullback, handed = jax.vjp(forward, start_rows, passing, weights, has_aux=True)
    grad_start, grad_passing, grads = pullback(cotangent.astype(jnp.float32))
    layer_out = jnp.stack([handed, final]).astype(jnp.bfloat16)
    input_grad = jnp.stack([grad_start, grad_passing]).astype(jnp.bfloat16)
    return (layer_out, input_grad, grads[0], grads[1], grads[2], grads[3], grads[4], grads[5], grads[6], grads[7])
```

```python
import jax
import jax.numpy as jnp
import numpy as np
from jax import lax
from jax.sharding import PartitionSpec as P

BUCKETS = 32
EPS = 1e-06
F32 = jnp.float32
BF = jnp.bfloat16
SWAP = [(0, 1), (1, 0)]
NT = (((1,), (1,)), ((), ()))
TN = (((0,), (0,)), ((), ()))
HALF = 1152
PACK = 1280
OUT_HALF = 384


def bucket_table(length, count):
    places = np.arange(length)
    distance = np.maximum(places[:, None] - places[None, :], 0)
    safe_distance = np.maximum(distance, 1)
    near_count = count // 2
    far_bucket = near_count + np.floor(
        np.log(safe_distance / near_count) / np.log(128.0 / near_count) * near_count
    ).astype(np.int32)
    return np.where(distance < near_count, distance, np.minimum(far_bucket, count - 1)).astype(
        np.int32
    )


def selections():
    rows = np.zeros((768, 1024), np.float32)
    outs = np.zeros((3, 768, 1024), np.float32)
    for f in range(768):
        d, r = divmod(f, 12)
        rows[f, 16 * d + r] = 1
        outs[r % 3, f, 16 * d + 12 + r // 3] = 1
    bias = np.zeros((1024, 384), np.float32)
    for b in range(384):
        bias[16 * (b // 6) + b % 6, b] = 1
    return rows, outs, bias


def dot(a, b, dims=(((1,), (0,)), ((), ()))):
    return lax.dot_general(a, b, dims, preferred_element_type=F32)


def dot_exact(a, b, dims):
    high = a.astype(BF)
    low = (a - high.astype(F32)).astype(BF)
    return dot(high, b, dims) + dot(low, b, dims)


def inverse_rms(value):
    return lax.rsqrt(jnp.mean(value * value, axis=-1, keepdims=True) + EPS)


def norm_backward(grad_normed, normed, scale):
    return scale * (grad_normed - normed * jnp.mean(grad_normed * normed, axis=-1, keepdims=True))


def gelu_grad(u, grad):
    _, pullback = jax.vjp(lambda inner: jax.nn.gelu(inner, approximate=True), u)
    return pullback(grad)[0]


def a2a(block):
    return lax.all_to_all(block, "dp", split_axis=0, concat_axis=0, tiled=True)


def swap(block):
    return lax.ppermute(block, "section", SWAP)


def doubled(rows):
    w = rows.shape[1]
    return jnp.broadcast_to(rows.reshape(32, 1, 8, w), (32, 2, 8, w)).reshape(64, 8, w)


def halves_summed(back):
    w = back.shape[-1]
    return jnp.sum(back.reshape(32, 2, 8, w).astype(F32), axis=1).astype(BF).reshape(256, w)


def forward(h, allowed, idx, dense, consts, first):
    own, other = dense
    e_rows, e_outs, e_bias, onehot = consts
    small = own[:, HALF:]
    rows_t = dot(small, e_rows, (((0,), (1,)), ((), ())))
    gain_one, gain_two = rows_t[32:33], rows_t[33:34]
    bias = dot(small, e_bias, TN)[34].reshape(12, BUCKETS)
    bias_scores = jnp.dot(bias, onehot, precision=lax.Precision.HIGHEST).reshape(12, 64, 64)

    def ordered(mine, theirs):
        return jnp.where(
            first,
            jnp.concatenate([mine, theirs], axis=1),
            jnp.concatenate([theirs, mine], axis=1),
        )

    r1 = inverse_rms(h)
    n1 = h * r1
    a = (n1 * gain_one).astype(BF)
    a_rows = dot(a, e_rows).astype(BF)
    qkv = ordered(
        dot(a_rows, own[:, :HALF]).astype(BF), dot(a_rows, other[:, :HALF]).astype(BF)
    ).reshape(64, 3, 12, 64)
    q, k, v = qkv[:, 0], qkv[:, 1], qkv[:, 2]
    scores = jnp.einsum("qhc,khc->hqk", q, k, preferred_element_type=F32) * 0.125 + bias_scores
    masked = jnp.where(allowed[None], scores, -1e30)
    raised = jnp.exp(masked - jnp.max(masked, axis=-1, keepdims=True))
    p = raised / jnp.sum(raised, axis=-1, keepdims=True)
    pl_ = p.astype(BF)
    o = jnp.einsum("hqk,khc->qhc", pl_, v, preferred_element_type=F32).reshape(64, 768).astype(BF)
    o_rows = [dot(o, e_outs[t]).astype(BF) for t in range(3)]

    def project(block):
        return sum(
            dot(o_rows[t], block[:, OUT_HALF * t : OUT_HALF * (t + 1)]) for t in range(3)
        )

    mid = h + ordered(project(own), project(other))
    r2 = inverse_rms(mid)
    n2 = mid * r2
    c = (n2 * gain_two).astype(BF)
    c_rows = dot(c, e_rows).astype(BF)
    z = dot(c_rows, small)[:, :32]
    hot = ((idx[:, :, None] >> 3) == jnp.arange(32)[None, None, :]).astype(F32)
    chosen = jnp.sum(z[:, None, :] * hot, axis=-1)
    e = jnp.exp(chosen - jnp.max(chosen, axis=1, keepdims=True))
    gates = e / jnp.sum(e, axis=1, keepdims=True)
    slot_hot = (idx[:, :, None] == jnp.arange(256)[None, None, :]).astype(BF)
    send = dot(slot_hot[:, 0] + slot_hot[:, 1], c, TN).astype(BF)
    kept = dict(
        r1=r1, n1=n1, a_rows=a_rows, q=q, k=k, v=v, p=p, pl=pl_, o_rows=o_rows, mid=mid, r2=r2,
        n2=n2, c_rows=c_rows, hot=hot, gates=gates, slot_hot=slot_hot, gain_one=gain_one,
        gain_two=gain_two,
    )
    return kept, send


def picked_rows(kept, returned):
    return [dot(kept["slot_hot"][:, j], returned) for j in range(2)]


def combine(kept, picked):
    g = kept["gates"]
    return kept["mid"] + g[:, 0:1] * picked[0] + g[:, 1:2] * picked[1]


def grads_to_send(kept, grad):
    g, hot = kept["gates"], kept["slot_hot"]
    return (
        dot(hot[:, 0], (g[:, 0:1] * grad).astype(BF), TN)
        + dot(hot[:, 1], (g[:, 1:2] * grad).astype(BF), TN)
    ).astype(BF)


def backward(grad, kept, picked, dx_rows, dense, consts, first):
    own, other = dense
    e_rows, e_outs, e_bias, onehot = consts
    small = own[:, HALF:]
    gates, hot, slot_hot = kept["gates"], kept["hot"], kept["slot_hot"]
    dg = jnp.stack([jnp.sum(y * grad, axis=-1) for y in picked], axis=1)
    dzc = gates * (dg - jnp.sum(gates * dg, axis=1, keepdims=True))
    dz = jnp.sum(dzc[:, :, None] * hot, axis=1).astype(BF)
    dc = dot_exact(dot(dz, small[:, :32], NT), e_rows, NT)
    dc = dc + dot(slot_hot[:, 0] + slot_hot[:, 1], dx_rows)
    n2, n1 = kept["n2"], kept["n1"]
    dgain_two = jnp.sum(dc * n2, axis=0)
    dmid = grad + norm_backward(dc * kept["gain_two"], n2, kept["r2"])
    datt = dmid.astype(BF)

    def split(block, width):
        left, right = block[:, :width], block[:, width:]
        return jnp.where(first, left, right), jnp.where(first, right, left)

    datt_own, datt_other = split(datt, OUT_HALF)
    do = 0.0
    for t in range(3):
        cols = slice(OUT_HALF * t, OUT_HALF * (t + 1))
        part = dot(datt_own, own[:, cols], NT) + dot(datt_other, other[:, cols], NT)
        do = do + dot(part.astype(BF), e_outs[t], NT)
    do = do.astype(BF).reshape(64, 12, 64)
    q, k, v, p, pl_ = (kept[x] for x in ("q", "k", "v", "p", "pl"))
    dv = jnp.einsum("hqk,qhc->khc", pl_, do, preferred_element_type=F32)
    dp = jnp.einsum("qhc,khc->hqk", do, v, preferred_element_type=F32)
    ds = (p * (dp - jnp.sum(dp * p, axis=-1, keepdims=True))).astype(BF)
    dbias = dot(ds.reshape(12, 4096), onehot.astype(BF), NT).reshape(1, 384)
    dq = jnp.einsum("hqk,khc->qhc", ds, k, preferred_element_type=F32) * 0.125
    dk = jnp.einsum("hqk,qhc->khc", ds, q, preferred_element_type=F32) * 0.125
    dqkv = jnp.stack([dq, dk, dv], axis=1).reshape(64, 2304).astype(BF)
    dqkv_own, dqkv_other = split(dqkv, HALF)
    da = dot(dqkv_own, own[:, :HALF], NT) + dot(dqkv_other, other[:, :HALF], NT)
    da = dot_exact(da, e_rows, NT)
    dgain_one = jnp.sum(da * n1, axis=0)
    dh = dmid + norm_backward(da * kept["gain_one"], n1, kept["r1"])
    extra = jnp.concatenate(
        [
            dot(jnp.stack([dgain_one, dgain_two]).astype(BF), e_rows).astype(BF),
            dot(dbias.astype(BF), e_bias, NT).astype(BF),
            jnp.zeros((61, 1024), BF),
        ],
        axis=0,
    )
    left = jnp.concatenate([kept["a_rows"], *kept["o_rows"], kept["c_rows"], extra], axis=0)
    marks = jnp.zeros((64, 128), BF).at[jnp.arange(3), 32 + jnp.arange(3)].set(1)
    dz_wide = jnp.pad(dz, ((0, 0), (0, 96)))

    def right(dqkv_half, datt_half):
        blocks = [jnp.pad(dqkv_half, ((0, 0), (0, 128)))]
        for t in range(3):
            blocks.append(jnp.pad(datt_half, ((0, 0), (OUT_HALF * t, PACK - OUT_HALF * (t + 1)))))
        blocks.append(jnp.pad(dz_wide, ((0, 0), (HALF, 0))))
        blocks.append(jnp.pad(marks, ((0, 0), (HALF, 0))))
        return jnp.concatenate(blocks, axis=0)

    mine = dot(left, right(dqkv_own, datt_own), TN)
    theirs = dot(left, right(dqkv_other, datt_other), TN).astype(BF)
    total = (mine + swap(theirs).astype(F32)).astype(BF)
    return dh, total


def scattered(total):
    return jnp.sum(a2a(total.reshape(64, 16, PACK)).astype(F32), axis=0)


def body(
    inputs, cotangent, segments, routes, slots, qkv_weight, out_weight, router_weight, gain_one,
    gain_two, bias_table, w_in, w_out,
):
    section = lax.axis_index("section")
    first = section == 0

    def pick(pair):
        return jnp.where(first, pair[0], pair[1])

    def pick_other(pair):
        return jnp.where(first, pair[1], pair[0])

    rows_np, outs_np, bias_np = selections()
    onehot = (bucket_table(64, BUCKETS).reshape(1, -1) == np.arange(BUCKETS)[:, None]).astype(
        np.float32
    )
    consts = (
        jnp.asarray(rows_np, BF),
        jnp.asarray(outs_np, BF),
        jnp.asarray(bias_np, BF),
        jnp.asarray(onehot),
    )

    small = jnp.concatenate(
        [
            router_weight[0],
            gain_one[0][:, None],
            gain_two[0][:, None],
            jnp.pad(bias_table[0], (0, 6))[:, None],
        ],
        axis=1,
    )
    small = jnp.pad(small, ((0, 4), (0, 128 - 35)))

    def packed(half):
        q = qkv_weight[0][:, HALF * half : HALF * (half + 1)]
        o = out_weight[0][:, OUT_HALF * half : OUT_HALF * (half + 1)].reshape(4, HALF)
        return jnp.concatenate([jnp.concatenate([q, o], axis=0), small], axis=1)

    halves = (packed(0), packed(1))
    mine, theirs = pick(halves), swap(pick_other(halves))
    w_in_other, w_out_other = swap(w_in[0, 0]), swap(w_out[0, 0])
    flat = routes[0] * 8 + slots[0]
    flat_mine, flat_theirs = pick(flat), swap(pick_other(flat))

    def gathered(block):
        return a2a(jnp.broadcast_to(block[None], (64, 16, PACK))).reshape(1024, PACK)

    block_0, block_1 = pick((mine, theirs)), pick((theirs, mine))
    got_0 = gathered(block_0)
    dense_0 = (got_0, swap(got_0))
    got_1 = gathered(block_1)
    dense_1 = (got_1, swap(got_1))
    in_pair, out_pair = (w_in[0, 0], w_in_other), (w_out[0, 0], w_out_other)
    w_in_0, w_in_1 = pick(in_pair), pick_other(in_pair)
    w_out_0, w_out_1 = pick(out_pair), pick_other(out_pair)
    idx_pair = (flat_mine, flat_theirs)
    idx_0, idx_1 = pick(idx_pair), pick_other(idx_pair)

    h0 = pick(inputs).astype(F32)
    g1 = pick(cotangent).astype(F32)
    seg = pick(segments)
    places = np.arange(64)
    allowed = jnp.asarray(places[:, None] >= places[None, :]) & (seg[:, None] == seg[None, :])

    kept_0, send_0 = forward(h0, allowed, idx_0, dense_0, consts, first)
    x_0 = a2a(doubled(send_0)).reshape(512, 768)
    u_0 = dot(x_0, w_in_0)
    hid_0 = jax.nn.gelu(u_0, approximate=True).astype(BF)
    y_0 = dot(hid_0, w_out_0).astype(BF)
    picked_0 = picked_rows(kept_0, halves_summed(a2a(y_0.reshape(64, 8, 768))))
    out_0 = combine(kept_0, picked_0).astype(BF)

    kept_1, send_1 = forward(out_0.astype(F32), allowed, idx_1, dense_1, consts, first)
    both = jnp.concatenate([send_1, grads_to_send(kept_1, g1)], axis=1)
    arrived = a2a(doubled(both)).reshape(512, 1536)
    x_1, dy_1 = arrived[:, :768], arrived[:, 768:]
    u_1 = dot(x_1, w_in_1)
    hid_1 = jax.nn.gelu(u_1, approximate=True).astype(BF)
    y_1 = dot(hid_1, w_out_1).astype(BF)
    du_1 = gelu_grad(u_1, dot(dy_1, w_out_1, NT)).astype(BF)
    dx_1 = dot(du_1, w_in_1, NT).astype(BF)
    back = halves_summed(a2a(jnp.concatenate([y_1, dx_1], axis=1).reshape(64, 8, 1536)))
    picked_1 = picked_rows(kept_1, back[:, :768])
    out_1 = combine(kept_1, picked_1).astype(BF)
    dh_1, total_1 = backward(g1, kept_1, picked_1, back[:, 768:], dense_1, consts, first)
    ig_1 = dh_1.astype(BF)

    g0 = ig_1.astype(F32)
    dy_0 = a2a(doubled(grads_to_send(kept_0, g0))).reshape(512, 768)
    du_0 = gelu_grad(u_0, dot(dy_0, w_out_0, NT)).astype(BF)
    dx_0 = dot(du_0, w_in_0, NT).astype(BF)
    dx_rows = halves_summed(a2a(dx_0.reshape(64, 8, 768)))
    dh_0, total_0 = backward(g0, kept_0, picked_0, dx_rows, dense_0, consts, first)
    ig_0 = dh_0.astype(BF)

    acts = [(x_0, x_1), (du_0, du_1), (hid_0, hid_1), (dy_0, dy_1)]
    xs, dus, hids, dys = [
        jnp.concatenate([pick(pair), swap(pick_other(pair))], axis=0) for pair in acts
    ]
    grad_in = dot(xs, dus, TN)
    grad_out = dot(hids, dys, TN)

    red = (scattered(total_0), scattered(total_1))
    red_mine, red_theirs = pick(red), swap(pick_other(red))
    half_0, half_1 = pick((red_mine, red_theirs)), pick((red_theirs, red_mine))
    grad_qkv = jnp.concatenate([half_0[:12, :HALF], half_1[:12, :HALF]], axis=1)
    grad_dense_out = jnp.concatenate(
        [b[12:, :HALF].reshape(12, OUT_HALF) for b in (half_0, half_1)], axis=1
    )
    tail = red_mine[:12, HALF:]

    def by_micro(values):
        own, other = pick(values), swap(pick_other(values))
        return jnp.stack([pick((own, other)), pick((other, own))])[None]

    return (
        by_micro((out_0, out_1)),
        by_micro((ig_0, ig_1)),
        grad_qkv[None],
        grad_dense_out[None],
        tail[:, :32][None],
        tail[:, 32][None],
        tail[:, 33][None],
        tail[:6, 34][None],
        grad_in[None, None],
        grad_out[None, None],
    )


def solution(mesh):
    placed = (
        P(None, "dp", None),
        P(None, "dp", None),
        P(None, "dp"),
        P("section", None, "dp", None),
        P("section", None, "dp", None),
        P("section", "dp", None),
        P("section", "dp", None),
        P("section", "dp", None),
        P("section", "dp"),
        P("section", "dp"),
        P("section", "dp"),
        P("section", "dp", None, None),
        P("section", "dp", None, None),
    )
    return jax.shard_map(
        body,
        mesh=mesh,
        in_specs=placed,
        out_specs=(
            P("section", None, "dp", None),
            P("section", None, "dp", None),
            P("section", "dp", None),
            P("section", "dp", None),
            P("section", "dp", None),
            P("section", "dp"),
            P("section", "dp"),
            P("section", "dp"),
            P("section", "dp", None, None),
            P("section", "dp", None, None),
        ),
        check_vma=False,
    )
```

```python
import functools

import jax
import jax.numpy as jnp
import numpy as np
from jax import lax
from jax.experimental import pallas as pl
from jax.experimental.pallas import tpu as pltpu
from jax.sharding import PartitionSpec as P

BUCKETS = 32
EPS = 1e-06
F32 = jnp.float32
BF = jnp.bfloat16
SWAP = [(0, 1), (1, 0)]
NT = (((1,), (1,)), ((), ()))
TN = (((0,), (0,)), ((), ()))
HALF = 1152
PACK = 1280
OUT_HALF = 384
VMEM_BYTES = 24 * 2**20


def bucket_table(length, count):
    places = np.arange(length)
    distance = np.maximum(places[:, None] - places[None, :], 0)
    safe_distance = np.maximum(distance, 1)
    near_count = count // 2
    far_bucket = near_count + np.floor(
        np.log(safe_distance / near_count) / np.log(128.0 / near_count) * near_count
    ).astype(np.int32)
    return np.where(distance < near_count, distance, np.minimum(far_bucket, count - 1)).astype(
        np.int32
    )


def selections():
    rows = np.zeros((768, 1024), np.float32)
    for f in range(768):
        d, r = divmod(f, 12)
        rows[f, 16 * d + r] = 1
        rows[f, 16 * d + 12 + r // 3] = 1
    bias = np.zeros((384, 1024), np.float32)
    for b in range(384):
        bias[b, 16 * (b // 6) + b % 6] = 1
    buckets = bucket_table(64, BUCKETS)[:, 0]
    diagonals = np.zeros((128, 384), np.float32)
    for delta in range(64):
        diagonals[63 - delta, buckets[delta] :: BUCKETS] = 1
    toeplitz = np.zeros((384, 128), np.float32)
    for delta in range(64):
        toeplitz[buckets[delta] :: BUCKETS, (128 - delta) % 128] = 1
    return rows, bias, diagonals, np.eye(64)[::-1], toeplitz


def dot(a, b, dims=(((1,), (0,)), ((), ()))):
    return lax.dot_general(a, b, dims, preferred_element_type=F32)


def inverse_rms(value):
    return lax.rsqrt(jnp.mean(value * value, axis=-1, keepdims=True) + EPS)


def norm_backward(grad_normed, normed, scale):
    return scale * (grad_normed - normed * jnp.mean(grad_normed * normed, axis=-1, keepdims=True))


def a2a(block):
    return lax.all_to_all(block, "dp", split_axis=0, concat_axis=0, tiled=True)


def swap(block):
    return lax.ppermute(block, "section", SWAP)


def lanes(rows, width):
    return lax.broadcasted_iota(jnp.int32, (rows, width), 1)


def ordered(first, mine, theirs):
    return jnp.concatenate(
        [lax.select(first, mine, theirs), lax.select(first, theirs, mine)], axis=1
    )


def split(first, block, width):
    left, right = block[:, :width], block[:, width:]
    return lax.select(first, left, right), lax.select(first, right, left)


def packed_rows():
    return lax.rem(lanes(1, 1024), 16) < 12


def thirds(o):
    third = lax.rem(lanes(1, 768), 3)
    return [jnp.where(third == t, o, 0.0) for t in range(3)]


def spread(value, e):
    return jnp.where(packed_rows(), dot(value, e), 0.0)


def collected(value, e):
    value = jnp.where(packed_rows(), value, 0.0)
    high = value.astype(BF)
    low = (value - high.astype(F32)).astype(BF)
    both = dot(jnp.concatenate([high, low], axis=0), e, NT)
    return both[:64] + both[64:]


def slot_mask(idx):
    row = lanes(64, 512)
    return ((row >> 4) * 8 + (row & 7) == idx).astype(F32).astype(BF)


def slot_mask_rows(idx_row):
    row = lax.broadcasted_iota(jnp.int32, (512, 64), 0)
    return ((row >> 4) * 8 + (row & 7) == idx_row).astype(F32).astype(BF)


def mixed_out(mid, gates, idx, back):
    out = mid
    for j in range(2):
        picked = dot(slot_mask(idx[:, j : j + 1]), back)
        out = out + gates[:, j : j + 1] * picked
    return out


def pair_masks():
    low = (lanes(1, 128) < 64).astype(F32).astype(BF)
    return low, (1.0 - low.astype(F32)).astype(BF)


def stacked(pair):
    low, high = pair_masks()
    return jnp.concatenate([pair * low, pair * high], axis=0)


def unstacked(both):
    return jnp.where(lanes(1, 128) < 64, both[:64], both[64:])


def bias_scores(row, toeplitz):
    head = lax.broadcasted_iota(jnp.int32, (16, 384), 0)
    table = jnp.where(head == lanes(16, 384) // 32, row, 0.0).astype(BF)
    table = dot(table, toeplitz)
    heads = []
    for j in range(12):
        wide = jnp.broadcast_to(table[j : j + 1], (64, 128))
        heads.append(pltpu.roll(wide, 0, 1, stride=1, stride_axis=0)[:, :64])
    return jnp.concatenate(heads, axis=0)


def forward_kernel(
    first_ref, *refs, entering,
):
    if entering:
        (h_ref, own, other, e_ref, b_ref, toeplitz, allowed, idx, idx_t,
         h_out, qkv_ref, p_ref, left, mid_ref, gate_ref, gains, send) = refs
        h = h_ref[...].astype(F32)
    else:
        (mid_0, gate_0, idx_0, back_0, grad, own, other, e_ref, b_ref, toeplitz, allowed, idx,
         idx_t, h_out, qkv_ref, p_ref, left, mid_ref, gate_ref, gains, send) = refs
        h = mixed_out(mid_0[...], gate_0[...], idx_0[...], back_0[...]).astype(BF).astype(F32)
    first = first_ref[0] == 1
    h_out[...] = h.astype(BF)
    e = e_ref[...]
    small = own[:, HALF:]
    small_t = small.astype(F32).T[32:48].astype(BF)
    gains[...] = dot(small_t, e, NT)
    bias = bias_scores(dot(small_t, b_ref[...], NT)[2:3], toeplitz[...])
    a = (h * inverse_rms(h) * gains[0:1, :]).astype(BF)
    a_rows = spread(a, e).astype(BF)
    left[0:64, :] = a_rows
    qkv = ordered(
        first,
        dot(a_rows, own[:, :HALF]).astype(BF),
        dot(a_rows, other[:, :HALF]).astype(BF),
    )
    qkv_ref[...] = qkv
    scores = []
    for pair in range(6):
        at = 128 * pair
        scores.append(dot(stacked(qkv[:, at : at + 128]), qkv[:, 768 + at : 896 + at], NT))
    s = jnp.concatenate(scores, axis=0) * 0.125 + bias
    masked = jnp.where(jnp.concatenate([allowed[...]] * 12, axis=0) > 0, s, -1e30)
    raised = jnp.exp(masked - jnp.max(masked, axis=-1, keepdims=True))
    p = raised / jnp.sum(raised, axis=-1, keepdims=True)
    p_ref[...] = p
    p_low = p.astype(BF)
    outs = []
    for pair in range(6):
        at = 128 * pair
        outs.append(unstacked(dot(p_low[at : at + 128], qkv[:, 1536 + at : 1664 + at])))
    o = jnp.concatenate(outs, axis=1)
    o_rows = jnp.where(
        packed_rows(), 0.0, dot(jnp.concatenate(thirds(o), axis=0).astype(BF), e)
    ).astype(BF)
    left[64:256, :] = o_rows

    def project(block):
        return sum(
            dot(o_rows[64 * t : 64 * t + 64], block[:, OUT_HALF * t : OUT_HALF * (t + 1)])
            for t in range(3)
        )

    mid = h + ordered(first, project(own), project(other))
    mid_ref[...] = mid
    c = (mid * inverse_rms(mid) * gains[1:2, :]).astype(BF)
    c_rows = spread(c, e).astype(BF)
    left[256:320, :] = c_rows
    z = dot(c_rows, small)
    chosen = [
        jnp.sum(jnp.where(lanes(64, 128) == (idx[:, j : j + 1] >> 3), z, 0.0), axis=1, keepdims=True)
        for j in range(2)
    ]
    top = jnp.maximum(chosen[0], chosen[1])
    e0, e1 = jnp.exp(chosen[0] - top), jnp.exp(chosen[1] - top)
    g0, g1 = e0 / (e0 + e1), e1 / (e0 + e1)
    gate_ref[...] = jnp.concatenate([g0, g1], axis=1)
    hot = [slot_mask_rows(idx_t[j : j + 1, :]) for j in range(2)]
    send[:, 0:768] = dot(hot[0] + hot[1], c).astype(BF)
    if not entering:
        g = grad[...].astype(F32)
        grads = jnp.concatenate([(g0 * g).astype(BF), (g1 * g).astype(BF)], axis=0)
        send[:, 768:1536] = dot(jnp.concatenate(hot, axis=1), grads).astype(BF)


def backward_kernel(first_ref, *refs, leaving):
    if leaving:
        (grad, back_y, back_dx, idx_ref, gate_ref, h_ref, mid_ref, qkv_ref, p_ref, own,
         other, e_ref, gains, b_ref, diag_ref, flip_ref,
         ig_ref, extra, own_grads, other_grads) = refs
        y, dx = back_y[...], back_dx[...]
    else:
        (grad, back, idx_ref, gate_ref, h_ref, mid_ref, qkv_ref, p_ref, own,
         other, e_ref, gains, b_ref, diag_ref, flip_ref, gate_0, idx_0,
         ig_ref, extra, own_grads, other_grads, out_ref, send) = refs
        y, dx = back[:, 0:768], back[:, 768:1536]
    first = first_ref[0] == 1
    e = e_ref[...]
    g, gates, idx = grad[...].astype(F32), gate_ref[...], idx_ref[...]
    hot = [slot_mask(idx[:, j : j + 1]) for j in range(2)]
    picked = [dot(hot[j], y) for j in range(2)]
    mid = mid_ref[...]
    g0, g1 = gates[:, 0:1], gates[:, 1:2]
    if not leaving:
        out_ref[...] = (mid + g0 * picked[0] + g1 * picked[1]).astype(BF)
    dg = [jnp.sum(picked[j] * g, axis=1, keepdims=True) for j in range(2)]
    mean = g0 * dg[0] + g1 * dg[1]
    lane = lanes(64, 128)
    dz = jnp.where(lane == (idx[:, 0:1] >> 3), g0 * (dg[0] - mean), 0.0) + jnp.where(
        lane == (idx[:, 1:2] >> 3), g1 * (dg[1] - mean), 0.0
    )
    dz = dz.astype(BF)
    dc = collected(dot(dz, own[:, HALF:], NT), e) + dot(hot[0] + hot[1], dx)
    r2 = inverse_rms(mid)
    n2 = mid * r2
    dgain_two = jnp.sum(dc * n2, axis=0, keepdims=True)
    dmid = g + norm_backward(dc * gains[1:2, :], n2, r2)
    datt = dmid.astype(BF)
    datt_own, datt_other = split(first, datt, OUT_HALF)
    parts = []
    for t in range(3):
        cols = slice(OUT_HALF * t, OUT_HALF * (t + 1))
        parts.append(dot(datt_own, own[:, cols], NT) + dot(datt_other, other[:, cols], NT))
    parts = jnp.where(packed_rows(), 0.0, jnp.concatenate(parts, axis=0)).astype(BF)
    parts = dot(parts, e, NT)
    third = lax.rem(lanes(1, 768), 3)
    do = jnp.where(third == 0, parts[:64], jnp.where(third == 1, parts[64:128], parts[128:]))
    do = do.astype(BF)
    dos = [stacked(do[:, 128 * j : 128 * j + 128]) for j in range(6)]
    p = p_ref[...]
    p_low = p.astype(BF)
    qkv = qkv_ref[...]
    dp = jnp.concatenate(
        [dot(dos[j], qkv[:, 1536 + 128 * j : 1664 + 128 * j], NT) for j in range(6)], axis=0
    )
    ds = (p * (dp - jnp.sum(dp * p, axis=-1, keepdims=True))).astype(BF)
    dq, dk, dv, sums = [], [], [], []
    for j in range(6):
        at = 128 * j
        ds_pair = ds[at : at + 128]
        dv.append(dot(p_low[at : at + 128], dos[j], TN))
        dq.append(unstacked(dot(ds_pair, qkv[:, 768 + at : 896 + at])) * 0.125)
        dk.append(dot(ds_pair, stacked(qkv[:, at : at + 128]), TN) * 0.125)
        for half in range(2):
            turned = dot(flip_ref[...], ds_pair[64 * half : 64 * half + 64])
            turned = jnp.concatenate([turned, jnp.zeros((64, 64), F32)], axis=1)
            turned = pltpu.roll(turned, 0, 1, stride=1, stride_axis=0)
            sums.append(jnp.sum(turned, axis=0, keepdims=True))
    sums = jnp.concatenate(sums + [jnp.zeros((4, 128), F32)], axis=0)
    high = sums.astype(BF)
    low = (sums - high.astype(F32)).astype(BF)
    dbias = dot(high, diag_ref[...]) + dot(low, diag_ref[...])
    head = lax.broadcasted_iota(jnp.int32, (16, 384), 0)
    dbias = jnp.sum(jnp.where(head == lanes(16, 384) // 32, dbias, 0.0), axis=0, keepdims=True)
    dqkv = jnp.concatenate(dq + dk + dv, axis=1).astype(BF)
    dqkv_own, dqkv_other = split(first, dqkv, HALF)
    da = collected(dot(dqkv_own, own[:, :HALF], NT) + dot(dqkv_other, other[:, :HALF], NT), e)
    h = h_ref[...].astype(F32)
    r1 = inverse_rms(h)
    n1 = h * r1
    dgain_one = jnp.sum(da * n1, axis=0, keepdims=True)
    ig = (dmid + norm_backward(da * gains[0:1, :], n1, r1)).astype(BF)
    ig_ref[...] = ig
    if not leaving:
        g = ig.astype(F32)
        grads = jnp.concatenate(
            [(gate_0[:, j : j + 1] * g).astype(BF) for j in range(2)], axis=0
        )
        rows = jnp.concatenate([slot_mask_rows(idx_0[j : j + 1, :]) for j in range(2)], axis=1)
        send[...] = dot(rows, grads).astype(BF)
    row = lax.broadcasted_iota(jnp.int32, (16, 1), 0)
    both = jnp.where(row == 0, dgain_one, jnp.where(row == 1, dgain_two, 0.0)).astype(BF)
    dbias = jnp.where(row == 2, dbias, 0.0).astype(BF)
    extra[...] = (spread(both, e) + dot(dbias, b_ref[...])).astype(BF)
    for ref, dqkv_half, datt_half in (
        (own_grads, dqkv_own, datt_own),
        (other_grads, dqkv_other, datt_other),
    ):
        ref[:, 0:HALF] = dqkv_half
        ref[:, HALF:1536] = datt_half
        ref[:, 1536:1664] = dz


def call(kernel, args, outs, flops):
    specs = [pl.BlockSpec(memory_space=pltpu.SMEM)]
    specs += [pl.BlockSpec(memory_space=pltpu.VMEM)] * (len(args) - 1)
    return pl.pallas_call(
        kernel,
        in_specs=specs,
        out_specs=[pl.BlockSpec(memory_space=pltpu.VMEM)] * len(outs),
        out_shape=[jax.ShapeDtypeStruct(*out) for out in outs],
        compiler_params=pltpu.CompilerParams(vmem_limit_bytes=VMEM_BYTES),
        cost_estimate=pl.CostEstimate(flops=flops, bytes_accessed=12000000, transcendentals=50000),
    )(*args)


KEPT = [
    ((64, 768), BF),
    ((64, 2304), BF),
    ((768, 64), F32),
    ((320, 1024), BF),
    ((64, 768), F32),
    ((64, 2), F32),
    ((16, 768), F32),
]


def totals_block(refs, out, at):
    left, extra, grads, left_t, extra_t, grads_t = refs
    cols = slice(256 * at, 256 * at + 256)
    grads = jnp.concatenate([grads[...], grads_t[...]], axis=0)

    def rows(lo, hi):
        return jnp.concatenate([left[lo:hi, cols], left_t[lo:hi, cols]], axis=0)

    main = dot(rows(0, 64), grads[:, :HALF], TN)
    outs = [
        dot(rows(64 + 64 * t, 128 + 64 * t), grads[:, HALF:1536], TN) for t in range(3)
    ]
    marks = lax.broadcasted_iota(jnp.int32, (16, 128), 0) + 32 == lanes(16, 128)
    marks = ((lax.broadcasted_iota(jnp.int32, (16, 128), 0) < 3) & marks).astype(F32).astype(BF)
    rest = dot(
        jnp.concatenate([rows(256, 320), extra[:, cols], extra_t[:, cols]], axis=0),
        jnp.concatenate([grads[:, 1536:], marks, marks], axis=0),
        TN,
    )
    main = main + jnp.concatenate(outs, axis=1)
    block = jnp.concatenate([main, rest], axis=1).astype(BF)
    out[16 * at : 16 * at + 16, :, :] = block.reshape(16, 16, PACK)


def totals_early(*refs):
    for at in range(4):
        totals_block(refs[:6], refs[6], at)


def totals_late(*refs):
    early, out, held, sems = refs[6:]
    moved = pltpu.make_async_copy(early, out.at[:, 16:32, :], sems.at[4])
    moved.start()
    copies = []
    for at in range(4):
        totals_block(refs[:6], held, at)
        part = slice(16 * at, 16 * at + 16)
        copies.append(
            pltpu.make_async_copy(held.at[part], out.at[part, 0:16, :], sems.at[at])
        )
        copies[-1].start()
    for copy in copies:
        copy.wait()
    moved.wait()


def dense_totals(kernel, operands, early=None):
    left, extra, own_grads, other_grads = operands
    args = [left, extra, own_grads, swap(left), swap(extra), swap(other_grads)]
    specs = [pl.BlockSpec(memory_space=pltpu.VMEM)] * 6
    scratch, rows, place = [], 16, pltpu.VMEM
    if early is not None:
        args.append(early)
        specs.append(pl.BlockSpec(memory_space=pl.ANY))
        scratch = [pltpu.VMEM((64, 16, PACK), BF), pltpu.SemaphoreType.DMA((5,))]
        rows, place = 32, pl.ANY
    return pl.pallas_call(
        kernel,
        in_specs=specs,
        out_specs=pl.BlockSpec(memory_space=place),
        out_shape=jax.ShapeDtypeStruct((64, rows, PACK), BF),
        scratch_shapes=scratch,
        compiler_params=pltpu.CompilerParams(vmem_limit_bytes=VMEM_BYTES),
        cost_estimate=pl.CostEstimate(
            flops=1800000000, bytes_accessed=6000000, transcendentals=0
        ),
    )(*args)


def pack_kernel(first_ref, qkv, out, router, one, two, bias, mine, send):
    first = first_ref[0] == 1
    on_diagonal = lax.broadcasted_iota(jnp.int32, (12, 12), 0) == lanes(12, 12)

    def column(ref, width):
        wide = jnp.broadcast_to(ref[...].astype(F32), (12, width))
        return jnp.sum(jnp.where(on_diagonal[:, :width], wide, 0.0), axis=1, keepdims=True)

    lane = lanes(12, 128)
    rest = jnp.concatenate([router[0].astype(F32), jnp.zeros((12, 96), F32)], axis=1)
    for at, value in ((32, column(one, 12)), (33, column(two, 12)), (34, column(bias, 6))):
        rest = jnp.where(lane == at, value, rest)
    rest = jnp.concatenate([rest, jnp.zeros((4, 128), F32)], axis=0)
    outs = out[0].astype(F32)
    blocks = []
    for half in range(2):
        cols = slice(OUT_HALF * half, OUT_HALF * (half + 1))
        thin = [
            jnp.concatenate([outs[3 * j + t : 3 * j + t + 1, cols] for j in range(4)], axis=0)
            for t in range(3)
        ]
        rows = jnp.concatenate(
            [qkv[0, :, HALF * half : HALF * (half + 1)].astype(F32), jnp.concatenate(thin, axis=1)],
            axis=0,
        )
        blocks.append(jnp.concatenate([rows, rest], axis=1).astype(BF))
    mine[...] = lax.select(first, blocks[0], blocks[1])
    send[...] = lax.select(first, blocks[1], blocks[0])


def gelu_parts(u):
    inner = 0.7978845608028654 * (u + 0.044715 * (u * u * u))
    t = jnp.tanh(inner)
    half = 0.5 * (1.0 + t)
    slope = 0.7978845608028654 * (1.0 + 3 * 0.044715 * (u * u))
    return u * half, half + 0.5 * u * (1.0 - t * t) * slope


def load_weights(chosen, mine, theirs, held, sems):
    for cond, refs in ((chosen, mine), (jnp.logical_not(chosen), theirs)):

        @pl.when(cond)
        def _(refs=refs):
            for j in range(2):
                pltpu.make_async_copy(refs[j], held[j], sems.at[j]).start()

    return [pltpu.make_async_copy(mine[j], held[j], sems.at[j]) for j in range(2)]


CHUNK = 512


def expert_forward(flag, x, in_mine, in_theirs, out_mine, out_theirs, y, hid, slope, w1, w2, sems):
    copies = load_weights(
        flag[0] == 1, (in_mine, out_mine), (in_theirs, out_theirs), (w1, w2), sems
    )
    copies[0].wait()
    total = None
    for at in range(0, 1536, CHUNK):
        cols = slice(at, at + CHUNK)
        value, grad = gelu_parts(dot(x[...], w1[:, cols]))
        value = value.astype(BF)
        hid[:, cols] = value
        slope[:, cols] = grad.astype(BF)
        if at == 0:
            copies[1].wait()
        part = dot(value, w2[cols, :])
        total = part if total is None else total + part
    y[...] = total.astype(BF)


def expert_both(
    flag, arrived, in_mine, in_theirs, out_mine, out_theirs, back, hid, du, w1, w2, sems
):
    copies = load_weights(
        flag[0] == 0, (in_mine, out_mine), (in_theirs, out_theirs), (w1, w2), sems
    )
    x, dy = arrived[:, 0:768], arrived[:, 768:1536]
    copies[0].wait()
    total, total_dx = None, None
    for at in range(0, 1536, CHUNK):
        cols = slice(at, at + CHUNK)
        value, grad = gelu_parts(dot(x, w1[:, cols]))
        value = value.astype(BF)
        hid[:, cols] = value
        if at == 0:
            copies[1].wait()
        part = dot(value, w2[cols, :])
        pre = (dot(dy, w2[cols, :], NT) * grad).astype(BF)
        du[:, cols] = pre
        part_dx = dot(pre, w1[:, cols], NT)
        total = part if total is None else total + part
        total_dx = part_dx if total_dx is None else total_dx + part_dx
    back[:, 0:768] = total.astype(BF)
    back[:, 768:1536] = total_dx.astype(BF)


def expert_backward(
    flag, dy, slope, in_mine, in_theirs, out_mine, out_theirs, dx, du, w1, w2, sems
):
    copies = load_weights(
        flag[0] == 1, (in_mine, out_mine), (in_theirs, out_theirs), (w1, w2), sems
    )
    copies[1].wait()
    total = None
    for at in range(0, 1536, CHUNK):
        cols = slice(at, at + CHUNK)
        pre = (dot(dy[...], w2[cols, :], NT) * slope[:, cols].astype(F32)).astype(BF)
        du[:, cols] = pre
        if at == 0:
            copies[0].wait()
        part = dot(pre, w1[:, cols], NT)
        total = part if total is None else total + part
    dx[...] = total.astype(BF)


def call_expert(kernel, flag, acts, weights, outs, flops):
    specs = [pl.BlockSpec(memory_space=pltpu.SMEM)]
    specs += [pl.BlockSpec(memory_space=pltpu.VMEM)] * len(acts)
    specs += [pl.BlockSpec(memory_space=pl.ANY)] * 4
    return pl.pallas_call(
        kernel,
        in_specs=specs,
        out_specs=[pl.BlockSpec(memory_space=pltpu.VMEM)] * len(outs),
        out_shape=[jax.ShapeDtypeStruct(out, BF) for out in outs],
        scratch_shapes=[
            pltpu.VMEM((768, 1536), BF),
            pltpu.VMEM((1536, 768), BF),
            pltpu.SemaphoreType.DMA((2,)),
        ],
        compiler_params=pltpu.CompilerParams(vmem_limit_bytes=VMEM_BYTES),
        cost_estimate=pl.CostEstimate(
            flops=flops, bytes_accessed=10000000, transcendentals=800000
        ),
    )(flag, *acts, *weights)


def body(
    inputs, cotangent, segments, routes, slots, qkv_weight, out_weight, router_weight, gain_one,
    gain_two, bias_table, w_in, w_out,
):
    section = lax.axis_index("section")
    first = section == 0

    def pick(pair):
        return jnp.where(first, pair[0], pair[1])

    def pick_other(pair):
        return jnp.where(first, pair[1], pair[0])

    e, b_rows, diagonals, flip, toeplitz = (jnp.asarray(x, BF) for x in selections())
    flag = first.astype(jnp.int32).reshape(1)
    mine, theirs = call(
        pack_kernel,
        (flag, qkv_weight, out_weight, router_weight, gain_one, gain_two, bias_table),
        [((16, PACK), BF)] * 2,
        0,
    )
    theirs = swap(theirs)
    w_in_other, w_out_other = swap(w_in[0, 0]), swap(w_out[0, 0])
    flat = routes[0] * 8 + slots[0]
    flat_mine, flat_theirs = pick(flat), swap(pick_other(flat))

    def gathered(block):
        return a2a(jnp.broadcast_to(block[None], (64, 16, PACK))).reshape(1024, PACK)

    block_0, block_1 = pick((mine, theirs)), pick((theirs, mine))
    got_0 = gathered(block_0)
    dense_0 = (got_0, swap(got_0))
    got_1 = lax.all_gather(block_1, "dp", axis=0, tiled=True)
    weights = (w_in[0, 0], w_in_other, w_out[0, 0], w_out_other)
    idx_pair = (flat_mine, flat_theirs)
    idx_0, idx_1 = pick(idx_pair), pick_other(idx_pair)

    g1 = pick(cotangent)
    seg = pick(segments)
    places = np.arange(64)
    allowed = jnp.asarray(places[:, None] >= places[None, :]) & (seg[:, None] == seg[None, :])

    allowed = allowed.astype(F32)
    h_0, qkv_0, p_0, left_0, mid_0, gate_0, gains_0, send_0 = call(
        functools.partial(forward_kernel, entering=True),
        (flag, pick(inputs), *dense_0, e, b_rows, toeplitz, allowed, idx_0, idx_0.T),
        KEPT + [((512, 768), BF)],
        500000000,
    )
    x_0 = a2a(send_0.reshape(64, 8, 768)).reshape(512, 768)
    y_0, hid_0, slope_0 = call_expert(
        expert_forward, flag, (x_0,), weights, [(512, 768), (512, 1536), (512, 1536)], 2500000000
    )
    got_1, y_0 = lax.optimization_barrier((got_1, y_0))
    dense_1 = (got_1, swap(got_1))
    back_0 = a2a(y_0.reshape(64, 8, 768)).reshape(512, 768)

    h_1, qkv_1, p_1, left_1, mid_1, gate_1, gains_1, send_1 = call(
        functools.partial(forward_kernel, entering=False),
        (flag, mid_0, gate_0, idx_0, back_0, g1, *dense_1, e, b_rows, toeplitz, allowed,
         idx_1, idx_1.T),
        KEPT + [((512, 1536), BF)],
        700000000,
    )
    arrived = a2a(send_1.reshape(64, 8, 1536)).reshape(512, 1536)
    x_1, dy_1 = arrived[:, :768], arrived[:, 768:]
    back_1, hid_1, du_1 = call_expert(
        expert_both, flag, (arrived,), weights, [(512, 1536)] * 3, 5000000000
    )
    back_1 = a2a(back_1.reshape(64, 8, 1536)).reshape(512, 1536)
    operands = [((16, 1024), BF), ((64, 1664), BF), ((64, 1664), BF)]
    ig_1, extra_1, own_1, other_1, out_1, send_0 = call(
        functools.partial(backward_kernel, leaving=False),
        (flag, g1, back_1, idx_1, gate_1, h_1, mid_1, qkv_1, p_1, *dense_1, e, gains_1,
         b_rows, diagonals, flip, gate_0, idx_0.T),
        [((64, 768), BF)] + operands + [((64, 768), BF), ((512, 768), BF)],
        1000000000,
    )

    total_1 = dense_totals(totals_early, (left_1, extra_1, own_1, other_1))

    dy_0 = a2a(send_0.reshape(64, 8, 768)).reshape(512, 768)
    dx_0, du_0 = call_expert(
        expert_backward, flag, (dy_0, slope_0), weights, [(512, 768), (512, 1536)], 2500000000
    )
    dx_rows = a2a(dx_0.reshape(64, 8, 768)).reshape(512, 768)
    ig_0, extra_0, own_0, other_0 = call(
        functools.partial(backward_kernel, leaving=True),
        (flag, ig_1, back_0, dx_rows, idx_0, gate_0, h_0, mid_0, qkv_0, p_0, *dense_0, e,
         gains_0, b_rows, diagonals, flip),
        [((64, 768), BF)] + operands,
        1000000000,
    )
    totals = a2a(dense_totals(totals_late, (left_0, extra_0, own_0, other_0), total_1))

    acts = [(x_0, x_1), (du_0, du_1), (hid_0, hid_1), (dy_0, dy_1)]
    xs, dus, hids, dys = [
        jnp.concatenate([pick(pair), swap(pick_other(pair))], axis=0) for pair in acts
    ]
    grad_in = dot(xs, dus, TN)
    grad_out = dot(hids, dys, TN)

    totals, grad_in, grad_out = lax.optimization_barrier((totals, grad_in, grad_out))
    summed = jnp.sum(totals.astype(F32), axis=0)
    red = (summed[:16], summed[16:])
    red_mine, red_theirs = pick(red), swap(pick_other(red))
    half_0, half_1 = pick((red_mine, red_theirs)), pick((red_theirs, red_mine))
    grad_qkv = jnp.concatenate([half_0[:12, :HALF], half_1[:12, :HALF]], axis=1)
    grad_dense_out = jnp.concatenate(
        [b[12:, :HALF].reshape(12, OUT_HALF) for b in (half_0, half_1)], axis=1
    )
    tail = red_mine[:12, HALF:]

    def by_micro(values):
        own, other = pick(values), swap(pick_other(values))
        return jnp.stack([pick((own, other)), pick((other, own))])[None]

    return (
        by_micro((h_1, out_1)),
        by_micro((ig_0, ig_1)),
        grad_qkv[None],
        grad_dense_out[None],
        tail[:, :32][None],
        tail[:, 32][None],
        tail[:, 33][None],
        tail[:6, 34][None],
        grad_in[None, None],
        grad_out[None, None],
    )


def solution(mesh):
    placed = (
        P(None, "dp", None),
        P(None, "dp", None),
        P(None, "dp"),
        P("section", None, "dp", None),
        P("section", None, "dp", None),
        P("section", "dp", None),
        P("section", "dp", None),
        P("section", "dp", None),
        P("section", "dp"),
        P("section", "dp"),
        P("section", "dp"),
        P("section", "dp", None, None),
        P("section", "dp", None, None),
    )
    return jax.shard_map(
        body,
        mesh=mesh,
        in_specs=placed,
        out_specs=(
            P("section", None, "dp", None),
            P("section", None, "dp", None),
            P("section", "dp", None),
            P("section", "dp", None),
            P("section", "dp", None),
            P("section", "dp"),
            P("section", "dp"),
            P("section", "dp"),
            P("section", "dp", None, None),
            P("section", "dp", None, None),
        ),
        check_vma=False,
    )
```

```python
import functools

import jax
import jax.numpy as jnp
import numpy as np
from jax import lax
from jax.experimental import pallas as pl
from jax.experimental.pallas import tpu as pltpu
from jax.sharding import PartitionSpec as P

BUCKETS = 32
EPS = 1e-06
F32 = jnp.float32
BF = jnp.bfloat16
SWAP = [(0, 1), (1, 0)]
NT = (((1,), (1,)), ((), ()))
TN = (((0,), (0,)), ((), ()))
HALF = 1152
PACK = 1280
OUT_HALF = 384
VMEM_BYTES = 40 * 2**20
SEMS = 40
WIDE = slice(0, 768)
CHUNK = 512


def bucket_table(length, count):
    places = np.arange(length)
    distance = np.maximum(places[:, None] - places[None, :], 0)
    safe_distance = np.maximum(distance, 1)
    near_count = count // 2
    far_bucket = near_count + np.floor(
        np.log(safe_distance / near_count) / np.log(128.0 / near_count) * near_count
    ).astype(np.int32)
    return np.where(distance < near_count, distance, np.minimum(far_bucket, count - 1)).astype(
        np.int32
    )


def selections():
    rows = np.zeros((768, 1024), np.float32)
    for f in range(768):
        d, r = divmod(f, 12)
        rows[f, 16 * d + r] = 1
        rows[f, 16 * d + 12 + r // 3] = 1
    bias = np.zeros((384, 1024), np.float32)
    for b in range(384):
        bias[b, 16 * (b // 6) + b % 6] = 1
    buckets = bucket_table(64, BUCKETS)[:, 0]
    diagonals = np.zeros((128, 384), np.float32)
    for delta in range(64):
        diagonals[63 - delta, buckets[delta] :: BUCKETS] = 1
    toeplitz = np.zeros((384, 128), np.float32)
    for delta in range(64):
        toeplitz[buckets[delta] :: BUCKETS, (128 - delta) % 128] = 1
    return rows, bias, diagonals, np.eye(64)[::-1], toeplitz


def dot(a, b, dims=(((1,), (0,)), ((), ()))):
    return lax.dot_general(a, b, dims, preferred_element_type=F32)


def inverse_rms(value):
    return lax.rsqrt(jnp.mean(value * value, axis=-1, keepdims=True) + EPS)


def norm_backward(grad_normed, normed, scale):
    return scale * (grad_normed - normed * jnp.mean(grad_normed * normed, axis=-1, keepdims=True))


def a2a(block):
    return lax.all_to_all(block, "dp", split_axis=0, concat_axis=0, tiled=True)


def swap(block):
    return lax.ppermute(block, "section", SWAP)


def lanes(rows, width):
    return lax.broadcasted_iota(jnp.int32, (rows, width), 1)


def ordered(first, mine, theirs):
    return jnp.concatenate(
        [lax.select(first, mine, theirs), lax.select(first, theirs, mine)], axis=1
    )


def split(first, block, width):
    left, right = block[:, :width], block[:, width:]
    return lax.select(first, left, right), lax.select(first, right, left)


def packed_rows():
    return lax.rem(lanes(1, 1024), 16) < 12


def thirds(o):
    third = lax.rem(lanes(1, 768), 3)
    return [jnp.where(third == t, o, 0.0) for t in range(3)]


def spread(value, e):
    return jnp.where(packed_rows(), dot(value, e), 0.0)


def collected(value, e):
    value = jnp.where(packed_rows(), value, 0.0)
    high = value.astype(BF)
    low = (value - high.astype(F32)).astype(BF)
    both = dot(jnp.concatenate([high, low], axis=0), e, NT)
    return both[:64] + both[64:]


def slot_mask(idx):
    row = lanes(64, 512)
    return ((row >> 4) * 8 + (row & 7) == idx).astype(F32).astype(BF)


def slot_mask_rows(idx_row):
    row = lax.broadcasted_iota(jnp.int32, (512, 64), 0)
    return ((row >> 4) * 8 + (row & 7) == idx_row).astype(F32).astype(BF)


def mixed_out(mid, gates, idx, back):
    out = mid
    for j in range(2):
        picked = dot(slot_mask(idx[:, j : j + 1]), back)
        out = out + gates[:, j : j + 1] * picked
    return out


def pair_masks():
    low = (lanes(1, 128) < 64).astype(F32).astype(BF)
    return low, (1.0 - low.astype(F32)).astype(BF)


def stacked(pair):
    low, high = pair_masks()
    return jnp.concatenate([pair * low, pair * high], axis=0)


def unstacked(both):
    return jnp.where(lanes(1, 128) < 64, both[:64], both[64:])


def bias_scores(row, toeplitz):
    head = lax.broadcasted_iota(jnp.int32, (16, 384), 0)
    table = jnp.where(head == lanes(16, 384) // 32, row, 0.0).astype(BF)
    table = dot(table, toeplitz)
    heads = []
    for j in range(12):
        wide = jnp.broadcast_to(table[j : j + 1], (64, 128))
        heads.append(pltpu.roll(wide, 0, 1, stride=1, stride_axis=0)[:, :64])
    return jnp.concatenate(heads, axis=0)


def forward_kernel(
    first_ref, *refs, entering,
):
    if entering:
        (h_ref, own, other, e_ref, b_ref, toeplitz, allowed, idx, idx_t,
         h_out, qkv_ref, p_ref, left, mid_ref, gate_ref, gains, send) = refs
        h = h_ref[...].astype(F32)
    else:
        (mid_0, gate_0, idx_0, back_0, grad, own, other, e_ref, b_ref, toeplitz, allowed, idx,
         idx_t, h_out, qkv_ref, p_ref, left, mid_ref, gate_ref, gains, send) = refs
        h = mixed_out(mid_0[...], gate_0[...], idx_0[...], back_0[...]).astype(BF).astype(F32)
    first = first_ref[0] == 1
    h_out[...] = h.astype(BF)
    e = e_ref[...]
    idx, idx_t = idx[...], idx_t[...]
    small = own[:, HALF:]
    small_t = small.astype(F32).T[32:48].astype(BF)
    gains[...] = dot(small_t, e, NT)
    bias = bias_scores(dot(small_t, b_ref[...], NT)[2:3], toeplitz[...])
    a = (h * inverse_rms(h) * gains[0:1, :]).astype(BF)
    a_rows = spread(a, e).astype(BF)
    left[0:64, :] = a_rows
    qkv = ordered(
        first,
        dot(a_rows, own[:, :HALF]).astype(BF),
        dot(a_rows, other[:, :HALF]).astype(BF),
    )
    qkv_ref[...] = qkv
    scores = []
    for pair in range(6):
        at = 128 * pair
        scores.append(dot(stacked(qkv[:, at : at + 128]), qkv[:, 768 + at : 896 + at], NT))
    s = jnp.concatenate(scores, axis=0) * 0.125 + bias
    masked = jnp.where(jnp.concatenate([allowed[...]] * 12, axis=0) > 0, s, -1e30)
    raised = jnp.exp(masked - jnp.max(masked, axis=-1, keepdims=True))
    p = raised / jnp.sum(raised, axis=-1, keepdims=True)
    p_ref[...] = p
    p_low = p.astype(BF)
    outs = []
    for pair in range(6):
        at = 128 * pair
        outs.append(unstacked(dot(p_low[at : at + 128], qkv[:, 1536 + at : 1664 + at])))
    o = jnp.concatenate(outs, axis=1)
    o_rows = jnp.where(
        packed_rows(), 0.0, dot(jnp.concatenate(thirds(o), axis=0).astype(BF), e)
    ).astype(BF)
    left[64:256, :] = o_rows

    def project(block):
        return sum(
            dot(o_rows[64 * t : 64 * t + 64], block[:, OUT_HALF * t : OUT_HALF * (t + 1)])
            for t in range(3)
        )

    mid = h + ordered(first, project(own), project(other))
    mid_ref[...] = mid
    c = (mid * inverse_rms(mid) * gains[1:2, :]).astype(BF)
    c_rows = spread(c, e).astype(BF)
    left[256:320, :] = c_rows
    z = dot(c_rows, small)
    chosen = [
        jnp.sum(jnp.where(lanes(64, 128) == (idx[:, j : j + 1] >> 3), z, 0.0), axis=1, keepdims=True)
        for j in range(2)
    ]
    top = jnp.maximum(chosen[0], chosen[1])
    e0, e1 = jnp.exp(chosen[0] - top), jnp.exp(chosen[1] - top)
    g0, g1 = e0 / (e0 + e1), e1 / (e0 + e1)
    gate_ref[...] = jnp.concatenate([g0, g1], axis=1)
    hot = [slot_mask_rows(idx_t[j : j + 1, :]) for j in range(2)]
    send[:, 0:768] = dot(hot[0] + hot[1], c).astype(BF)
    if not entering:
        g = grad[...].astype(F32)
        grads = jnp.concatenate([(g0 * g).astype(BF), (g1 * g).astype(BF)], axis=0)
        send[:, 768:1536] = dot(jnp.concatenate(hot, axis=1), grads).astype(BF)


def backward_kernel(first_ref, *refs, leaving):
    if leaving:
        (grad, back_y, back_dx, idx_ref, gate_ref, h_ref, mid_ref, qkv_ref, p_ref, own,
         other, e_ref, gains, b_ref, diag_ref, flip_ref,
         ig_ref, extra, own_grads, other_grads) = refs
        y, dx = back_y[...], back_dx[...]
    else:
        (grad, back, idx_ref, gate_ref, h_ref, mid_ref, qkv_ref, p_ref, own,
         other, e_ref, gains, b_ref, diag_ref, flip_ref, gate_0, idx_0,
         ig_ref, extra, own_grads, other_grads, out_ref, send) = refs
        y, dx = back[:, 0:768], back[:, 768:1536]
    first = first_ref[0] == 1
    e = e_ref[...]
    g, gates, idx = grad[...].astype(F32), gate_ref[...], idx_ref[...]
    hot = [slot_mask(idx[:, j : j + 1]) for j in range(2)]
    picked = [dot(hot[j], y) for j in range(2)]
    mid = mid_ref[...]
    g0, g1 = gates[:, 0:1], gates[:, 1:2]
    if not leaving:
        out_ref[...] = (mid + g0 * picked[0] + g1 * picked[1]).astype(BF)
    dg = [jnp.sum(picked[j] * g, axis=1, keepdims=True) for j in range(2)]
    mean = g0 * dg[0] + g1 * dg[1]
    lane = lanes(64, 128)
    dz = jnp.where(lane == (idx[:, 0:1] >> 3), g0 * (dg[0] - mean), 0.0) + jnp.where(
        lane == (idx[:, 1:2] >> 3), g1 * (dg[1] - mean), 0.0
    )
    dz = dz.astype(BF)
    dc = collected(dot(dz, own[:, HALF:], NT), e) + dot(hot[0] + hot[1], dx)
    r2 = inverse_rms(mid)
    n2 = mid * r2
    dgain_two = jnp.sum(dc * n2, axis=0, keepdims=True)
    dmid = g + norm_backward(dc * gains[1:2, :], n2, r2)
    datt = dmid.astype(BF)
    datt_own, datt_other = split(first, datt, OUT_HALF)
    parts = []
    for t in range(3):
        cols = slice(OUT_HALF * t, OUT_HALF * (t + 1))
        parts.append(dot(datt_own, own[:, cols], NT) + dot(datt_other, other[:, cols], NT))
    parts = jnp.where(packed_rows(), 0.0, jnp.concatenate(parts, axis=0)).astype(BF)
    parts = dot(parts, e, NT)
    third = lax.rem(lanes(1, 768), 3)
    do = jnp.where(third == 0, parts[:64], jnp.where(third == 1, parts[64:128], parts[128:]))
    do = do.astype(BF)
    dos = [stacked(do[:, 128 * j : 128 * j + 128]) for j in range(6)]
    p = p_ref[...]
    p_low = p.astype(BF)
    qkv = qkv_ref[...]
    dp = jnp.concatenate(
        [dot(dos[j], qkv[:, 1536 + 128 * j : 1664 + 128 * j], NT) for j in range(6)], axis=0
    )
    ds = (p * (dp - jnp.sum(dp * p, axis=-1, keepdims=True))).astype(BF)
    dq, dk, dv, sums = [], [], [], []
    flip = flip_ref[...]
    for j in range(6):
        at = 128 * j
        ds_pair = ds[at : at + 128]
        dv.append(dot(p_low[at : at + 128], dos[j], TN))
        dq.append(unstacked(dot(ds_pair, qkv[:, 768 + at : 896 + at])) * 0.125)
        dk.append(dot(ds_pair, stacked(qkv[:, at : at + 128]), TN) * 0.125)
        for half in range(2):
            turned = dot(flip, ds_pair[64 * half : 64 * half + 64])
            turned = jnp.concatenate([turned, jnp.zeros((64, 64), F32)], axis=1)
            turned = pltpu.roll(turned, 0, 1, stride=1, stride_axis=0)
            sums.append(jnp.sum(turned, axis=0, keepdims=True))
    sums = jnp.concatenate(sums + [jnp.zeros((4, 128), F32)], axis=0)
    high = sums.astype(BF)
    low = (sums - high.astype(F32)).astype(BF)
    dbias = dot(high, diag_ref[...]) + dot(low, diag_ref[...])
    head = lax.broadcasted_iota(jnp.int32, (16, 384), 0)
    dbias = jnp.sum(jnp.where(head == lanes(16, 384) // 32, dbias, 0.0), axis=0, keepdims=True)
    dqkv = jnp.concatenate(dq + dk + dv, axis=1).astype(BF)
    dqkv_own, dqkv_other = split(first, dqkv, HALF)
    da = collected(dot(dqkv_own, own[:, :HALF], NT) + dot(dqkv_other, other[:, :HALF], NT), e)
    h = h_ref[...].astype(F32)
    r1 = inverse_rms(h)
    n1 = h * r1
    dgain_one = jnp.sum(da * n1, axis=0, keepdims=True)
    ig = (dmid + norm_backward(da * gains[0:1, :], n1, r1)).astype(BF)
    ig_ref[...] = ig
    if not leaving:
        g = ig.astype(F32)
        gate_0, idx_0 = gate_0[...], idx_0[...]
        grads = jnp.concatenate(
            [(gate_0[:, j : j + 1] * g).astype(BF) for j in range(2)], axis=0
        )
        rows = jnp.concatenate([slot_mask_rows(idx_0[j : j + 1, :]) for j in range(2)], axis=1)
        send[...] = dot(rows, grads).astype(BF)
    row = lax.broadcasted_iota(jnp.int32, (16, 1), 0)
    both = jnp.where(row == 0, dgain_one, jnp.where(row == 1, dgain_two, 0.0)).astype(BF)
    dbias = jnp.where(row == 2, dbias, 0.0).astype(BF)
    extra[...] = (spread(both, e) + dot(dbias, b_ref[...])).astype(BF)
    for ref, dqkv_half, datt_half in (
        (own_grads, dqkv_own, datt_own),
        (other_grads, dqkv_other, datt_other),
    ):
        ref[:, 0:HALF] = dqkv_half
        ref[:, HALF:1536] = datt_half
        ref[:, 1536:1664] = dz


class Loaded:
    def __init__(self, source, held, sem):
        self.held, self.waited = held, False
        self.copy = pltpu.make_async_copy(source, held, sem)
        self.copy.start()

    def ready(self):
        if not self.waited:
            self.copy.wait()
            self.waited = True
        return self.held

    def __getitem__(self, at):
        return self.ready()[at]


class Stored:
    def __init__(self, target, held, fresh):
        self.target, self.held, self.fresh, self.copies = target, held, fresh, []

    def __setitem__(self, at, value):
        self.held[at] = value
        self.send(at)

    def __getitem__(self, at):
        return self.held[at]

    def send(self, at):
        source, target = (self.held, self.target)
        if at is not Ellipsis:
            source, target = source.at[at], target.at[at]
        self.copies.append(pltpu.make_async_copy(source, target, self.fresh()))
        self.copies[-1].start()

    def wait(self):
        for copy in self.copies:
            copy.wait()


def call(kernel, args, outs, flops, raw=0, scratch=(), direct=(), keeps=(), order=()):
    flag, *arrays = args
    n_in, n_out = len(arrays), len(outs)
    staged = [j for j in range(n_in - raw) if j not in direct]
    staged = list(order) + [j for j in staged if j not in order]
    n_held = len(staged) + n_out

    def body(flag, *refs):
        ins, results = list(refs[:n_in]), refs[n_in : n_in + n_out]
        copied = refs[n_in + n_out : n_in + n_out + len(keeps)]
        held = refs[n_in + n_out + len(keeps) :]
        own, sems = held[n_held:-1], held[-1]
        count = iter(range(SEMS))

        def fresh():
            return sems.at[next(count)]

        moves = []
        for (j, cols), target in zip(keeps, copied):
            moves.append(pltpu.make_async_copy(ins[j].at[:, cols], target, fresh()))
            moves[-1].start()
        for n, j in enumerate(staged):
            ins[j] = Loaded(ins[j], held[n], fresh())
        stored = [Stored(results[j], held[len(staged) + j], fresh) for j in range(n_out)]
        kernel(flag, *ins, *stored, *own)
        for j in staged:
            ins[j].ready()
        for item in stored + moves:
            item.wait()

    hbm = pl.BlockSpec(memory_space=pltpu.HBM)
    spaces = [pltpu.VMEM if j in direct else pltpu.HBM for j in range(n_in)]
    kept = [
        pltpu.HBM((arrays[j].shape[0], cols.stop - cols.start), arrays[j].dtype)
        for j, cols in keeps
    ]
    return pl.pallas_call(
        body,
        in_specs=[pl.BlockSpec(memory_space=pltpu.SMEM)]
        + [pl.BlockSpec(memory_space=space) for space in spaces],
        out_specs=[hbm] * (n_out + len(keeps)),
        out_shape=[pltpu.HBM(*out) for out in outs] + kept,
        scratch_shapes=[pltpu.VMEM(arrays[j].shape, arrays[j].dtype) for j in staged]
        + [pltpu.VMEM(*out) for out in outs]
        + list(scratch)
        + [pltpu.SemaphoreType.DMA((SEMS,))],
        compiler_params=pltpu.CompilerParams(vmem_limit_bytes=VMEM_BYTES),
        cost_estimate=pl.CostEstimate(flops=flops, bytes_accessed=12000000, transcendentals=50000),
    )(flag, *(pltpu.with_memory_space_constraint(x, space) for x, space in zip(arrays, spaces)))


KEPT = [
    ((64, 768), BF),
    ((64, 2304), BF),
    ((768, 64), F32),
    ((320, 1024), BF),
    ((64, 768), F32),
    ((64, 2), F32),
    ((16, 768), F32),
]


def copies_kernel(first_ref, mine, theirs, copies, block_1):
    first = first_ref[0] == 1
    mine, theirs = mine[...], theirs[...]
    block = lax.select(first, mine, theirs)
    block_1[...] = lax.select(first, theirs, mine)
    for at in range(0, 64, 16):
        copies[at : at + 16] = jnp.broadcast_to(block[None], (16, 16, PACK))


def totals_block(refs, out, at):
    left, extra, grads, left_t, extra_t, grads_t = refs
    cols = slice(256 * at, 256 * at + 256)
    grads = jnp.concatenate([grads[...], grads_t[...]], axis=0)

    def rows(lo, hi):
        return jnp.concatenate([left[lo:hi, cols], left_t[lo:hi, cols]], axis=0)

    main = dot(rows(0, 64), grads[:, :HALF], TN)
    outs = [
        dot(rows(64 + 64 * t, 128 + 64 * t), grads[:, HALF:1536], TN) for t in range(3)
    ]
    marks = lax.broadcasted_iota(jnp.int32, (16, 128), 0) + 32 == lanes(16, 128)
    marks = ((lax.broadcasted_iota(jnp.int32, (16, 128), 0) < 3) & marks).astype(F32).astype(BF)
    rest = dot(
        jnp.concatenate([rows(256, 320), extra[:, cols], extra_t[:, cols]], axis=0),
        jnp.concatenate([grads[:, 1536:], marks, marks], axis=0),
        TN,
    )
    main = main + jnp.concatenate(outs, axis=1)
    block = jnp.concatenate([main, rest], axis=1).astype(BF)
    out[16 * at : 16 * at + 16, 0:16, :] = block.reshape(16, 16, PACK)


def totals_kernel(flag, *refs):
    for at in range(4):
        totals_block(refs[:6], refs[6], at)


def dense_totals(flag, operands):
    left, left_t, extra, own_grads, other_grads = operands
    args = (flag, left, extra, own_grads, left_t, swap(extra), swap(other_grads))
    return call(totals_kernel, args, [((64, 16, PACK), BF)], 1800000000, direct=(3, 4, 5))[0]


def reduce_kernel(first_ref, parts_0, parts_1, mine, send):
    first = first_ref[0] == 1
    parts_1 = parts_1.ready()
    for at in range(0, PACK, 256):
        cols = slice(at, at + 256)
        sums = []
        for parts in (parts_0, parts_1):

            def add(j, total, parts=parts):
                return total + parts[j, :, cols].astype(F32)

            sums.append(lax.fori_loop(0, 64, add, jnp.zeros((16, 256), F32), unroll=16))
        mine[:, cols] = lax.select(first, sums[0], sums[1])
        send[:, cols] = lax.select(first, sums[1], sums[0])


def unpack_kernel(first_ref, mine, theirs, qkv, out, router, one, two, bias):
    first = first_ref[0] == 1
    halves = [
        lax.select(first, mine[...], theirs[...]),
        lax.select(first, theirs[...], mine[...]),
    ]
    qkv[...] = jnp.concatenate([block[:12, :HALF] for block in halves], axis=1).reshape(
        12, 1, 2304
    )
    row = lax.broadcasted_iota(jnp.int32, (12, 1), 0)
    wide = []
    for block in halves:
        total = jnp.zeros((12, OUT_HALF), F32)
        for j in range(4):
            for t in range(3):
                part = block[12 + j : 13 + j, OUT_HALF * t : OUT_HALF * (t + 1)]
                total = jnp.where(row == 3 * j + t, part, total)
        wide.append(total)
    out[...] = jnp.concatenate(wide, axis=1).reshape(12, 1, 768)
    rest = halves[0][:12, HALF:]
    router[...] = rest[:, :32].reshape(12, 1, 32)
    on_diagonal = lax.broadcasted_iota(jnp.int32, (12, 12), 0) == lanes(12, 12)

    def row(at):
        return jnp.sum(jnp.where(on_diagonal, rest[:, at : at + 1], 0.0), axis=0, keepdims=True)

    one[...] = row(32)
    two[...] = row(33)
    bias[...] = row(34)[:, :6]


def pack_kernel(first_ref, qkv, out, router, one, two, bias, mine, send):
    first = first_ref[0] == 1
    on_diagonal = lax.broadcasted_iota(jnp.int32, (12, 12), 0) == lanes(12, 12)

    def column(ref, width):
        wide = jnp.broadcast_to(ref[...].astype(F32), (12, width))
        return jnp.sum(jnp.where(on_diagonal[:, :width], wide, 0.0), axis=1, keepdims=True)

    lane = lanes(12, 128)
    rest = jnp.concatenate([router[0].astype(F32), jnp.zeros((12, 96), F32)], axis=1)
    for at, value in ((32, column(one, 12)), (33, column(two, 12)), (34, column(bias, 6))):
        rest = jnp.where(lane == at, value, rest)
    rest = jnp.concatenate([rest, jnp.zeros((4, 128), F32)], axis=0)
    outs = out[0].astype(F32)
    blocks = []
    for half in range(2):
        cols = slice(OUT_HALF * half, OUT_HALF * (half + 1))
        thin = [
            jnp.concatenate([outs[3 * j + t : 3 * j + t + 1, cols] for j in range(4)], axis=0)
            for t in range(3)
        ]
        rows = jnp.concatenate(
            [qkv[0, :, HALF * half : HALF * (half + 1)].astype(F32), jnp.concatenate(thin, axis=1)],
            axis=0,
        )
        blocks.append(jnp.concatenate([rows, rest], axis=1).astype(BF))
    mine[...] = lax.select(first, blocks[0], blocks[1])
    send[...] = lax.select(first, blocks[1], blocks[0])


def gelu_parts(u):
    inner = 0.7978845608028654 * (u + 0.044715 * (u * u * u))
    t = jnp.tanh(inner)
    half = 0.5 * (1.0 + t)
    slope = 0.7978845608028654 * (1.0 + 3 * 0.044715 * (u * u))
    return u * half, half + 0.5 * u * (1.0 - t * t) * slope


def load_weights(chosen, mine, theirs, held, sems):
    parts = [(slice(None), cols) for _, cols in chunks()], [(cols,) for _, cols in chunks()]

    def copies(refs, j):
        return [
            pltpu.make_async_copy(refs[j].at[at], held[j].at[at], sems.at[j, n])
            for n, at in enumerate(parts[j])
        ]

    for cond, refs in ((chosen, mine), (jnp.logical_not(chosen), theirs)):

        @pl.when(cond)
        def _(refs=refs):
            for pair in zip(copies(refs, 0), copies(refs, 1)):
                for copy in pair:
                    copy.start()

    return copies(mine, 0), copies(mine, 1)


def chunks():
    return [(n, slice(CHUNK * n, CHUNK * n + CHUNK)) for n in range(1536 // CHUNK)]


def expert_forward(flag, x, in_mine, in_theirs, out_mine, out_theirs, y, hid, slope, w1, w2, sems):
    copies = load_weights(
        flag[0] == 1, (in_mine, out_mine), (in_theirs, out_theirs), (w1, w2), sems
    )
    total = None
    for at, cols in chunks():
        copies[0][at].wait()
        value, grad = gelu_parts(dot(x[...], w1[:, cols]))
        value = value.astype(BF)
        hid[:, cols] = value
        slope[:, cols] = grad.astype(BF)
        copies[1][at].wait()
        part = dot(value, w2[cols, :])
        total = part if total is None else total + part
    y[...] = total.astype(BF)


def expert_both(
    flag, arrived, in_mine, in_theirs, out_mine, out_theirs, back, hid, du, w1, w2, sems
):
    copies = load_weights(
        flag[0] == 0, (in_mine, out_mine), (in_theirs, out_theirs), (w1, w2), sems
    )
    x, dy = arrived[:, 0:768], arrived[:, 768:1536]
    total, total_dx = None, None
    for at, cols in chunks():
        copies[0][at].wait()
        value, grad = gelu_parts(dot(x, w1[:, cols]))
        value = value.astype(BF)
        hid[:, cols] = value
        copies[1][at].wait()
        part = dot(value, w2[cols, :])
        pre = (dot(dy, w2[cols, :], NT) * grad).astype(BF)
        du[:, cols] = pre
        part_dx = dot(pre, w1[:, cols], NT)
        total = part if total is None else total + part
        total_dx = part_dx if total_dx is None else total_dx + part_dx
    back[:, 0:768] = total.astype(BF)
    back[:, 768:1536] = total_dx.astype(BF)


def expert_backward(
    flag, dy, slope, in_mine, in_theirs, out_mine, out_theirs, dx, du, w1, w2, sems
):
    copies = load_weights(
        flag[0] == 1, (in_mine, out_mine), (in_theirs, out_theirs), (w1, w2), sems
    )
    total = None
    for at, cols in chunks():
        copies[1][at].wait()
        pre = (dot(dy[...], w2[cols, :], NT) * slope[:, cols].astype(F32)).astype(BF)
        du[:, cols] = pre
        copies[0][at].wait()
        part = dot(pre, w1[:, cols], NT)
        total = part if total is None else total + part
    dx[...] = total.astype(BF)


def call_expert(kernel, flag, acts, weights, outs, flops, keeps):
    return call(
        kernel,
        (flag, *acts, *weights),
        [(out, BF) for out in outs],
        flops,
        4,
        [
            pltpu.VMEM((768, 1536), BF),
            pltpu.VMEM((1536, 768), BF),
            pltpu.SemaphoreType.DMA((2, 1536 // CHUNK)),
        ],
        (0,),
        keeps,
    )


def body(
    inputs, cotangent, segments, routes, slots, qkv_weight, out_weight, router_weight, gain_one,
    gain_two, bias_table, w_in, w_out,
):
    section = lax.axis_index("section")
    first = section == 0

    def pick(pair):
        return jnp.where(first, pair[0], pair[1])

    def pick_other(pair):
        return jnp.where(first, pair[1], pair[0])

    e, b_rows, diagonals, flip, toeplitz = (jnp.asarray(x, BF) for x in selections())
    flag = first.astype(jnp.int32).reshape(1)
    mine, theirs = call(
        pack_kernel,
        (flag, qkv_weight, out_weight, router_weight, gain_one, gain_two, bias_table),
        [((16, PACK), BF)] * 2,
        0,
    )
    theirs = swap(theirs)
    w_in_other, w_out_other = swap(w_in[0, 0]), swap(w_out[0, 0])
    flat = routes[0] * 8 + slots[0]
    flat_mine, flat_theirs = pick(flat), swap(pick_other(flat))

    copies_0, block_1 = call(
        copies_kernel, (flag, mine, theirs), [((64, 16, PACK), BF), ((16, PACK), BF)], 0
    )
    got_0 = a2a(copies_0).reshape(1024, PACK)
    dense_0 = (got_0, swap(got_0))
    got_1 = lax.all_gather(block_1, "dp", axis=0, tiled=True)
    weights = (w_in[0, 0], w_in_other, w_out[0, 0], w_out_other)
    idx_pair = (flat_mine, flat_theirs)
    idx_0, idx_1 = pick(idx_pair), pick_other(idx_pair)

    g1 = pick(cotangent)
    seg = pick(segments)
    places = np.arange(64)
    allowed = jnp.asarray(places[:, None] >= places[None, :]) & (seg[:, None] == seg[None, :])

    allowed = allowed.astype(F32)
    h_0, qkv_0, p_0, left_0, mid_0, gate_0, gains_0, send_0 = call(
        functools.partial(forward_kernel, entering=True),
        (flag, pick(inputs), *dense_0, e, b_rows, toeplitz, allowed, idx_0, idx_0.T),
        KEPT + [((512, 768), BF)],
        500000000,
        direct=(1, 2),
        order=(0, 3),
    )
    x_0 = a2a(send_0.reshape(64, 8, 768)).reshape(512, 768)
    left_0_theirs = swap(left_0)
    y_0, hid_0, slope_0, x_0 = call_expert(
        expert_forward, flag, (x_0,), weights, [(512, 768), (512, 1536), (512, 1536)],
        2500000000, ((0, WIDE),),
    )
    got_1, y_0 = lax.optimization_barrier((got_1, y_0))
    dense_1 = (got_1, swap(got_1))
    back_0 = a2a(y_0.reshape(64, 8, 768)).reshape(512, 768)

    h_1, qkv_1, p_1, left_1, mid_1, gate_1, gains_1, send_1, back_0 = call(
        functools.partial(forward_kernel, entering=False),
        (flag, mid_0, gate_0, idx_0, back_0, g1, *dense_1, e, b_rows, toeplitz, allowed,
         idx_1, idx_1.T),
        KEPT + [((512, 1536), BF)],
        700000000,
        direct=(3, 6),
        order=(0, 1, 2, 7, 5),
        keeps=((3, WIDE),),
    )
    arrived = a2a(send_1.reshape(64, 8, 1536)).reshape(512, 1536)
    left_1_theirs = swap(left_1)
    back_1, hid_1, du_1, x_1, dy_1 = call_expert(
        expert_both, flag, (arrived,), weights, [(512, 1536)] * 3, 5000000000,
        ((0, WIDE), (0, slice(768, 1536))),
    )
    back_1 = a2a(back_1.reshape(64, 8, 1536)).reshape(512, 1536)
    operands = [((16, 1024), BF), ((64, 1664), BF), ((64, 1664), BF)]
    ig_1, extra_1, own_1, other_1, out_1, send_0 = call(
        functools.partial(backward_kernel, leaving=False),
        (flag, g1, back_1, idx_1, gate_1, h_1, mid_1, qkv_1, p_1, *dense_1, e, gains_1,
         b_rows, diagonals, flip, gate_0, idx_0.T),
        [((64, 768), BF)] + operands + [((64, 768), BF), ((512, 768), BF)],
        1000000000,
        direct=(1,),
        order=(0, 2, 3, 5, 10, 11, 8, 9, 7, 6),
    )

    total_1 = dense_totals(flag, (left_1, left_1_theirs, extra_1, own_1, other_1))

    dy_0 = a2a(send_0.reshape(64, 8, 768)).reshape(512, 768)
    dy_0, total_1 = lax.optimization_barrier((dy_0, total_1))
    dx_0, du_0, dy_0 = call_expert(
        expert_backward, flag, (dy_0, slope_0), weights, [(512, 768), (512, 1536)],
        2500000000, ((0, WIDE),),
    )
    dx_rows = a2a(dx_0.reshape(64, 8, 768)).reshape(512, 768)
    dx_rows, total_1 = lax.optimization_barrier((dx_rows, total_1))
    total_1 = a2a(total_1)
    ig_0, extra_0, own_0, other_0 = call(
        functools.partial(backward_kernel, leaving=True),
        (flag, ig_1, back_0, dx_rows, idx_0, gate_0, h_0, mid_0, qkv_0, p_0, *dense_0, e,
         gains_0, b_rows, diagonals, flip),
        [((64, 768), BF)] + operands,
        1000000000,
        direct=(2,),
        order=(0, 3, 4, 1, 6, 11, 12, 9, 10, 8, 7),
    )
    total_1, own_0 = lax.optimization_barrier((total_1, own_0))
    total_0 = a2a(dense_totals(flag, (left_0, left_0_theirs, extra_0, own_0, other_0)))

    acts = [(x_0, x_1), (du_0, du_1), (hid_0, hid_1), (dy_0, dy_1)]
    xs, dus, hids, dys = [
        jnp.concatenate([pick(pair), swap(pick_other(pair))], axis=0) for pair in acts
    ]
    grad_in = dot(xs, dus, TN)
    grad_out = dot(hids, dys, TN)

    total_0, grad_in, grad_out = lax.optimization_barrier((total_0, grad_in, grad_out))
    red_mine, red_theirs = call(
        reduce_kernel, (flag, total_0, total_1), [((16, PACK), F32)] * 2, 0, direct=(0,)
    )
    dense = call(
        unpack_kernel,
        (flag, red_mine, swap(red_theirs)),
        [((12, 1, 2304), F32), ((12, 1, 768), F32), ((12, 1, 32), F32)]
        + [((1, 12), F32)] * 2
        + [((1, 6), F32)],
        0,
    )

    def by_micro(values):
        own, other = pick(values), swap(pick_other(values))
        return jnp.stack([pick((own, other)), pick((other, own))])[None]

    return (
        by_micro((h_1, out_1)),
        by_micro((ig_0, ig_1)),
        *(x.transpose(1, 0, 2) for x in dense[:3]),
        *dense[3:],
        grad_in[None, None],
        grad_out[None, None],
    )


def solution(mesh):
    placed = (
        P(None, "dp", None),
        P(None, "dp", None),
        P(None, "dp"),
        P("section", None, "dp", None),
        P("section", None, "dp", None),
        P("section", "dp", None),
        P("section", "dp", None),
        P("section", "dp", None),
        P("section", "dp"),
        P("section", "dp"),
        P("section", "dp"),
        P("section", "dp", None, None),
        P("section", "dp", None, None),
    )
    return jax.shard_map(
        body,
        mesh=mesh,
        in_specs=placed,
        out_specs=(
            P("section", None, "dp", None),
            P("section", None, "dp", None),
            P("section", "dp", None),
            P("section", "dp", None),
            P("section", "dp", None),
            P("section", "dp"),
            P("section", "dp"),
            P("section", "dp"),
            P("section", "dp", None, None),
            P("section", "dp", None, None),
        ),
        check_vma=False,
    )
```

```python
import functools

import jax
import jax.numpy as jnp
import numpy as np
from jax import lax
from jax.experimental import pallas as pl
from jax.experimental.pallas import tpu as pltpu
from jax.sharding import PartitionSpec as P

BUCKETS = 32
EPS = 1e-06
F32 = jnp.float32
BF = jnp.bfloat16
SWAP = [(0, 1), (1, 0)]
NT = (((1,), (1,)), ((), ()))
TN = (((0,), (0,)), ((), ()))
HALF = 1152
PACK = 1280
OUT_HALF = 384
VMEM_BYTES = 40 * 2**20
SEMS = 40
WIDE = slice(0, 768)
CHUNK = 512


def bucket_table(length, count):
    places = np.arange(length)
    distance = np.maximum(places[:, None] - places[None, :], 0)
    safe_distance = np.maximum(distance, 1)
    near_count = count // 2
    far_bucket = near_count + np.floor(
        np.log(safe_distance / near_count) / np.log(128.0 / near_count) * near_count
    ).astype(np.int32)
    return np.where(distance < near_count, distance, np.minimum(far_bucket, count - 1)).astype(
        np.int32
    )


def selections():
    rows = np.zeros((384, 512), np.float32)
    for f in range(384):
        d, r = divmod(f, 12)
        rows[f, 16 * d + r] = 1
        rows[f, 16 * d + 12 + r // 3] = 1
    bias = np.zeros((384, 1024), np.float32)
    for b in range(384):
        bias[b, 16 * (b // 6) + b % 6] = 1
    buckets = bucket_table(64, BUCKETS)[:, 0]
    diagonals = np.zeros((128, 384), np.float32)
    for delta in range(64):
        diagonals[63 - delta, buckets[delta] :: BUCKETS] = 1
    toeplitz = np.zeros((384, 128), np.float32)
    for delta in range(64):
        toeplitz[buckets[delta] :: BUCKETS, (128 - delta) % 128] = 1
    return rows, bias, diagonals, np.eye(64)[::-1], toeplitz


def dot(a, b, dims=(((1,), (0,)), ((), ()))):
    return lax.dot_general(a, b, dims, preferred_element_type=F32)


def inverse_rms(value):
    return lax.rsqrt(jnp.mean(value * value, axis=-1, keepdims=True) + EPS)


def norm_backward(grad_normed, normed, scale):
    return scale * (grad_normed - normed * jnp.mean(grad_normed * normed, axis=-1, keepdims=True))


def a2a(block):
    return lax.all_to_all(block, "dp", split_axis=0, concat_axis=0, tiled=True)


def swap(block):
    return lax.ppermute(block, "section", SWAP)


def lanes(rows, width):
    return lax.broadcasted_iota(jnp.int32, (rows, width), 1)


def ordered(first, mine, theirs):
    return jnp.concatenate(
        [lax.select(first, mine, theirs), lax.select(first, theirs, mine)], axis=1
    )


def split(first, block, width):
    left, right = block[:, :width], block[:, width:]
    return lax.select(first, left, right), lax.select(first, right, left)


def packed_rows():
    return lax.rem(lanes(1, 1024), 16) < 12


def thirds(o):
    third = lax.rem(lanes(1, 768), 3)
    return [jnp.where(third == t, o, 0.0) for t in range(3)]


def by_e(value, e):
    return jnp.concatenate([dot(value[:, :384], e), dot(value[:, 384:], e)], axis=1)


def by_e_back(value, e):
    return jnp.concatenate([dot(value[:, :512], e, NT), dot(value[:, 512:], e, NT)], axis=1)


def spread(value, e):
    return jnp.where(packed_rows(), by_e(value, e), 0.0)


def collected(value, e):
    value = jnp.where(packed_rows(), value, 0.0)
    high = value.astype(BF)
    low = (value - high.astype(F32)).astype(BF)
    both = by_e_back(jnp.concatenate([high, low], axis=0), e)
    return both[:64] + both[64:]


def slot_mask(idx):
    row = lanes(64, 512)
    return ((row >> 4) * 8 + (row & 7) == idx).astype(F32).astype(BF)


def slot_mask_rows(idx_row):
    row = lax.broadcasted_iota(jnp.int32, (512, 64), 0)
    return ((row >> 4) * 8 + (row & 7) == idx_row).astype(F32).astype(BF)


def mixed_out(mid, gates, idx, back):
    out = mid
    for j in range(2):
        picked = dot(slot_mask(idx[:, j : j + 1]), back)
        out = out + gates[:, j : j + 1] * picked
    return out


def pair_masks():
    low = (lanes(1, 128) < 64).astype(F32).astype(BF)
    return low, (1.0 - low.astype(F32)).astype(BF)


def stacked(pair):
    low, high = pair_masks()
    return jnp.concatenate([pair * low, pair * high], axis=0)


def unstacked(both):
    return jnp.where(lanes(1, 128) < 64, both[:64], both[64:])


def bias_scores(row, toeplitz):
    head = lax.broadcasted_iota(jnp.int32, (16, 384), 0)
    table = jnp.where(head == lanes(16, 384) // 32, row, 0.0).astype(BF)
    table = dot(table, toeplitz)
    heads = []
    for j in range(12):
        wide = jnp.broadcast_to(table[j : j + 1], (64, 128))
        heads.append(pltpu.roll(wide, 0, 1, stride=1, stride_axis=0)[:, :64])
    return jnp.concatenate(heads, axis=0)


def forward_kernel(
    first_ref, *refs, entering,
):
    if entering:
        (h_ref, own, other, e_ref, b_ref, toeplitz, allowed, idx, idx_t,
         h_out, qkv_ref, p_ref, left, mid_ref, gate_ref, gains, send) = refs
        h = h_ref[...].astype(F32)
    else:
        (mid_0, gate_0, idx_0, back_0, own, other, e_ref, b_ref, toeplitz, allowed, idx,
         idx_t, h_out, qkv_ref, p_ref, left, mid_ref, gate_ref, gains, send) = refs
        h = mixed_out(mid_0[...], gate_0[...], idx_0[...], back_0[...]).astype(BF).astype(F32)
    first = first_ref[0] == 1
    h_out[...] = h.astype(BF)
    e = e_ref[...]
    idx, idx_t = idx[...], idx_t[...]
    small = own[:, HALF:]
    small_t = small.astype(F32).T[32:48].astype(BF)
    gains[...] = by_e_back(small_t, e)
    a = (h * inverse_rms(h) * gains[0:1, :]).astype(BF)
    a_rows = spread(a, e).astype(BF)
    left[0:64, :] = a_rows
    qkv = ordered(
        first,
        dot(a_rows, own[:, :HALF]).astype(BF),
        dot(a_rows, other[:, :HALF]).astype(BF),
    )
    qkv_ref[...] = qkv
    bias = bias_scores(dot(small_t, b_ref[...], NT)[2:3], toeplitz[...])
    scores = []
    for pair in range(6):
        at = 128 * pair
        scores.append(dot(stacked(qkv[:, at : at + 128]), qkv[:, 768 + at : 896 + at], NT))
    s = jnp.concatenate(scores, axis=0) * 0.125 + bias
    masked = jnp.where(jnp.concatenate([allowed[...]] * 12, axis=0) > 0, s, -1e30)
    raised = jnp.exp(masked - jnp.max(masked, axis=-1, keepdims=True))
    p = raised / jnp.sum(raised, axis=-1, keepdims=True)
    p_ref[...] = p
    p_low = p.astype(BF)
    outs = []
    for pair in range(6):
        at = 128 * pair
        outs.append(unstacked(dot(p_low[at : at + 128], qkv[:, 1536 + at : 1664 + at])))
    o = jnp.concatenate(outs, axis=1)
    o_rows = jnp.where(
        packed_rows(), 0.0, by_e(jnp.concatenate(thirds(o), axis=0).astype(BF), e)
    ).astype(BF)
    left[64:256, :] = o_rows

    def project(block):
        return sum(
            dot(o_rows[64 * t : 64 * t + 64], block[:, OUT_HALF * t : OUT_HALF * (t + 1)])
            for t in range(3)
        )

    mid = h + ordered(first, project(own), project(other))
    mid_ref[...] = mid
    c = (mid * inverse_rms(mid) * gains[1:2, :]).astype(BF)
    c_rows = spread(c, e).astype(BF)
    left[256:320, :] = c_rows
    z = dot(c_rows, small)
    chosen = [
        jnp.sum(jnp.where(lanes(64, 128) == (idx[:, j : j + 1] >> 3), z, 0.0), axis=1, keepdims=True)
        for j in range(2)
    ]
    top = jnp.maximum(chosen[0], chosen[1])
    e0, e1 = jnp.exp(chosen[0] - top), jnp.exp(chosen[1] - top)
    g0, g1 = e0 / (e0 + e1), e1 / (e0 + e1)
    gate_ref[...] = jnp.concatenate([g0, g1], axis=1)
    hot = [slot_mask_rows(idx_t[j : j + 1, :]) for j in range(2)]
    send[:, 0:768] = dot(hot[0] + hot[1], c).astype(BF)
    if not entering:
        lane = lanes(64, 128)
        pieces = []
        for g in (g0, g1):
            row = jnp.zeros((64, 128), F32)
            for n in range(3):
                piece = g.astype(BF).astype(F32)
                row = jnp.where(lane == n, piece, row)
                g = g - piece
            pieces.append(row.astype(BF))
        send[:, 768:896] = dot(
            jnp.concatenate(hot, axis=1), jnp.concatenate(pieces, axis=0)
        ).astype(BF)


def backward_kernel(first_ref, *refs, leaving):
    if leaving:
        (grad, back_y, back_dx, idx_ref, gate_ref, h_ref, mid_ref, qkv_ref, p_ref, own,
         other, e_ref, gains, b_ref, diag_ref, flip_ref,
         ig_ref, extra, own_grads, other_grads) = refs
        y, dx = back_y[...], back_dx[...]
    else:
        (grad, back, idx_ref, gate_ref, h_ref, mid_ref, qkv_ref, p_ref, own,
         other, e_ref, gains, b_ref, diag_ref, flip_ref, gate_0, idx_0,
         ig_ref, extra, own_grads, other_grads, out_ref, send) = refs
        y, dx = back[:, 0:768], back[:, 768:1536]
    first = first_ref[0] == 1
    e = e_ref[...]
    g, gates, idx = grad[...].astype(F32), gate_ref[...], idx_ref[...]
    hot = [slot_mask(idx[:, j : j + 1]) for j in range(2)]
    picked = [dot(hot[j], y) for j in range(2)]
    mid = mid_ref[...]
    g0, g1 = gates[:, 0:1], gates[:, 1:2]
    if not leaving:
        out_ref[...] = (mid + g0 * picked[0] + g1 * picked[1]).astype(BF)
    dg = [jnp.sum(picked[j] * g, axis=1, keepdims=True) for j in range(2)]
    mean = g0 * dg[0] + g1 * dg[1]
    lane = lanes(64, 128)
    dz = jnp.where(lane == (idx[:, 0:1] >> 3), g0 * (dg[0] - mean), 0.0) + jnp.where(
        lane == (idx[:, 1:2] >> 3), g1 * (dg[1] - mean), 0.0
    )
    dz = dz.astype(BF)
    dc = collected(dot(dz, own[:, HALF:], NT), e) + dot(hot[0] + hot[1], dx)
    r2 = inverse_rms(mid)
    n2 = mid * r2
    dgain_two = jnp.sum(dc * n2, axis=0, keepdims=True)
    dmid = g + norm_backward(dc * gains[1:2, :], n2, r2)
    datt = dmid.astype(BF)
    datt_own, datt_other = split(first, datt, OUT_HALF)
    parts = []
    for t in range(3):
        cols = slice(OUT_HALF * t, OUT_HALF * (t + 1))
        parts.append(dot(datt_own, own[:, cols], NT) + dot(datt_other, other[:, cols], NT))
    parts = jnp.where(packed_rows(), 0.0, jnp.concatenate(parts, axis=0)).astype(BF)
    parts = by_e_back(parts, e)
    third = lax.rem(lanes(1, 768), 3)
    do = jnp.where(third == 0, parts[:64], jnp.where(third == 1, parts[64:128], parts[128:]))
    do = do.astype(BF)
    dos = [stacked(do[:, 128 * j : 128 * j + 128]) for j in range(6)]
    p = p_ref[...]
    p_low = p.astype(BF)
    qkv = qkv_ref[...]
    dp = jnp.concatenate(
        [dot(dos[j], qkv[:, 1536 + 128 * j : 1664 + 128 * j], NT) for j in range(6)], axis=0
    )
    ds = (p * (dp - jnp.sum(dp * p, axis=-1, keepdims=True))).astype(BF)
    dq, dk, dv, sums = [], [], [], []
    flip = flip_ref[...]
    for j in range(6):
        at = 128 * j
        ds_pair = ds[at : at + 128]
        dv.append(dot(p_low[at : at + 128], dos[j], TN))
        dq.append(unstacked(dot(ds_pair, qkv[:, 768 + at : 896 + at])) * 0.125)
        dk.append(dot(ds_pair, stacked(qkv[:, at : at + 128]), TN) * 0.125)
        for half in range(2):
            turned = dot(flip, ds_pair[64 * half : 64 * half + 64])
            turned = jnp.concatenate([turned, jnp.zeros((64, 64), F32)], axis=1)
            turned = pltpu.roll(turned, 0, 1, stride=1, stride_axis=0)
            sums.append(jnp.sum(turned, axis=0, keepdims=True))
    sums = jnp.concatenate(sums + [jnp.zeros((4, 128), F32)], axis=0)
    high = sums.astype(BF)
    low = (sums - high.astype(F32)).astype(BF)
    dbias = dot(high, diag_ref[...]) + dot(low, diag_ref[...])
    head = lax.broadcasted_iota(jnp.int32, (16, 384), 0)
    dbias = jnp.sum(jnp.where(head == lanes(16, 384) // 32, dbias, 0.0), axis=0, keepdims=True)
    dqkv = jnp.concatenate(dq + dk + dv, axis=1).astype(BF)
    dqkv_own, dqkv_other = split(first, dqkv, HALF)
    da = collected(dot(dqkv_own, own[:, :HALF], NT) + dot(dqkv_other, other[:, :HALF], NT), e)
    h = h_ref[...].astype(F32)
    r1 = inverse_rms(h)
    n1 = h * r1
    dgain_one = jnp.sum(da * n1, axis=0, keepdims=True)
    ig = (dmid + norm_backward(da * gains[0:1, :], n1, r1)).astype(BF)
    ig_ref[...] = ig
    if not leaving:
        g = ig.astype(F32)
        gate_0, idx_0 = gate_0[...], idx_0[...]
        grads = jnp.concatenate(
            [(gate_0[:, j : j + 1] * g).astype(BF) for j in range(2)], axis=0
        )
        rows = jnp.concatenate([slot_mask_rows(idx_0[j : j + 1, :]) for j in range(2)], axis=1)
        send[...] = dot(rows, grads).astype(BF)
    row = lax.broadcasted_iota(jnp.int32, (16, 1), 0)
    both = jnp.where(row == 0, dgain_one, jnp.where(row == 1, dgain_two, 0.0)).astype(BF)
    dbias = jnp.where(row == 2, dbias, 0.0).astype(BF)
    extra[...] = (spread(both, e) + dot(dbias, b_ref[...])).astype(BF)
    for ref, dqkv_half, datt_half in (
        (own_grads, dqkv_own, datt_own),
        (other_grads, dqkv_other, datt_other),
    ):
        ref[:, 0:HALF] = dqkv_half
        ref[:, HALF:1536] = datt_half
        ref[:, 1536:1664] = dz


class Loaded:
    def __init__(self, source, held, sem):
        self.held, self.waited = held, False
        self.copy = pltpu.make_async_copy(source, held, sem)
        self.copy.start()

    def ready(self):
        if not self.waited:
            self.copy.wait()
            self.waited = True
        return self.held

    def __getitem__(self, at):
        return self.ready()[at]


class Stored:
    def __init__(self, target, held, fresh):
        self.target, self.held, self.fresh, self.copies = target, held, fresh, []

    def __setitem__(self, at, value):
        self.held[at] = value
        self.send(at)

    def __getitem__(self, at):
        return self.held[at]

    def send(self, at):
        source, target = (self.held, self.target)
        if at is not Ellipsis:
            source, target = source.at[at], target.at[at]
        self.copies.append(pltpu.make_async_copy(source, target, self.fresh()))
        self.copies[-1].start()

    def wait(self):
        for copy in self.copies:
            copy.wait()


def call(kernel, args, outs, flops, raw=0, scratch=(), direct=(), keeps=(), order=()):
    flag, *arrays = args
    n_in, n_out = len(arrays), len(outs)
    staged = [j for j in range(n_in - raw) if j not in direct]
    staged = list(order) + [j for j in staged if j not in order]
    n_held = len(staged) + n_out

    def body(flag, *refs):
        ins, results = list(refs[:n_in]), refs[n_in : n_in + n_out]
        copied = refs[n_in + n_out : n_in + n_out + len(keeps)]
        held = refs[n_in + n_out + len(keeps) :]
        own, sems = held[n_held:-1], held[-1]
        count = iter(range(SEMS))

        def fresh():
            return sems.at[next(count)]

        moves = []
        for (j, cols), target in zip(keeps, copied):
            moves.append(pltpu.make_async_copy(ins[j].at[:, cols], target, fresh()))
            moves[-1].start()
        for n, j in enumerate(staged):
            ins[j] = Loaded(ins[j], held[n], fresh())
        stored = [Stored(results[j], held[len(staged) + j], fresh) for j in range(n_out)]
        kernel(flag, *ins, *stored, *own)
        for j in staged:
            ins[j].ready()
        for item in stored + moves:
            item.wait()

    hbm = pl.BlockSpec(memory_space=pltpu.HBM)
    spaces = [pltpu.VMEM if j in direct else pltpu.HBM for j in range(n_in)]
    kept = [
        pltpu.HBM((arrays[j].shape[0], cols.stop - cols.start), arrays[j].dtype)
        for j, cols in keeps
    ]
    return pl.pallas_call(
        body,
        in_specs=[pl.BlockSpec(memory_space=pltpu.SMEM)]
        + [pl.BlockSpec(memory_space=space) for space in spaces],
        out_specs=[hbm] * (n_out + len(keeps)),
        out_shape=[pltpu.HBM(*out) for out in outs] + kept,
        scratch_shapes=[pltpu.VMEM(arrays[j].shape, arrays[j].dtype) for j in staged]
        + [pltpu.VMEM(*out) for out in outs]
        + list(scratch)
        + [pltpu.SemaphoreType.DMA((SEMS,))],
        compiler_params=pltpu.CompilerParams(vmem_limit_bytes=VMEM_BYTES),
        cost_estimate=pl.CostEstimate(flops=flops, bytes_accessed=12000000, transcendentals=50000),
    )(flag, *(pltpu.with_memory_space_constraint(x, space) for x, space in zip(arrays, spaces)))


KEPT = [
    ((64, 768), BF),
    ((64, 2304), BF),
    ((768, 64), F32),
    ((320, 1024), BF),
    ((64, 768), F32),
    ((64, 2), F32),
    ((16, 768), F32),
]


def place_kernel(first_ref, grad, idx_t, rows):
    idx_t = idx_t[...]
    hot = slot_mask_rows(idx_t[0:1, :]) + slot_mask_rows(idx_t[1:2, :])
    rows[...] = dot(hot, grad[...]).astype(BF)


def copies_kernel(first_ref, mine, theirs, copies, block_1):
    first = first_ref[0] == 1
    mine, theirs = mine[...], theirs[...]
    block = lax.select(first, mine, theirs)
    block_1[...] = lax.select(first, theirs, mine)
    for at in range(0, 64, 16):
        copies[at : at + 16] = jnp.broadcast_to(block[None], (16, 16, PACK))


def totals_block(refs, out, at):
    left, extra, grads, left_t, extra_t, grads_t = refs
    cols = slice(256 * at, 256 * at + 256)
    grads = jnp.concatenate([grads[...], grads_t[...]], axis=0)

    def rows(lo, hi):
        return jnp.concatenate([left[lo:hi, cols], left_t[lo:hi, cols]], axis=0)

    main = dot(rows(0, 64), grads[:, :HALF], TN)
    outs = [
        dot(rows(64 + 64 * t, 128 + 64 * t), grads[:, HALF:1536], TN) for t in range(3)
    ]
    marks = lax.broadcasted_iota(jnp.int32, (16, 128), 0) + 32 == lanes(16, 128)
    marks = ((lax.broadcasted_iota(jnp.int32, (16, 128), 0) < 3) & marks).astype(F32).astype(BF)
    rest = dot(
        jnp.concatenate([rows(256, 320), extra[:, cols], extra_t[:, cols]], axis=0),
        jnp.concatenate([grads[:, 1536:], marks, marks], axis=0),
        TN,
    )
    main = main + jnp.concatenate(outs, axis=1)
    block = jnp.concatenate([main, rest], axis=1).astype(BF)
    out[16 * at : 16 * at + 16, 0:16, :] = block.reshape(16, 16, PACK)


def totals_kernel(flag, *refs):
    for at in range(4):
        totals_block(refs[:6], refs[6], at)


def dense_totals(flag, operands):
    left, left_t, extra, own_grads, other_grads = operands
    args = (flag, left, extra, own_grads, left_t, swap(extra), swap(other_grads))
    return call(totals_kernel, args, [((64, 16, PACK), BF)], 1800000000, direct=(3, 4, 5))[0]


def reduce_kernel(first_ref, parts_0, parts_1, mine, send):
    first = first_ref[0] == 1
    parts_1 = parts_1.ready()
    for at in range(0, PACK, 256):
        cols = slice(at, at + 256)
        sums = []
        for parts in (parts_0, parts_1):

            def add(j, total, parts=parts):
                return total + parts[j, :, cols].astype(F32)

            sums.append(lax.fori_loop(0, 64, add, jnp.zeros((16, 256), F32), unroll=16))
        mine[:, cols] = lax.select(first, sums[0], sums[1])
        send[:, cols] = lax.select(first, sums[1], sums[0])


def unpack_kernel(first_ref, mine, theirs, qkv, out, router, one, two, bias):
    first = first_ref[0] == 1
    halves = [
        lax.select(first, mine[...], theirs[...]),
        lax.select(first, theirs[...], mine[...]),
    ]
    qkv[...] = jnp.concatenate([block[:12, :HALF] for block in halves], axis=1).reshape(
        12, 1, 2304
    )
    row = lax.broadcasted_iota(jnp.int32, (12, 1), 0)
    wide = []
    for block in halves:
        total = jnp.zeros((12, OUT_HALF), F32)
        for j in range(4):
            for t in range(3):
                part = block[12 + j : 13 + j, OUT_HALF * t : OUT_HALF * (t + 1)]
                total = jnp.where(row == 3 * j + t, part, total)
        wide.append(total)
    out[...] = jnp.concatenate(wide, axis=1).reshape(12, 1, 768)
    rest = halves[0][:12, HALF:]
    router[...] = rest[:, :32].reshape(12, 1, 32)
    on_diagonal = lax.broadcasted_iota(jnp.int32, (12, 12), 0) == lanes(12, 12)

    def row(at):
        return jnp.sum(jnp.where(on_diagonal, rest[:, at : at + 1], 0.0), axis=0, keepdims=True)

    one[...] = row(32)
    two[...] = row(33)
    bias[...] = row(34)[:, :6]


def pack_kernel(first_ref, qkv, out, router, one, two, bias, mine, send):
    first = first_ref[0] == 1
    on_diagonal = lax.broadcasted_iota(jnp.int32, (12, 12), 0) == lanes(12, 12)

    def column(ref, width):
        wide = jnp.broadcast_to(ref[...].astype(F32), (12, width))
        return jnp.sum(jnp.where(on_diagonal[:, :width], wide, 0.0), axis=1, keepdims=True)

    lane = lanes(12, 128)
    rest = jnp.concatenate([router[0].astype(F32), jnp.zeros((12, 96), F32)], axis=1)
    for at, value in ((32, column(one, 12)), (33, column(two, 12)), (34, column(bias, 6))):
        rest = jnp.where(lane == at, value, rest)
    rest = jnp.concatenate([rest, jnp.zeros((4, 128), F32)], axis=0)
    outs = out[0].astype(F32)
    blocks = []
    for half in range(2):
        cols = slice(OUT_HALF * half, OUT_HALF * (half + 1))
        thin = [
            jnp.concatenate([outs[3 * j + t : 3 * j + t + 1, cols] for j in range(4)], axis=0)
            for t in range(3)
        ]
        rows = jnp.concatenate(
            [qkv[0, :, HALF * half : HALF * (half + 1)].astype(F32), jnp.concatenate(thin, axis=1)],
            axis=0,
        )
        blocks.append(jnp.concatenate([rows, rest], axis=1).astype(BF))
    mine[...] = lax.select(first, blocks[0], blocks[1])
    send[...] = lax.select(first, blocks[1], blocks[0])


def gelu_parts(u):
    inner = 0.7978845608028654 * (u + 0.044715 * (u * u * u))
    t = jnp.tanh(inner)
    half = 0.5 * (1.0 + t)
    slope = 0.7978845608028654 * (1.0 + 3 * 0.044715 * (u * u))
    return u * half, half + 0.5 * u * (1.0 - t * t) * slope


def load_weights(chosen, mine, theirs, held, sems, order=(0, 1)):
    for cond, refs in ((chosen, mine), (jnp.logical_not(chosen), theirs)):

        @pl.when(cond)
        def _(refs=refs):
            for j in order:
                pltpu.make_async_copy(refs[j], held[j], sems.at[j]).start()

    return [pltpu.make_async_copy(mine[j], held[j], sems.at[j]) for j in range(2)]


def chunks():
    return [(n, slice(CHUNK * n, CHUNK * n + CHUNK)) for n in range(1536 // CHUNK)]


def expert_forward(flag, x, in_mine, in_theirs, out_mine, out_theirs, y, hid, slope, w1, w2, sems):
    copies = load_weights(
        flag[0] == 1, (in_mine, out_mine), (in_theirs, out_theirs), (w1, w2), sems
    )
    total = None
    for at, cols in chunks():
        if at == 0:
            copies[0].wait()
        value, grad = gelu_parts(dot(x[...], w1[:, cols]))
        value = value.astype(BF)
        hid[:, cols] = value
        slope[:, cols] = grad.astype(BF)
        if at == 0:
            copies[1].wait()
        part = dot(value, w2[cols, :])
        total = part if total is None else total + part
    y[...] = total.astype(BF)


def expert_both(
    flag, arrived, grad, in_mine, in_theirs, out_mine, out_theirs, back, hid, du, dy_out,
    w1, w2, sems,
):
    copies = load_weights(
        flag[0] == 0, (in_mine, out_mine), (in_theirs, out_theirs), (w1, w2), sems
    )
    x = arrived[:, 0:768]
    gate = jnp.sum(arrived[:, 768:896].astype(F32), axis=1, keepdims=True)
    dy = (gate * grad[...].astype(F32)).astype(BF)
    dy_out[...] = dy
    total, total_dx = None, None
    for at, cols in chunks():
        if at == 0:
            copies[0].wait()
        value, grad = gelu_parts(dot(x, w1[:, cols]))
        value = value.astype(BF)
        hid[:, cols] = value
        if at == 0:
            copies[1].wait()
        part = dot(value, w2[cols, :])
        pre = (dot(dy, w2[cols, :], NT) * grad).astype(BF)
        du[:, cols] = pre
        part_dx = dot(pre, w1[:, cols], NT)
        total = part if total is None else total + part
        total_dx = part_dx if total_dx is None else total_dx + part_dx
    back[:, 0:768] = total.astype(BF)
    back[:, 768:1536] = total_dx.astype(BF)


def expert_backward(
    flag, dy, slope, in_mine, in_theirs, out_mine, out_theirs, dx, du, w1, w2, sems
):
    copies = load_weights(
        flag[0] == 1, (in_mine, out_mine), (in_theirs, out_theirs), (w1, w2), sems, (1, 0)
    )
    total = None
    for at, cols in chunks():
        if at == 0:
            copies[1].wait()
        pre = (dot(dy[...], w2[cols, :], NT) * slope[:, cols].astype(F32)).astype(BF)
        du[:, cols] = pre
        if at == 0:
            copies[0].wait()
        part = dot(pre, w1[:, cols], NT)
        total = part if total is None else total + part
    dx[...] = total.astype(BF)


def call_expert(kernel, flag, acts, weights, outs, flops, keeps):
    return call(
        kernel,
        (flag, *acts, *weights),
        [(out, BF) for out in outs],
        flops,
        4,
        [
            pltpu.VMEM((768, 1536), BF),
            pltpu.VMEM((1536, 768), BF),
            pltpu.SemaphoreType.DMA((2,)),
        ],
        (0,),
        keeps,
    )


def body(
    inputs, cotangent, segments, routes, slots, qkv_weight, out_weight, router_weight, gain_one,
    gain_two, bias_table, w_in, w_out,
):
    section = lax.axis_index("section")
    first = section == 0

    def pick(pair):
        return jnp.where(first, pair[0], pair[1])

    def pick_other(pair):
        return jnp.where(first, pair[1], pair[0])

    e, b_rows, diagonals, flip, toeplitz = (jnp.asarray(x, BF) for x in selections())
    flag = first.astype(jnp.int32).reshape(1)
    mine, theirs = call(
        pack_kernel,
        (flag, qkv_weight, out_weight, router_weight, gain_one, gain_two, bias_table),
        [((16, PACK), BF)] * 2,
        0,
    )
    theirs = swap(theirs)
    w_in_other, w_out_other = swap(w_in[0, 0]), swap(w_out[0, 0])
    flat = routes[0] * 8 + slots[0]
    flat_mine, flat_theirs = pick(flat), swap(pick_other(flat))

    copies_0, block_1 = call(
        copies_kernel, (flag, mine, theirs), [((64, 16, PACK), BF), ((16, PACK), BF)], 0
    )
    got_0 = a2a(copies_0).reshape(1024, PACK)
    got_1 = lax.all_gather(block_1, "dp", axis=0, tiled=True)
    weights = (w_in[0, 0], w_in_other, w_out[0, 0], w_out_other)
    idx_pair = (flat_mine, flat_theirs)
    idx_0, idx_1 = pick(idx_pair), pick_other(idx_pair)

    g1 = pick(cotangent)
    seg = pick(segments)
    places = np.arange(64)
    allowed = jnp.asarray(places[:, None] >= places[None, :]) & (seg[:, None] == seg[None, :])

    allowed = allowed.astype(F32)
    grad_rows = call(place_kernel, (flag, g1, idx_1.T), [((512, 768), BF)], 50000000)[0]
    got_0, grad_rows = lax.optimization_barrier((got_0, grad_rows))
    dense_0 = (got_0, swap(got_0))
    grad_rows = a2a(grad_rows.reshape(64, 8, 768)).reshape(512, 768)

    h_0, qkv_0, p_0, left_0, mid_0, gate_0, gains_0, send_0 = call(
        functools.partial(forward_kernel, entering=True),
        (flag, pick(inputs), *dense_0, e, b_rows, toeplitz, allowed, idx_0, idx_0.T),
        KEPT + [((512, 768), BF)],
        500000000,
        direct=(1, 2),
        order=(0, 3),
    )
    send_0, grad_rows = lax.optimization_barrier((send_0, grad_rows))
    x_0 = a2a(send_0.reshape(64, 8, 768)).reshape(512, 768)
    left_0_theirs = swap(left_0)
    y_0, hid_0, slope_0, x_0 = call_expert(
        expert_forward, flag, (x_0,), weights, [(512, 768), (512, 1536), (512, 1536)],
        2500000000, ((0, WIDE),),
    )
    got_1, y_0 = lax.optimization_barrier((got_1, y_0))
    dense_1 = (got_1, swap(got_1))
    back_0 = a2a(y_0.reshape(64, 8, 768)).reshape(512, 768)

    h_1, qkv_1, p_1, left_1, mid_1, gate_1, gains_1, send_1, back_0 = call(
        functools.partial(forward_kernel, entering=False),
        (flag, mid_0, gate_0, idx_0, back_0, *dense_1, e, b_rows, toeplitz, allowed,
         idx_1, idx_1.T),
        KEPT + [((512, 896), BF)],
        700000000,
        direct=(3, 5),
        order=(0, 1, 2, 6, 4),
        keeps=((3, WIDE),),
    )
    arrived = a2a(send_1.reshape(64, 8, 896)).reshape(512, 896)
    left_1_theirs = swap(left_1)
    back_1, hid_1, du_1, dy_1, x_1 = call_expert(
        expert_both, flag, (arrived, grad_rows), weights, [(512, 1536)] * 3 + [(512, 768)],
        5000000000, ((0, WIDE),),
    )
    back_1 = a2a(back_1.reshape(64, 8, 1536)).reshape(512, 1536)
    operands = [((16, 1024), BF), ((64, 1664), BF), ((64, 1664), BF)]
    ig_1, extra_1, own_1, other_1, out_1, send_0 = call(
        functools.partial(backward_kernel, leaving=False),
        (flag, g1, back_1, idx_1, gate_1, h_1, mid_1, qkv_1, p_1, *dense_1, e, gains_1,
         b_rows, diagonals, flip, gate_0, idx_0.T),
        [((64, 768), BF)] + operands + [((64, 768), BF), ((512, 768), BF)],
        1000000000,
        direct=(1,),
        order=(0, 2, 3, 5, 10, 11, 8, 9, 7, 6),
    )

    total_1 = dense_totals(flag, (left_1, left_1_theirs, extra_1, own_1, other_1))

    dy_0 = a2a(send_0.reshape(64, 8, 768)).reshape(512, 768)
    dy_0, total_1 = lax.optimization_barrier((dy_0, total_1))
    dx_0, du_0, dy_0 = call_expert(
        expert_backward, flag, (dy_0, slope_0), weights, [(512, 768), (512, 1536)],
        2500000000, ((0, WIDE),),
    )
    dx_rows = a2a(dx_0.reshape(64, 8, 768)).reshape(512, 768)
    dx_rows, total_1 = lax.optimization_barrier((dx_rows, total_1))
    total_1 = a2a(total_1)
    ig_0, extra_0, own_0, other_0 = call(
        functools.partial(backward_kernel, leaving=True),
        (flag, ig_1, back_0, dx_rows, idx_0, gate_0, h_0, mid_0, qkv_0, p_0, *dense_0, e,
         gains_0, b_rows, diagonals, flip),
        [((64, 768), BF)] + operands,
        1000000000,
        direct=(2,),
        order=(0, 3, 4, 1, 6, 11, 12, 9, 10, 8, 7),
    )
    total_1, own_0 = lax.optimization_barrier((total_1, own_0))
    total_0 = a2a(dense_totals(flag, (left_0, left_0_theirs, extra_0, own_0, other_0)))

    acts = [(x_0, x_1), (du_0, du_1), (hid_0, hid_1), (dy_0, dy_1)]
    xs, dus, hids, dys = [
        jnp.concatenate([pick(pair), swap(pick_other(pair))], axis=0) for pair in acts
    ]
    grad_in = dot(xs, dus, TN)
    grad_out = dot(hids, dys, TN)

    total_0, grad_in, grad_out = lax.optimization_barrier((total_0, grad_in, grad_out))
    red_mine, red_theirs = call(
        reduce_kernel, (flag, total_0, total_1), [((16, PACK), F32)] * 2, 0, direct=(0,)
    )
    dense = call(
        unpack_kernel,
        (flag, red_mine, swap(red_theirs)),
        [((12, 1, 2304), F32), ((12, 1, 768), F32), ((12, 1, 32), F32)]
        + [((1, 12), F32)] * 2
        + [((1, 6), F32)],
        0,
    )

    def by_micro(values):
        own, other = pick(values), swap(pick_other(values))
        return jnp.stack([pick((own, other)), pick((other, own))])[None]

    return (
        by_micro((h_1, out_1)),
        by_micro((ig_0, ig_1)),
        *(x.transpose(1, 0, 2) for x in dense[:3]),
        *dense[3:],
        grad_in[None, None],
        grad_out[None, None],
    )


def solution(mesh):
    placed = (
        P(None, "dp", None),
        P(None, "dp", None),
        P(None, "dp"),
        P("section", None, "dp", None),
        P("section", None, "dp", None),
        P("section", "dp", None),
        P("section", "dp", None),
        P("section", "dp", None),
        P("section", "dp"),
        P("section", "dp"),
        P("section", "dp"),
        P("section", "dp", None, None),
        P("section", "dp", None, None),
    )
    return jax.shard_map(
        body,
        mesh=mesh,
        in_specs=placed,
        out_specs=(
            P("section", None, "dp", None),
            P("section", None, "dp", None),
            P("section", "dp", None),
            P("section", "dp", None),
            P("section", "dp", None),
            P("section", "dp"),
            P("section", "dp"),
            P("section", "dp"),
            P("section", "dp", None, None),
            P("section", "dp", None, None),
        ),
        check_vma=False,
    )
```

```python
import functools

import jax
import jax.numpy as jnp
import numpy as np
from jax import lax
from jax.experimental import pallas as pl
from jax.experimental.pallas import tpu as pltpu
from jax.sharding import PartitionSpec as P

BUCKETS = 32
EPS = 1e-06
F32 = jnp.float32
BF = jnp.bfloat16
SWAP = [(0, 1), (1, 0)]
NT = (((1,), (1,)), ((), ()))
TN = (((0,), (0,)), ((), ()))
HALF = 1152
PACK = 1280
OUT_HALF = 384
VMEM_BYTES = 40 * 2**20
SEMS = 40
WIDE = slice(0, 768)
CHUNK = 512


def bucket_table(length, count):
    places = np.arange(length)
    distance = np.maximum(places[:, None] - places[None, :], 0)
    safe_distance = np.maximum(distance, 1)
    near_count = count // 2
    far_bucket = near_count + np.floor(
        np.log(safe_distance / near_count) / np.log(128.0 / near_count) * near_count
    ).astype(np.int32)
    return np.where(distance < near_count, distance, np.minimum(far_bucket, count - 1)).astype(
        np.int32
    )


def selections():
    rows = np.zeros((384, 512), np.float32)
    for f in range(384):
        d, r = divmod(f, 12)
        rows[f, 16 * d + r] = 1
        rows[f, 16 * d + 12 + r // 3] = 1
    bias = np.zeros((384, 1024), np.float32)
    for b in range(384):
        bias[b, 16 * (b // 6) + b % 6] = 1
    buckets = bucket_table(64, BUCKETS)[:, 0]
    diagonals = np.zeros((128, 384), np.float32)
    for delta in range(64):
        diagonals[63 - delta, buckets[delta] :: BUCKETS] = 1
    toeplitz = np.zeros((384, 128), np.float32)
    for delta in range(64):
        toeplitz[buckets[delta] :: BUCKETS, (128 - delta) % 128] = 1
    return rows, bias, diagonals, np.eye(64)[::-1], toeplitz


def dot(a, b, dims=(((1,), (0,)), ((), ()))):
    return lax.dot_general(a, b, dims, preferred_element_type=F32)


def inverse_rms(value):
    return lax.rsqrt(jnp.mean(value * value, axis=-1, keepdims=True) + EPS)


def norm_backward(grad_normed, normed, scale):
    return scale * (grad_normed - normed * jnp.mean(grad_normed * normed, axis=-1, keepdims=True))


def a2a(block):
    return lax.all_to_all(block, "dp", split_axis=0, concat_axis=0, tiled=True)


def swap(block):
    return lax.ppermute(block, "section", SWAP)


def lanes(rows, width):
    return lax.broadcasted_iota(jnp.int32, (rows, width), 1)


def ordered(first, mine, theirs):
    return jnp.concatenate(
        [lax.select(first, mine, theirs), lax.select(first, theirs, mine)], axis=1
    )


def split(first, block, width):
    left, right = block[:, :width], block[:, width:]
    return lax.select(first, left, right), lax.select(first, right, left)


def packed_rows():
    return lax.rem(lanes(1, 1024), 16) < 12


def thirds(o):
    third = lax.rem(lanes(1, 768), 3)
    return [jnp.where(third == t, o, 0.0) for t in range(3)]


def by_e(value, e):
    return jnp.concatenate([dot(value[:, :384], e), dot(value[:, 384:], e)], axis=1)


def by_e_back(value, e):
    return jnp.concatenate([dot(value[:, :512], e, NT), dot(value[:, 512:], e, NT)], axis=1)


def spread(value, e):
    return jnp.where(packed_rows(), by_e(value, e), 0.0)


def collected(value, e):
    value = jnp.where(packed_rows(), value, 0.0)
    high = value.astype(BF)
    low = (value - high.astype(F32)).astype(BF)
    both = by_e_back(jnp.concatenate([high, low], axis=0), e)
    return both[:64] + both[64:]


def slot_mask(idx):
    row = lanes(64, 512)
    return ((row >> 4) * 8 + (row & 7) == idx).astype(F32).astype(BF)


def slot_mask_rows(idx_row):
    row = lax.broadcasted_iota(jnp.int32, (512, 64), 0)
    return ((row >> 4) * 8 + (row & 7) == idx_row).astype(F32).astype(BF)


def mixed_out(mid, gates, idx, back):
    out = mid
    for j in range(2):
        picked = dot(slot_mask(idx[:, j : j + 1]), back)
        out = out + gates[:, j : j + 1] * picked
    return out


def pair_masks():
    low = (lanes(1, 128) < 64).astype(F32).astype(BF)
    return low, (1.0 - low.astype(F32)).astype(BF)


def stacked(pair):
    low, high = pair_masks()
    return jnp.concatenate([pair * low, pair * high], axis=0)


def unstacked(both):
    return jnp.where(lanes(1, 128) < 64, both[:64], both[64:])


def bias_scores(row, toeplitz):
    head = lax.broadcasted_iota(jnp.int32, (16, 384), 0)
    table = jnp.where(head == lanes(16, 384) // 32, row, 0.0).astype(BF)
    table = dot(table, toeplitz)
    heads = []
    for j in range(12):
        wide = jnp.broadcast_to(table[j : j + 1], (64, 128))
        heads.append(pltpu.roll(wide, 0, 1, stride=1, stride_axis=0)[:, :64])
    return jnp.concatenate(heads, axis=0)


def forward_kernel(
    first_ref, *refs, entering,
):
    if entering:
        (h_ref, own, other, e_ref, b_ref, toeplitz, allowed, idx, idx_t,
         h_out, qkv_ref, p_ref, left, mid_ref, gate_ref, gains, send) = refs
        h = h_ref[...].astype(F32)
    else:
        (mid_0, gate_0, idx_0, back_0, own, other, e_ref, b_ref, toeplitz, allowed, idx,
         idx_t, h_out, qkv_ref, p_ref, left, mid_ref, gate_ref, gains, send) = refs
        h = mixed_out(mid_0[...], gate_0[...], idx_0[...], back_0[...]).astype(BF).astype(F32)
    first = first_ref[0] == 1
    h_out[...] = h.astype(BF)
    e = e_ref[...]
    idx, idx_t = idx[...], idx_t[...]
    small = own[:, HALF:]
    small_t = small.astype(F32).T[32:48].astype(BF)
    gains[...] = by_e_back(small_t, e)
    a = (h * inverse_rms(h) * gains[0:1, :]).astype(BF)
    a_rows = spread(a, e).astype(BF)
    left[0:64, :] = a_rows
    qkv = ordered(
        first,
        dot(a_rows, own[:, :HALF]).astype(BF),
        dot(a_rows, other[:, :HALF]).astype(BF),
    )
    qkv_ref[...] = qkv
    bias = bias_scores(dot(small_t, b_ref[...], NT)[2:3], toeplitz[...])
    scores = []
    for pair in range(6):
        at = 128 * pair
        scores.append(dot(stacked(qkv[:, at : at + 128]), qkv[:, 768 + at : 896 + at], NT))
    s = jnp.concatenate(scores, axis=0) * 0.125 + bias
    masked = jnp.where(jnp.concatenate([allowed[...]] * 12, axis=0) > 0, s, -1e30)
    raised = jnp.exp(masked - jnp.max(masked, axis=-1, keepdims=True))
    p = raised / jnp.sum(raised, axis=-1, keepdims=True)
    p_ref[...] = p
    p_low = p.astype(BF)
    outs = []
    for pair in range(6):
        at = 128 * pair
        outs.append(unstacked(dot(p_low[at : at + 128], qkv[:, 1536 + at : 1664 + at])))
    o = jnp.concatenate(outs, axis=1)
    o_rows = jnp.where(
        packed_rows(), 0.0, by_e(jnp.concatenate(thirds(o), axis=0).astype(BF), e)
    ).astype(BF)
    left[64:256, :] = o_rows

    def project(block):
        return sum(
            dot(o_rows[64 * t : 64 * t + 64], block[:, OUT_HALF * t : OUT_HALF * (t + 1)])
            for t in range(3)
        )

    mid = h + ordered(first, project(own), project(other))
    mid_ref[...] = mid
    c = (mid * inverse_rms(mid) * gains[1:2, :]).astype(BF)
    c_rows = spread(c, e).astype(BF)
    left[256:320, :] = c_rows
    z = dot(c_rows, small)
    chosen = [
        jnp.sum(jnp.where(lanes(64, 128) == (idx[:, j : j + 1] >> 3), z, 0.0), axis=1, keepdims=True)
        for j in range(2)
    ]
    top = jnp.maximum(chosen[0], chosen[1])
    e0, e1 = jnp.exp(chosen[0] - top), jnp.exp(chosen[1] - top)
    g0, g1 = e0 / (e0 + e1), e1 / (e0 + e1)
    gate_ref[...] = jnp.concatenate([g0, g1], axis=1)
    hot = [slot_mask_rows(idx_t[j : j + 1, :]) for j in range(2)]
    send[:, 0:768] = dot(hot[0] + hot[1], c).astype(BF)
    if not entering:
        lane = lanes(64, 128)
        pieces = []
        for g in (g0, g1):
            row = jnp.zeros((64, 128), F32)
            for n in range(3):
                piece = g.astype(BF).astype(F32)
                row = jnp.where(lane == n, piece, row)
                g = g - piece
            pieces.append(row.astype(BF))
        send[:, 768:896] = dot(
            jnp.concatenate(hot, axis=1), jnp.concatenate(pieces, axis=0)
        ).astype(BF)


def backward_kernel(first_ref, *refs, leaving):
    if leaving:
        (grad, back_y, back_dx, idx_ref, gate_ref, h_ref, mid_ref, qkv_ref, p_ref, own,
         other, e_ref, gains, b_ref, diag_ref, flip_ref,
         ig_ref, extra, own_grads, other_grads) = refs
        y, dx = back_y[...], back_dx[...]
    else:
        (grad, back, idx_ref, gate_ref, h_ref, mid_ref, qkv_ref, p_ref, own,
         other, e_ref, gains, b_ref, diag_ref, flip_ref, gate_0, idx_0,
         ig_ref, extra, own_grads, other_grads, out_ref, send) = refs
        y, dx = back[:, 0:768], back[:, 768:1536]
    first = first_ref[0] == 1
    e = e_ref[...]
    g, gates, idx = grad[...].astype(F32), gate_ref[...], idx_ref[...]
    hot = [slot_mask(idx[:, j : j + 1]) for j in range(2)]
    picked = [dot(hot[j], y) for j in range(2)]
    mid = mid_ref[...]
    g0, g1 = gates[:, 0:1], gates[:, 1:2]
    if not leaving:
        out_ref[...] = (mid + g0 * picked[0] + g1 * picked[1]).astype(BF)
    dg = [jnp.sum(picked[j] * g, axis=1, keepdims=True) for j in range(2)]
    mean = g0 * dg[0] + g1 * dg[1]
    lane = lanes(64, 128)
    dz = jnp.where(lane == (idx[:, 0:1] >> 3), g0 * (dg[0] - mean), 0.0) + jnp.where(
        lane == (idx[:, 1:2] >> 3), g1 * (dg[1] - mean), 0.0
    )
    dz = dz.astype(BF)
    dc = collected(dot(dz, own[:, HALF:], NT), e) + dot(hot[0] + hot[1], dx)
    r2 = inverse_rms(mid)
    n2 = mid * r2
    dgain_two = jnp.sum(dc * n2, axis=0, keepdims=True)
    dmid = g + norm_backward(dc * gains[1:2, :], n2, r2)
    datt = dmid.astype(BF)
    datt_own, datt_other = split(first, datt, OUT_HALF)
    parts = []
    for t in range(3):
        cols = slice(OUT_HALF * t, OUT_HALF * (t + 1))
        parts.append(dot(datt_own, own[:, cols], NT) + dot(datt_other, other[:, cols], NT))
    parts = jnp.where(packed_rows(), 0.0, jnp.concatenate(parts, axis=0)).astype(BF)
    parts = by_e_back(parts, e)
    third = lax.rem(lanes(1, 768), 3)
    do = jnp.where(third == 0, parts[:64], jnp.where(third == 1, parts[64:128], parts[128:]))
    do = do.astype(BF)
    dos = [stacked(do[:, 128 * j : 128 * j + 128]) for j in range(6)]
    p = p_ref[...]
    p_low = p.astype(BF)
    qkv = qkv_ref[...]
    dp = jnp.concatenate(
        [dot(dos[j], qkv[:, 1536 + 128 * j : 1664 + 128 * j], NT) for j in range(6)], axis=0
    )
    ds = (p * (dp - jnp.sum(dp * p, axis=-1, keepdims=True))).astype(BF)
    dq, dk, dv, sums = [], [], [], []
    flip = flip_ref[...]
    for j in range(6):
        at = 128 * j
        ds_pair = ds[at : at + 128]
        dv.append(dot(p_low[at : at + 128], dos[j], TN))
        dq.append(unstacked(dot(ds_pair, qkv[:, 768 + at : 896 + at])) * 0.125)
        dk.append(dot(ds_pair, stacked(qkv[:, at : at + 128]), TN) * 0.125)
        for half in range(2):
            turned = dot(flip, ds_pair[64 * half : 64 * half + 64])
            turned = jnp.concatenate([turned, jnp.zeros((64, 64), F32)], axis=1)
            turned = pltpu.roll(turned, 0, 1, stride=1, stride_axis=0)
            sums.append(jnp.sum(turned, axis=0, keepdims=True))
    sums = jnp.concatenate(sums + [jnp.zeros((4, 128), F32)], axis=0)
    high = sums.astype(BF)
    low = (sums - high.astype(F32)).astype(BF)
    dbias = dot(high, diag_ref[...]) + dot(low, diag_ref[...])
    head = lax.broadcasted_iota(jnp.int32, (16, 384), 0)
    dbias = jnp.sum(jnp.where(head == lanes(16, 384) // 32, dbias, 0.0), axis=0, keepdims=True)
    dqkv = jnp.concatenate(dq + dk + dv, axis=1).astype(BF)
    dqkv_own, dqkv_other = split(first, dqkv, HALF)
    da = collected(dot(dqkv_own, own[:, :HALF], NT) + dot(dqkv_other, other[:, :HALF], NT), e)
    h = h_ref[...].astype(F32)
    r1 = inverse_rms(h)
    n1 = h * r1
    dgain_one = jnp.sum(da * n1, axis=0, keepdims=True)
    ig = (dmid + norm_backward(da * gains[0:1, :], n1, r1)).astype(BF)
    ig_ref[...] = ig
    if not leaving:
        g = ig.astype(F32)
        gate_0, idx_0 = gate_0[...], idx_0[...]
        grads = jnp.concatenate(
            [(gate_0[:, j : j + 1] * g).astype(BF) for j in range(2)], axis=0
        )
        rows = jnp.concatenate([slot_mask_rows(idx_0[j : j + 1, :]) for j in range(2)], axis=1)
        send[...] = dot(rows, grads).astype(BF)
    row = lax.broadcasted_iota(jnp.int32, (16, 1), 0)
    both = jnp.where(row == 0, dgain_one, jnp.where(row == 1, dgain_two, 0.0)).astype(BF)
    dbias = jnp.where(row == 2, dbias, 0.0).astype(BF)
    extra[...] = (spread(both, e) + dot(dbias, b_ref[...])).astype(BF)
    for ref, dqkv_half, datt_half in (
        (own_grads, dqkv_own, datt_own),
        (other_grads, dqkv_other, datt_other),
    ):
        ref[:, 0:HALF] = dqkv_half
        ref[:, HALF:1536] = datt_half
        ref[:, 1536:1664] = dz


class Loaded:
    def __init__(self, source, held, sem):
        self.held, self.waited = held, False
        self.copy = pltpu.make_async_copy(source, held, sem)
        self.copy.start()

    def ready(self):
        if not self.waited:
            self.copy.wait()
            self.waited = True
        return self.held

    def __getitem__(self, at):
        return self.ready()[at]


class Stored:
    def __init__(self, target, held, fresh):
        self.target, self.held, self.fresh, self.copies = target, held, fresh, []

    def __setitem__(self, at, value):
        self.held[at] = value
        self.send(at)

    def __getitem__(self, at):
        return self.held[at]

    def send(self, at):
        source, target = (self.held, self.target)
        if at is not Ellipsis:
            source, target = source.at[at], target.at[at]
        self.copies.append(pltpu.make_async_copy(source, target, self.fresh()))
        self.copies[-1].start()

    def wait(self):
        for copy in self.copies:
            copy.wait()


def call(kernel, args, outs, flops, raw=0, scratch=(), direct=(), keeps=(), order=()):
    flag, *arrays = args
    n_in, n_out = len(arrays), len(outs)
    staged = [j for j in range(n_in - raw) if j not in direct]
    staged = list(order) + [j for j in staged if j not in order]
    n_held = len(staged) + n_out

    def body(flag, *refs):
        ins, results = list(refs[:n_in]), refs[n_in : n_in + n_out]
        copied = refs[n_in + n_out : n_in + n_out + len(keeps)]
        held = refs[n_in + n_out + len(keeps) :]
        own, sems = held[n_held:-1], held[-1]
        count = iter(range(SEMS))

        def fresh():
            return sems.at[next(count)]

        moves = []
        for (j, cols), target in zip(keeps, copied):
            moves.append(pltpu.make_async_copy(ins[j].at[:, cols], target, fresh()))
            moves[-1].start()
        for n, j in enumerate(staged):
            ins[j] = Loaded(ins[j], held[n], fresh())
        stored = [Stored(results[j], held[len(staged) + j], fresh) for j in range(n_out)]
        kernel(flag, *ins, *stored, *own)
        for j in staged:
            ins[j].ready()
        for item in stored + moves:
            item.wait()

    hbm = pl.BlockSpec(memory_space=pltpu.HBM)
    spaces = [pltpu.VMEM if j in direct else pltpu.HBM for j in range(n_in)]
    kept = [
        pltpu.HBM((arrays[j].shape[0], cols.stop - cols.start), arrays[j].dtype)
        for j, cols in keeps
    ]
    return pl.pallas_call(
        body,
        in_specs=[pl.BlockSpec(memory_space=pltpu.SMEM)]
        + [pl.BlockSpec(memory_space=space) for space in spaces],
        out_specs=[hbm] * (n_out + len(keeps)),
        out_shape=[pltpu.HBM(*out) for out in outs] + kept,
        scratch_shapes=[pltpu.VMEM(arrays[j].shape, arrays[j].dtype) for j in staged]
        + [pltpu.VMEM(*out) for out in outs]
        + list(scratch)
        + [pltpu.SemaphoreType.DMA((SEMS,))],
        compiler_params=pltpu.CompilerParams(vmem_limit_bytes=VMEM_BYTES),
        cost_estimate=pl.CostEstimate(flops=flops, bytes_accessed=12000000, transcendentals=50000),
    )(flag, *(pltpu.with_memory_space_constraint(x, space) for x, space in zip(arrays, spaces)))


KEPT = [
    ((64, 768), BF),
    ((64, 2304), BF),
    ((768, 64), F32),
    ((320, 1024), BF),
    ((64, 768), F32),
    ((64, 2), F32),
    ((16, 768), F32),
]


def place_kernel(first_ref, grad, idx_t, rows):
    idx_t = idx_t[...]
    hot = slot_mask_rows(idx_t[0:1, :]) + slot_mask_rows(idx_t[1:2, :])
    rows[...] = dot(hot, grad[...]).astype(BF)


def copies_kernel(first_ref, mine, theirs, copies, block_1):
    first = first_ref[0] == 1
    mine, theirs = mine[...], theirs[...]
    block = lax.select(first, mine, theirs)
    block_1[...] = lax.select(first, theirs, mine)
    for at in range(0, 64, 16):
        copies[at : at + 16] = jnp.broadcast_to(block[None], (16, 16, PACK))


def totals_block(refs, at):
    left, extra, grads, left_t, extra_t, grads_t = refs
    cols = slice(256 * at, 256 * at + 256)
    grads = jnp.concatenate([grads[...], grads_t[...]], axis=0)

    def rows(lo, hi):
        return jnp.concatenate([left[lo:hi, cols], left_t[lo:hi, cols]], axis=0)

    main = dot(rows(0, 64), grads[:, :HALF], TN)
    outs = [
        dot(rows(64 + 64 * t, 128 + 64 * t), grads[:, HALF:1536], TN) for t in range(3)
    ]
    marks = lax.broadcasted_iota(jnp.int32, (16, 128), 0) + 32 == lanes(16, 128)
    marks = ((lax.broadcasted_iota(jnp.int32, (16, 128), 0) < 3) & marks).astype(F32).astype(BF)
    rest = dot(
        jnp.concatenate([rows(256, 320), extra[:, cols], extra_t[:, cols]], axis=0),
        jnp.concatenate([grads[:, 1536:], marks, marks], axis=0),
        TN,
    )
    main = main + jnp.concatenate(outs, axis=1)
    return main.astype(BF).reshape(16, 16, HALF), rest.astype(BF).reshape(16, 16, 128)


def totals_early(flag, *refs):
    wide, narrow = refs[6:]
    for at in range(4):
        rows = slice(16 * at, 16 * at + 16)
        wide[rows], narrow[rows] = totals_block(refs[:6], at)


def totals_late(flag, *refs):
    narrow, out = refs[6:]
    for at in range(4):
        rows = slice(16 * at, 16 * at + 16)
        main, rest = totals_block(refs[:6], at)
        out[rows] = jnp.concatenate(
            [main, lax.select(flag[0] == 1, rest, narrow[rows])], axis=2
        )


def dense_totals(kernel, flag, operands, outs, more=()):
    left, left_t, extra, own_grads, other_grads = operands
    args = (flag, left, extra, own_grads, left_t, swap(extra), swap(other_grads), *more)
    return call(kernel, args, outs, 0, direct=(3, 4, 5))


def reduce_kernel(first_ref, parts_0, parts_1, mine, send, tail):
    first = first_ref[0] == 1
    parts_1 = parts_1.ready()

    def total(parts, cols, width):
        def add(j, value):
            return value + parts[j, :, cols].astype(F32)

        return lax.fori_loop(0, 64, add, jnp.zeros((16, width), F32), unroll=16)

    for at in range(0, HALF, OUT_HALF):
        cols = slice(at, at + OUT_HALF)
        sums = [total(parts, cols, OUT_HALF) for parts in (parts_0, parts_1)]
        mine[:, cols] = lax.select(first, sums[0], sums[1])
        send[:, cols] = lax.select(first, sums[1], sums[0])
    tail[...] = total(parts_0, slice(HALF, PACK), 128)


def unpack_kernel(first_ref, mine, theirs, tail, qkv, out, router, one, two, bias):
    first = first_ref[0] == 1
    halves = [
        lax.select(first, mine[...], theirs[...]),
        lax.select(first, theirs[...], mine[...]),
    ]
    qkv[...] = jnp.concatenate([block[:12, :HALF] for block in halves], axis=1).reshape(
        12, 1, 2304
    )
    row = lax.broadcasted_iota(jnp.int32, (12, 1), 0)
    wide = []
    for block in halves:
        total = jnp.zeros((12, OUT_HALF), F32)
        for j in range(4):
            for t in range(3):
                part = block[12 + j : 13 + j, OUT_HALF * t : OUT_HALF * (t + 1)]
                total = jnp.where(row == 3 * j + t, part, total)
        wide.append(total)
    out[...] = jnp.concatenate(wide, axis=1).reshape(12, 1, 768)
    rest = tail[...][:12]
    router[...] = rest[:, :32].reshape(12, 1, 32)
    on_diagonal = lax.broadcasted_iota(jnp.int32, (12, 12), 0) == lanes(12, 12)

    def row(at):
        return jnp.sum(jnp.where(on_diagonal, rest[:, at : at + 1], 0.0), axis=0, keepdims=True)

    one[...] = row(32)
    two[...] = row(33)
    bias[...] = row(34)[:, :6]


def pack_kernel(first_ref, qkv, out, router, one, two, bias, mine, send):
    first = first_ref[0] == 1
    on_diagonal = lax.broadcasted_iota(jnp.int32, (12, 12), 0) == lanes(12, 12)

    def column(ref, width):
        wide = jnp.broadcast_to(ref[...].astype(F32), (12, width))
        return jnp.sum(jnp.where(on_diagonal[:, :width], wide, 0.0), axis=1, keepdims=True)

    lane = lanes(12, 128)
    rest = jnp.concatenate([router[0].astype(F32), jnp.zeros((12, 96), F32)], axis=1)
    for at, value in ((32, column(one, 12)), (33, column(two, 12)), (34, column(bias, 6))):
        rest = jnp.where(lane == at, value, rest)
    rest = jnp.concatenate([rest, jnp.zeros((4, 128), F32)], axis=0)
    outs = out[0].astype(F32)
    blocks = []
    for half in range(2):
        cols = slice(OUT_HALF * half, OUT_HALF * (half + 1))
        thin = [
            jnp.concatenate([outs[3 * j + t : 3 * j + t + 1, cols] for j in range(4)], axis=0)
            for t in range(3)
        ]
        rows = jnp.concatenate(
            [qkv[0, :, HALF * half : HALF * (half + 1)].astype(F32), jnp.concatenate(thin, axis=1)],
            axis=0,
        )
        blocks.append(jnp.concatenate([rows, rest], axis=1).astype(BF))
    mine[...] = lax.select(first, blocks[0], blocks[1])
    send[...] = lax.select(first, blocks[1], blocks[0])


def gelu_parts(u):
    inner = 0.7978845608028654 * (u + 0.044715 * (u * u * u))
    t = jnp.tanh(inner)
    half = 0.5 * (1.0 + t)
    slope = 0.7978845608028654 * (1.0 + 3 * 0.044715 * (u * u))
    return u * half, half + 0.5 * u * (1.0 - t * t) * slope


def load_weights(chosen, mine, theirs, held, sems, order=(0, 1)):
    for cond, refs in ((chosen, mine), (jnp.logical_not(chosen), theirs)):

        @pl.when(cond)
        def _(refs=refs):
            for j in order:
                pltpu.make_async_copy(refs[j], held[j], sems.at[j]).start()

    return [pltpu.make_async_copy(mine[j], held[j], sems.at[j]) for j in range(2)]


def chunks():
    return [(n, slice(CHUNK * n, CHUNK * n + CHUNK)) for n in range(1536 // CHUNK)]


def expert_forward(flag, x, in_mine, in_theirs, out_mine, out_theirs, y, hid, slope, w1, w2, sems):
    copies = load_weights(
        flag[0] == 1, (in_mine, out_mine), (in_theirs, out_theirs), (w1, w2), sems
    )
    total = None
    for at, cols in chunks():
        if at == 0:
            copies[0].wait()
        value, grad = gelu_parts(dot(x[...], w1[:, cols]))
        value = value.astype(BF)
        hid[:, cols] = value
        slope[:, cols] = grad.astype(BF)
        if at == 0:
            copies[1].wait()
        part = dot(value, w2[cols, :])
        total = part if total is None else total + part
    y[...] = total.astype(BF)


def expert_both(
    flag, arrived, grad, in_mine, in_theirs, out_mine, out_theirs, back, hid, du, dy_out,
    w1, w2, sems,
):
    copies = load_weights(
        flag[0] == 0, (in_mine, out_mine), (in_theirs, out_theirs), (w1, w2), sems
    )
    x = arrived[:, 0:768]
    gate = jnp.sum(arrived[:, 768:896].astype(F32), axis=1, keepdims=True)
    dy = (gate * grad[...].astype(F32)).astype(BF)
    dy_out[...] = dy
    total, total_dx = None, None
    for at, cols in chunks():
        if at == 0:
            copies[0].wait()
        value, grad = gelu_parts(dot(x, w1[:, cols]))
        value = value.astype(BF)
        hid[:, cols] = value
        if at == 0:
            copies[1].wait()
        part = dot(value, w2[cols, :])
        pre = (dot(dy, w2[cols, :], NT) * grad).astype(BF)
        du[:, cols] = pre
        part_dx = dot(pre, w1[:, cols], NT)
        total = part if total is None else total + part
        total_dx = part_dx if total_dx is None else total_dx + part_dx
    back[:, 0:768] = total.astype(BF)
    back[:, 768:1536] = total_dx.astype(BF)


def expert_backward(
    flag, dy, slope, in_mine, in_theirs, out_mine, out_theirs, dx, du, w1, w2, sems
):
    copies = load_weights(
        flag[0] == 1, (in_mine, out_mine), (in_theirs, out_theirs), (w1, w2), sems, (1, 0)
    )
    total = None
    for at, cols in chunks():
        if at == 0:
            copies[1].wait()
        pre = (dot(dy[...], w2[cols, :], NT) * slope[:, cols].astype(F32)).astype(BF)
        du[:, cols] = pre
        if at == 0:
            copies[0].wait()
        part = dot(pre, w1[:, cols], NT)
        total = part if total is None else total + part
    dx[...] = total.astype(BF)


def call_expert(kernel, flag, acts, weights, outs, flops, keeps):
    return call(
        kernel,
        (flag, *acts, *weights),
        [(out, BF) for out in outs],
        flops,
        4,
        [
            pltpu.VMEM((768, 1536), BF),
            pltpu.VMEM((1536, 768), BF),
            pltpu.SemaphoreType.DMA((2,)),
        ],
        (0,),
        keeps,
    )


def body(
    inputs, cotangent, segments, routes, slots, qkv_weight, out_weight, router_weight, gain_one,
    gain_two, bias_table, w_in, w_out,
):
    section = lax.axis_index("section")
    first = section == 0

    def pick(pair):
        return jnp.where(first, pair[0], pair[1])

    def pick_other(pair):
        return jnp.where(first, pair[1], pair[0])

    e, b_rows, diagonals, flip, toeplitz = (jnp.asarray(x, BF) for x in selections())
    flag = first.astype(jnp.int32).reshape(1)
    mine, theirs = call(
        pack_kernel,
        (flag, qkv_weight, out_weight, router_weight, gain_one, gain_two, bias_table),
        [((16, PACK), BF)] * 2,
        0,
    )
    theirs = swap(theirs)
    w_in_other, w_out_other = swap(w_in[0, 0]), swap(w_out[0, 0])
    flat = routes[0] * 8 + slots[0]
    flat_mine, flat_theirs = pick(flat), swap(pick_other(flat))

    copies_0, block_1 = call(
        copies_kernel, (flag, mine, theirs), [((64, 16, PACK), BF), ((16, PACK), BF)], 0
    )
    got_0 = a2a(copies_0).reshape(1024, PACK)
    got_1 = lax.all_gather(block_1, "dp", axis=0, tiled=True)
    idx_pair = (flat_mine, flat_theirs)
    idx_0, idx_1 = pick(idx_pair), pick_other(idx_pair)

    g1 = pick(cotangent)
    seg = pick(segments)
    places = np.arange(64)
    allowed = jnp.asarray(places[:, None] >= places[None, :]) & (seg[:, None] == seg[None, :])

    allowed = allowed.astype(F32)
    grad_rows = call(place_kernel, (flag, g1, idx_1.T), [((512, 768), BF)], 50000000)[0]
    ready = (grad_rows, w_in_other, w_out_other, pick(inputs), allowed, idx_0, idx_0.T)
    got_0, ready = lax.optimization_barrier((got_0, ready))
    grad_rows, w_in_other, w_out_other, x_in, allowed, idx_0, idx_0_t = ready
    weights = (w_in[0, 0], w_in_other, w_out[0, 0], w_out_other)
    dense_0 = (got_0, swap(got_0))
    grad_rows = a2a(grad_rows.reshape(64, 8, 768)).reshape(512, 768)

    h_0, qkv_0, p_0, left_0, mid_0, gate_0, gains_0, send_0 = call(
        functools.partial(forward_kernel, entering=True),
        (flag, x_in, *dense_0, e, b_rows, toeplitz, allowed, idx_0, idx_0_t),
        KEPT + [((512, 768), BF)],
        500000000,
        direct=(1, 2),
        order=(0, 3),
    )
    send_0, grad_rows = lax.optimization_barrier((send_0, grad_rows))
    x_0 = a2a(send_0.reshape(64, 8, 768)).reshape(512, 768)
    left_0_theirs = swap(left_0)
    y_0, hid_0, slope_0, x_0 = call_expert(
        expert_forward, flag, (x_0,), weights, [(512, 768), (512, 1536), (512, 1536)],
        2500000000, ((0, WIDE),),
    )
    got_1, y_0 = lax.optimization_barrier((got_1, y_0))
    dense_1 = (got_1, swap(got_1))
    back_0 = a2a(y_0.reshape(64, 8, 768)).reshape(512, 768)

    h_1, qkv_1, p_1, left_1, mid_1, gate_1, gains_1, send_1, back_0 = call(
        functools.partial(forward_kernel, entering=False),
        (flag, mid_0, gate_0, idx_0, back_0, *dense_1, e, b_rows, toeplitz, allowed,
         idx_1, idx_1.T),
        KEPT + [((512, 896), BF)],
        700000000,
        direct=(3, 5),
        order=(0, 1, 2, 6, 4),
        keeps=((3, WIDE),),
    )
    arrived = a2a(send_1.reshape(64, 8, 896)).reshape(512, 896)
    left_1_theirs = swap(left_1)
    back_1, hid_1, du_1, dy_1, x_1 = call_expert(
        expert_both, flag, (arrived, grad_rows), weights, [(512, 1536)] * 3 + [(512, 768)],
        5000000000, ((0, WIDE),),
    )
    back_1 = a2a(back_1.reshape(64, 8, 1536)).reshape(512, 1536)
    operands = [((16, 1024), BF), ((64, 1664), BF), ((64, 1664), BF)]
    ig_1, extra_1, own_1, other_1, out_1, send_0 = call(
        functools.partial(backward_kernel, leaving=False),
        (flag, g1, back_1, idx_1, gate_1, h_1, mid_1, qkv_1, p_1, *dense_1, e, gains_1,
         b_rows, diagonals, flip, gate_0, idx_0_t),
        [((64, 768), BF)] + operands + [((64, 768), BF), ((512, 768), BF)],
        1000000000,
        direct=(1,),
        order=(0, 2, 3, 5, 10, 11, 8, 9, 7, 6),
    )

    total_1, narrow_1 = dense_totals(
        totals_early, flag, (left_1, left_1_theirs, extra_1, own_1, other_1),
        [((64, 16, HALF), BF), ((64, 16, 128), BF)],
    )

    dy_0 = a2a(send_0.reshape(64, 8, 768)).reshape(512, 768)
    dy_0, total_1 = lax.optimization_barrier((dy_0, total_1))
    dx_0, du_0, dy_0 = call_expert(
        expert_backward, flag, (dy_0, slope_0), weights, [(512, 768), (512, 1536)],
        2500000000, ((0, WIDE),),
    )
    dx_rows = a2a(dx_0.reshape(64, 8, 768)).reshape(512, 768)
    dx_rows, total_1 = lax.optimization_barrier((dx_rows, total_1))
    total_1 = a2a(total_1)
    ig_0, extra_0, own_0, other_0 = call(
        functools.partial(backward_kernel, leaving=True),
        (flag, ig_1, back_0, dx_rows, idx_0, gate_0, h_0, mid_0, qkv_0, p_0, *dense_0, e,
         gains_0, b_rows, diagonals, flip),
        [((64, 768), BF)] + operands,
        1000000000,
        direct=(2,),
        order=(0, 3, 4, 1, 6, 11, 12, 9, 10, 8, 7),
    )
    (total_0,) = dense_totals(
        totals_late, flag, (left_0, left_0_theirs, extra_0, own_0, other_0),
        [((64, 16, PACK), BF)], (narrow_1,),
    )
    total_1, total_0 = lax.optimization_barrier((total_1, total_0))
    total_0 = a2a(total_0)

    acts = [(x_0, x_1), (du_0, du_1), (hid_0, hid_1), (dy_0, dy_1)]
    xs, dus, hids, dys = [
        jnp.concatenate([pick(pair), swap(pick_other(pair))], axis=0) for pair in acts
    ]
    grad_in = dot(xs, dus, TN)
    grad_out = dot(hids, dys, TN)

    total_0, grad_in, grad_out = lax.optimization_barrier((total_0, grad_in, grad_out))
    red_mine, red_theirs, tail = call(
        reduce_kernel, (flag, total_0, total_1),
        [((16, HALF), F32)] * 2 + [((16, 128), F32)], 0, direct=(0,),
    )
    dense = call(
        unpack_kernel,
        (flag, red_mine, swap(red_theirs), tail),
        [((12, 1, 2304), F32), ((12, 1, 768), F32), ((12, 1, 32), F32)]
        + [((1, 12), F32)] * 2
        + [((1, 6), F32)],
        0,
    )

    def by_micro(values):
        own, other = pick(values), swap(pick_other(values))
        return jnp.stack([pick((own, other)), pick((other, own))])[None]

    return (
        by_micro((h_1, out_1)),
        by_micro((ig_0, ig_1)),
        *(x.transpose(1, 0, 2) for x in dense[:3]),
        *dense[3:],
        grad_in[None, None],
        grad_out[None, None],
    )


def solution(mesh):
    placed = (
        P(None, "dp", None),
        P(None, "dp", None),
        P(None, "dp"),
        P("section", None, "dp", None),
        P("section", None, "dp", None),
        P("section", "dp", None),
        P("section", "dp", None),
        P("section", "dp", None),
        P("section", "dp"),
        P("section", "dp"),
        P("section", "dp"),
        P("section", "dp", None, None),
        P("section", "dp", None, None),
    )
    return jax.shard_map(
        body,
        mesh=mesh,
        in_specs=placed,
        out_specs=(
            P("section", None, "dp", None),
            P("section", None, "dp", None),
            P("section", "dp", None),
            P("section", "dp", None),
            P("section", "dp", None),
            P("section", "dp"),
            P("section", "dp"),
            P("section", "dp"),
            P("section", "dp", None, None),
            P("section", "dp", None, None),
        ),
        check_vma=False,
    )
```

```python
import functools

import jax
import jax.numpy as jnp
import numpy as np
from jax import lax
from jax.experimental import pallas as pl
from jax.experimental.pallas import tpu as pltpu
from jax.sharding import PartitionSpec as P

BUCKETS = 32
EPS = 1e-06
F32 = jnp.float32
BF = jnp.bfloat16
SWAP = [(0, 1), (1, 0)]
NT = (((1,), (1,)), ((), ()))
TN = (((0,), (0,)), ((), ()))
HALF = 1152
PACK = 1280
OUT_HALF = 384
VMEM_BYTES = 40 * 2**20
SEMS = 40
WIDE = slice(0, 768)
CHUNK = 768


def bucket_table(length, count):
    places = np.arange(length)
    distance = np.maximum(places[:, None] - places[None, :], 0)
    safe_distance = np.maximum(distance, 1)
    near_count = count // 2
    far_bucket = near_count + np.floor(
        np.log(safe_distance / near_count) / np.log(128.0 / near_count) * near_count
    ).astype(np.int32)
    return np.where(distance < near_count, distance, np.minimum(far_bucket, count - 1)).astype(
        np.int32
    )


def selections():
    rows = np.zeros((384, 512), np.float32)
    for f in range(384):
        d, r = divmod(f, 12)
        rows[f, 16 * d + r] = 1
        rows[f, 16 * d + 12 + r // 3] = 1
    bias = np.zeros((384, 1024), np.float32)
    for b in range(384):
        bias[b, 16 * (b // 6) + b % 6] = 1
    buckets = bucket_table(64, BUCKETS)[:, 0]
    diagonals = np.zeros((128, 384), np.float32)
    for delta in range(64):
        diagonals[63 - delta, buckets[delta] :: BUCKETS] = 1
    toeplitz = np.zeros((384, 128), np.float32)
    for delta in range(64):
        toeplitz[buckets[delta] :: BUCKETS, (128 - delta) % 128] = 1
    return rows, bias, diagonals, np.eye(64)[::-1], toeplitz


def dot(a, b, dims=(((1,), (0,)), ((), ()))):
    return lax.dot_general(a, b, dims, preferred_element_type=F32)


def inverse_rms(value):
    return lax.rsqrt(jnp.mean(value * value, axis=-1, keepdims=True) + EPS)


def norm_backward(grad_normed, normed, scale):
    return scale * (grad_normed - normed * jnp.mean(grad_normed * normed, axis=-1, keepdims=True))


def a2a(block):
    return lax.all_to_all(block, "dp", split_axis=0, concat_axis=0, tiled=True)


def swap(block):
    return lax.ppermute(block, "section", SWAP)


def lanes(rows, width):
    return lax.broadcasted_iota(jnp.int32, (rows, width), 1)


def ordered(first, mine, theirs):
    return jnp.concatenate(
        [lax.select(first, mine, theirs), lax.select(first, theirs, mine)], axis=1
    )


def split(first, block, width):
    left, right = block[:, :width], block[:, width:]
    return lax.select(first, left, right), lax.select(first, right, left)


def packed_rows():
    return lax.rem(lanes(1, 1024), 16) < 12


def thirds(o):
    third = lax.rem(lanes(1, 768), 3)
    return [jnp.where(third == t, o, 0.0) for t in range(3)]


def by_e(value, e):
    return jnp.concatenate([dot(value[:, :384], e), dot(value[:, 384:], e)], axis=1)


def by_e_back(value, e):
    return jnp.concatenate([dot(value[:, :512], e, NT), dot(value[:, 512:], e, NT)], axis=1)


def spread(value, e):
    return jnp.where(packed_rows(), by_e(value, e), 0.0)


def collected(value, e):
    value = jnp.where(packed_rows(), value, 0.0)
    high = value.astype(BF)
    low = (value - high.astype(F32)).astype(BF)
    both = by_e_back(jnp.concatenate([high, low], axis=0), e)
    return both[:64] + both[64:]


def slot_mask(idx):
    row = lanes(64, 512)
    return ((row >> 4) * 8 + (row & 7) == idx).astype(F32).astype(BF)


def slot_mask_rows(idx_row):
    row = lax.broadcasted_iota(jnp.int32, (512, 64), 0)
    return ((row >> 4) * 8 + (row & 7) == idx_row).astype(F32).astype(BF)


def mixed_out(mid, gates, idx, back):
    out = mid
    for j in range(2):
        picked = dot(slot_mask(idx[:, j : j + 1]), back)
        out = out + gates[:, j : j + 1] * picked
    return out


def pair_masks():
    low = (lanes(1, 128) < 64).astype(F32).astype(BF)
    return low, (1.0 - low.astype(F32)).astype(BF)


def stacked(pair):
    low, high = pair_masks()
    return jnp.concatenate([pair * low, pair * high], axis=0)


def unstacked(both):
    return jnp.where(lanes(1, 128) < 64, both[:64], both[64:])


def bias_scores(row, toeplitz):
    head = lax.broadcasted_iota(jnp.int32, (16, 384), 0)
    table = jnp.where(head == lanes(16, 384) // 32, row, 0.0).astype(BF)
    table = dot(table, toeplitz)
    heads = []
    for j in range(12):
        wide = jnp.broadcast_to(table[j : j + 1], (64, 128))
        heads.append(pltpu.roll(wide, 0, 1, stride=1, stride_axis=0)[:, :64])
    return jnp.concatenate(heads, axis=0)


def forward_kernel(
    first_ref, *refs, entering,
):
    if entering:
        (h_ref, own, other, e_ref, b_ref, toeplitz, allowed, idx, idx_t,
         h_out, qkv_ref, p_ref, left, mid_ref, gate_ref, gains, send) = refs
        h = h_ref[...].astype(F32)
    else:
        (mid_0, gate_0, idx_0, back_0, own, other, e_ref, b_ref, toeplitz, allowed, idx,
         idx_t, h_out, qkv_ref, p_ref, left, mid_ref, gate_ref, gains, send) = refs
        h = mixed_out(mid_0[...], gate_0[...], idx_0[...], back_0[...]).astype(BF).astype(F32)
    first = first_ref[0] == 1
    h_out[...] = h.astype(BF)
    e = e_ref[...]
    idx, idx_t = idx[...], idx_t[...]
    small = own[:, HALF:]
    small_t = small.astype(F32).T[32:48].astype(BF)
    gains[...] = by_e_back(small_t, e)
    a = (h * inverse_rms(h) * gains[0:1, :]).astype(BF)
    a_rows = spread(a, e).astype(BF)
    left[0:64, :] = a_rows
    qkv = ordered(
        first,
        dot(a_rows, own[:, :HALF]).astype(BF),
        dot(a_rows, other[:, :HALF]).astype(BF),
    )
    qkv_ref[...] = qkv
    bias = bias_scores(dot(small_t, b_ref[...], NT)[2:3], toeplitz[...])
    scores = []
    for pair in range(6):
        at = 128 * pair
        scores.append(dot(stacked(qkv[:, at : at + 128]), qkv[:, 768 + at : 896 + at], NT))
    s = jnp.concatenate(scores, axis=0) * 0.125 + bias
    masked = jnp.where(jnp.concatenate([allowed[...]] * 12, axis=0) > 0, s, -1e30)
    raised = jnp.exp(masked - jnp.max(masked, axis=-1, keepdims=True))
    p = raised / jnp.sum(raised, axis=-1, keepdims=True)
    p_ref[...] = p
    p_low = p.astype(BF)
    outs = []
    for pair in range(6):
        at = 128 * pair
        outs.append(unstacked(dot(p_low[at : at + 128], qkv[:, 1536 + at : 1664 + at])))
    o = jnp.concatenate(outs, axis=1)
    o_rows = jnp.where(
        packed_rows(), 0.0, by_e(jnp.concatenate(thirds(o), axis=0).astype(BF), e)
    ).astype(BF)
    left[64:256, :] = o_rows

    def project(block):
        return sum(
            dot(o_rows[64 * t : 64 * t + 64], block[:, OUT_HALF * t : OUT_HALF * (t + 1)])
            for t in range(3)
        )

    mid = h + ordered(first, project(own), project(other))
    mid_ref[...] = mid
    c = (mid * inverse_rms(mid) * gains[1:2, :]).astype(BF)
    c_rows = spread(c, e).astype(BF)
    left[256:320, :] = c_rows
    z = dot(c_rows, small)
    chosen = [
        jnp.sum(jnp.where(lanes(64, 128) == (idx[:, j : j + 1] >> 3), z, 0.0), axis=1, keepdims=True)
        for j in range(2)
    ]
    top = jnp.maximum(chosen[0], chosen[1])
    e0, e1 = jnp.exp(chosen[0] - top), jnp.exp(chosen[1] - top)
    g0, g1 = e0 / (e0 + e1), e1 / (e0 + e1)
    gate_ref[...] = jnp.concatenate([g0, g1], axis=1)
    hot = [slot_mask_rows(idx_t[j : j + 1, :]) for j in range(2)]
    send[:, 0:768] = dot(hot[0] + hot[1], c).astype(BF)
    if not entering:
        lane = lanes(64, 128)
        pieces = []
        for g in (g0, g1):
            row = jnp.zeros((64, 128), F32)
            for n in range(3):
                piece = g.astype(BF).astype(F32)
                row = jnp.where(lane == n, piece, row)
                g = g - piece
            pieces.append(row.astype(BF))
        send[:, 768:896] = dot(
            jnp.concatenate(hot, axis=1), jnp.concatenate(pieces, axis=0)
        ).astype(BF)


def backward_kernel(first_ref, *refs, leaving):
    if leaving:
        (grad, back_y, back_dx, idx_ref, gate_ref, h_ref, mid_ref, qkv_ref, p_ref, own,
         other, e_ref, gains, b_ref, diag_ref, flip_ref,
         ig_ref, extra, own_grads, other_grads) = refs
        y, dx = back_y[...], back_dx[...]
    else:
        (grad, back, idx_ref, gate_ref, h_ref, mid_ref, qkv_ref, p_ref, own,
         other, e_ref, gains, b_ref, diag_ref, flip_ref, gate_0, idx_0,
         ig_ref, extra, own_grads, other_grads, out_ref, send) = refs
        y, dx = back[:, 0:768], back[:, 768:1536]
    first = first_ref[0] == 1
    e = e_ref[...]
    g, gates, idx = grad[...].astype(F32), gate_ref[...], idx_ref[...]
    hot = [slot_mask(idx[:, j : j + 1]) for j in range(2)]
    picked = [dot(hot[j], y) for j in range(2)]
    mid = mid_ref[...]
    g0, g1 = gates[:, 0:1], gates[:, 1:2]
    if not leaving:
        out_ref[...] = (mid + g0 * picked[0] + g1 * picked[1]).astype(BF)
    dg = [jnp.sum(picked[j] * g, axis=1, keepdims=True) for j in range(2)]
    mean = g0 * dg[0] + g1 * dg[1]
    lane = lanes(64, 128)
    dz = jnp.where(lane == (idx[:, 0:1] >> 3), g0 * (dg[0] - mean), 0.0) + jnp.where(
        lane == (idx[:, 1:2] >> 3), g1 * (dg[1] - mean), 0.0
    )
    dz = dz.astype(BF)
    dc = collected(dot(dz, own[:, HALF:], NT), e) + dot(hot[0] + hot[1], dx)
    r2 = inverse_rms(mid)
    n2 = mid * r2
    dgain_two = jnp.sum(dc * n2, axis=0, keepdims=True)
    dmid = g + norm_backward(dc * gains[1:2, :], n2, r2)
    datt = dmid.astype(BF)
    datt_own, datt_other = split(first, datt, OUT_HALF)
    parts = []
    for t in range(3):
        cols = slice(OUT_HALF * t, OUT_HALF * (t + 1))
        parts.append(dot(datt_own, own[:, cols], NT) + dot(datt_other, other[:, cols], NT))
    parts = jnp.where(packed_rows(), 0.0, jnp.concatenate(parts, axis=0)).astype(BF)
    parts = by_e_back(parts, e)
    third = lax.rem(lanes(1, 768), 3)
    do = jnp.where(third == 0, parts[:64], jnp.where(third == 1, parts[64:128], parts[128:]))
    do = do.astype(BF)
    dos = [stacked(do[:, 128 * j : 128 * j + 128]) for j in range(6)]
    p = p_ref[...]
    p_low = p.astype(BF)
    qkv = qkv_ref[...]
    dp = jnp.concatenate(
        [dot(dos[j], qkv[:, 1536 + 128 * j : 1664 + 128 * j], NT) for j in range(6)], axis=0
    )
    ds = (p * (dp - jnp.sum(dp * p, axis=-1, keepdims=True))).astype(BF)
    dq, dk, dv, sums = [], [], [], []
    flip = flip_ref[...]
    for j in range(6):
        at = 128 * j
        ds_pair = ds[at : at + 128]
        dv.append(dot(p_low[at : at + 128], dos[j], TN))
        dq.append(unstacked(dot(ds_pair, qkv[:, 768 + at : 896 + at])) * 0.125)
        dk.append(dot(ds_pair, stacked(qkv[:, at : at + 128]), TN) * 0.125)
        for half in range(2):
            turned = dot(flip, ds_pair[64 * half : 64 * half + 64])
            turned = jnp.concatenate([turned, jnp.zeros((64, 64), F32)], axis=1)
            turned = pltpu.roll(turned, 0, 1, stride=1, stride_axis=0)
            sums.append(jnp.sum(turned, axis=0, keepdims=True))
    sums = jnp.concatenate(sums + [jnp.zeros((4, 128), F32)], axis=0)
    high = sums.astype(BF)
    low = (sums - high.astype(F32)).astype(BF)
    dbias = dot(high, diag_ref[...]) + dot(low, diag_ref[...])
    head = lax.broadcasted_iota(jnp.int32, (16, 384), 0)
    dbias = jnp.sum(jnp.where(head == lanes(16, 384) // 32, dbias, 0.0), axis=0, keepdims=True)
    dqkv = jnp.concatenate(dq + dk + dv, axis=1).astype(BF)
    dqkv_own, dqkv_other = split(first, dqkv, HALF)
    da = collected(dot(dqkv_own, own[:, :HALF], NT) + dot(dqkv_other, other[:, :HALF], NT), e)
    h = h_ref[...].astype(F32)
    r1 = inverse_rms(h)
    n1 = h * r1
    dgain_one = jnp.sum(da * n1, axis=0, keepdims=True)
    ig = (dmid + norm_backward(da * gains[0:1, :], n1, r1)).astype(BF)
    ig_ref[...] = ig
    if not leaving:
        g = ig.astype(F32)
        gate_0, idx_0 = gate_0[...], idx_0[...]
        grads = jnp.concatenate(
            [(gate_0[:, j : j + 1] * g).astype(BF) for j in range(2)], axis=0
        )
        rows = jnp.concatenate([slot_mask_rows(idx_0[j : j + 1, :]) for j in range(2)], axis=1)
        send[...] = dot(rows, grads).astype(BF)
    row = lax.broadcasted_iota(jnp.int32, (16, 1), 0)
    both = jnp.where(row == 0, dgain_one, jnp.where(row == 1, dgain_two, 0.0)).astype(BF)
    dbias = jnp.where(row == 2, dbias, 0.0).astype(BF)
    extra[...] = (spread(both, e) + dot(dbias, b_ref[...])).astype(BF)
    for ref, dqkv_half, datt_half in (
        (own_grads, dqkv_own, datt_own),
        (other_grads, dqkv_other, datt_other),
    ):
        ref[:, 0:HALF] = dqkv_half
        ref[:, HALF:1536] = datt_half
        ref[:, 1536:1664] = dz


class Loaded:
    def __init__(self, source, held, sem):
        self.held, self.waited = held, False
        self.copy = pltpu.make_async_copy(source, held, sem)
        self.copy.start()

    def ready(self):
        if not self.waited:
            self.copy.wait()
            self.waited = True
        return self.held

    def __getitem__(self, at):
        return self.ready()[at]


class Stored:
    def __init__(self, target, held, fresh):
        self.target, self.held, self.fresh, self.copies = target, held, fresh, []

    def __setitem__(self, at, value):
        self.held[at] = value
        self.send(at)

    def __getitem__(self, at):
        return self.held[at]

    def send(self, at):
        source, target = (self.held, self.target)
        if at is not Ellipsis:
            source, target = source.at[at], target.at[at]
        self.copies.append(pltpu.make_async_copy(source, target, self.fresh()))
        self.copies[-1].start()

    def wait(self):
        for copy in self.copies:
            copy.wait()


def call(kernel, args, outs, flops, raw=0, scratch=(), direct=(), keeps=(), order=()):
    flag, *arrays = args
    n_in, n_out = len(arrays), len(outs)
    staged = [j for j in range(n_in - raw) if j not in direct]
    staged = list(order) + [j for j in staged if j not in order]
    n_held = len(staged) + n_out

    def body(flag, *refs):
        ins, results = list(refs[:n_in]), refs[n_in : n_in + n_out]
        copied = refs[n_in + n_out : n_in + n_out + len(keeps)]
        held = refs[n_in + n_out + len(keeps) :]
        own, sems = held[n_held:-1], held[-1]
        count = iter(range(SEMS))

        def fresh():
            return sems.at[next(count)]

        moves = []
        for (j, cols), target in zip(keeps, copied):
            moves.append(pltpu.make_async_copy(ins[j].at[:, cols], target, fresh()))
            moves[-1].start()
        for n, j in enumerate(staged):
            ins[j] = Loaded(ins[j], held[n], fresh())
        stored = [Stored(results[j], held[len(staged) + j], fresh) for j in range(n_out)]
        kernel(flag, *ins, *stored, *own)
        for j in staged:
            ins[j].ready()
        for item in stored + moves:
            item.wait()

    hbm = pl.BlockSpec(memory_space=pltpu.HBM)
    spaces = [pltpu.VMEM if j in direct else pltpu.HBM for j in range(n_in)]
    kept = [
        pltpu.HBM((arrays[j].shape[0], cols.stop - cols.start), arrays[j].dtype)
        for j, cols in keeps
    ]
    return pl.pallas_call(
        body,
        in_specs=[pl.BlockSpec(memory_space=pltpu.SMEM)]
        + [pl.BlockSpec(memory_space=space) for space in spaces],
        out_specs=[hbm] * (n_out + len(keeps)),
        out_shape=[pltpu.HBM(*out) for out in outs] + kept,
        scratch_shapes=[pltpu.VMEM(arrays[j].shape, arrays[j].dtype) for j in staged]
        + [pltpu.VMEM(*out) for out in outs]
        + list(scratch)
        + [pltpu.SemaphoreType.DMA((SEMS,))],
        compiler_params=pltpu.CompilerParams(vmem_limit_bytes=VMEM_BYTES),
        cost_estimate=pl.CostEstimate(flops=flops, bytes_accessed=12000000, transcendentals=50000),
    )(flag, *(pltpu.with_memory_space_constraint(x, space) for x, space in zip(arrays, spaces)))


KEPT = [
    ((64, 768), BF),
    ((64, 2304), BF),
    ((768, 64), F32),
    ((320, 1024), BF),
    ((64, 768), F32),
    ((64, 2), F32),
    ((16, 768), F32),
]


def place_kernel(first_ref, grad, idx_t, rows):
    idx_t = idx_t[...]
    hot = slot_mask_rows(idx_t[0:1, :]) + slot_mask_rows(idx_t[1:2, :])
    rows[...] = dot(hot, grad[...]).astype(BF)


def copies_kernel(first_ref, mine, theirs, copies, block_1):
    first = first_ref[0] == 1
    mine, theirs = mine[...], theirs[...]
    block = lax.select(first, mine, theirs)
    block_1[...] = lax.select(first, theirs, mine)
    for at in range(0, 64, 16):
        copies[at : at + 16] = jnp.broadcast_to(block[None], (16, 16, PACK))


def totals_block(refs, at):
    left, extra, grads, left_t, extra_t, grads_t = refs
    cols = slice(256 * at, 256 * at + 256)
    grads = jnp.concatenate([grads[...], grads_t[...]], axis=0)

    def rows(lo, hi):
        return jnp.concatenate([left[lo:hi, cols], left_t[lo:hi, cols]], axis=0)

    main = dot(rows(0, 64), grads[:, :HALF], TN)
    outs = [
        dot(rows(64 + 64 * t, 128 + 64 * t), grads[:, HALF:1536], TN) for t in range(3)
    ]
    marks = lax.broadcasted_iota(jnp.int32, (16, 128), 0) + 32 == lanes(16, 128)
    marks = ((lax.broadcasted_iota(jnp.int32, (16, 128), 0) < 3) & marks).astype(F32).astype(BF)
    rest = dot(
        jnp.concatenate([rows(256, 320), extra[:, cols], extra_t[:, cols]], axis=0),
        jnp.concatenate([grads[:, 1536:], marks, marks], axis=0),
        TN,
    )
    main = main + jnp.concatenate(outs, axis=1)
    return main.astype(BF).reshape(16, 16, HALF), rest.astype(BF).reshape(16, 16, 128)


def totals_early(flag, *refs):
    wide, narrow = refs[6:]
    for at in range(4):
        rows = slice(16 * at, 16 * at + 16)
        wide[rows], narrow[rows] = totals_block(refs[:6], at)


def totals_late(flag, *refs):
    narrow, out = refs[6:]
    for at in range(4):
        rows = slice(16 * at, 16 * at + 16)
        main, rest = totals_block(refs[:6], at)
        out[rows] = jnp.concatenate(
            [main, lax.select(flag[0] == 1, rest, narrow[rows])], axis=2
        )


def dense_totals(kernel, flag, operands, outs, more=()):
    left, left_t, extra, own_grads, other_grads = operands
    args = (flag, left, extra, own_grads, left_t, swap(extra), swap(other_grads), *more)
    return call(kernel, args, outs, 0, direct=(3, 4, 5))


def reduce_kernel(first_ref, parts_0, parts_1, mine, send, tail):
    first = first_ref[0] == 1
    parts_1 = parts_1.ready()

    def total(parts, cols, width):
        def add(j, value):
            return value + parts[j, :, cols].astype(F32)

        return lax.fori_loop(0, 64, add, jnp.zeros((16, width), F32), unroll=16)

    for at in range(0, HALF, OUT_HALF):
        cols = slice(at, at + OUT_HALF)
        sums = [total(parts, cols, OUT_HALF) for parts in (parts_0, parts_1)]
        mine[:, cols] = lax.select(first, sums[0], sums[1])
        send[:, cols] = lax.select(first, sums[1], sums[0])
    tail[...] = total(parts_0, slice(HALF, PACK), 128)


def unpack_kernel(first_ref, mine, theirs, tail, qkv, out, router, one, two, bias):
    first = first_ref[0] == 1
    halves = [
        lax.select(first, mine[...], theirs[...]),
        lax.select(first, theirs[...], mine[...]),
    ]
    qkv[...] = jnp.concatenate([block[:12, :HALF] for block in halves], axis=1).reshape(
        12, 1, 2304
    )
    row = lax.broadcasted_iota(jnp.int32, (12, 1), 0)
    wide = []
    for block in halves:
        total = jnp.zeros((12, OUT_HALF), F32)
        for j in range(4):
            for t in range(3):
                part = block[12 + j : 13 + j, OUT_HALF * t : OUT_HALF * (t + 1)]
                total = jnp.where(row == 3 * j + t, part, total)
        wide.append(total)
    out[...] = jnp.concatenate(wide, axis=1).reshape(12, 1, 768)
    rest = tail[...][:12]
    router[...] = rest[:, :32].reshape(12, 1, 32)
    on_diagonal = lax.broadcasted_iota(jnp.int32, (12, 12), 0) == lanes(12, 12)

    def row(at):
        return jnp.sum(jnp.where(on_diagonal, rest[:, at : at + 1], 0.0), axis=0, keepdims=True)

    one[...] = row(32)
    two[...] = row(33)
    bias[...] = row(34)[:, :6]


def pack_kernel(first_ref, qkv, out, router, one, two, bias, mine, send):
    first = first_ref[0] == 1
    on_diagonal = lax.broadcasted_iota(jnp.int32, (12, 12), 0) == lanes(12, 12)

    def column(ref, width):
        wide = jnp.broadcast_to(ref[...].astype(F32), (12, width))
        return jnp.sum(jnp.where(on_diagonal[:, :width], wide, 0.0), axis=1, keepdims=True)

    lane = lanes(12, 128)
    rest = jnp.concatenate([router[0].astype(F32), jnp.zeros((12, 96), F32)], axis=1)
    for at, value in ((32, column(one, 12)), (33, column(two, 12)), (34, column(bias, 6))):
        rest = jnp.where(lane == at, value, rest)
    rest = jnp.concatenate([rest, jnp.zeros((4, 128), F32)], axis=0)
    outs = out[0].astype(F32)
    blocks = []
    for half in range(2):
        cols = slice(OUT_HALF * half, OUT_HALF * (half + 1))
        thin = [
            jnp.concatenate([outs[3 * j + t : 3 * j + t + 1, cols] for j in range(4)], axis=0)
            for t in range(3)
        ]
        rows = jnp.concatenate(
            [qkv[0, :, HALF * half : HALF * (half + 1)].astype(F32), jnp.concatenate(thin, axis=1)],
            axis=0,
        )
        blocks.append(jnp.concatenate([rows, rest], axis=1).astype(BF))
    mine[...] = lax.select(first, blocks[0], blocks[1])
    send[...] = lax.select(first, blocks[1], blocks[0])


def gelu_parts(u):
    inner = 0.7978845608028654 * (u + 0.044715 * (u * u * u))
    t = jnp.tanh(inner)
    half = 0.5 * (1.0 + t)
    slope = 0.7978845608028654 * (1.0 + 3 * 0.044715 * (u * u))
    return u * half, half + 0.5 * u * (1.0 - t * t) * slope


def load_weights(chosen, mine, theirs, held, sems, order=(0, 1)):
    for cond, refs in ((chosen, mine), (jnp.logical_not(chosen), theirs)):

        @pl.when(cond)
        def _(refs=refs):
            for j in order:
                pltpu.make_async_copy(refs[j], held[j], sems.at[j]).start()

    return [pltpu.make_async_copy(mine[j], held[j], sems.at[j]) for j in range(2)]


def chunks():
    return [(n, slice(CHUNK * n, CHUNK * n + CHUNK)) for n in range(1536 // CHUNK)]


def expert_forward(flag, x, in_mine, in_theirs, out_mine, out_theirs, y, hid, slope, w1, w2, sems):
    copies = load_weights(
        flag[0] == 1, (in_mine, out_mine), (in_theirs, out_theirs), (w1, w2), sems
    )
    total = None
    for at, cols in chunks():
        if at == 0:
            copies[0].wait()
        value, grad = gelu_parts(dot(x[...], w1[:, cols]))
        value = value.astype(BF)
        hid[:, cols] = value
        slope[:, cols] = grad.astype(BF)
        if at == 0:
            copies[1].wait()
        part = dot(value, w2[cols, :])
        total = part if total is None else total + part
    y[...] = total.astype(BF)


def expert_both(
    flag, arrived, grad, in_mine, in_theirs, out_mine, out_theirs, back, hid, du, dy_out,
    w1, w2, sems,
):
    copies = load_weights(
        flag[0] == 0, (in_mine, out_mine), (in_theirs, out_theirs), (w1, w2), sems
    )
    x = arrived[:, 0:768]
    gate = jnp.sum(arrived[:, 768:896].astype(F32), axis=1, keepdims=True)
    dy = (gate * grad[...].astype(F32)).astype(BF)
    dy_out[...] = dy
    total, total_dx = None, None
    for at, cols in chunks():
        if at == 0:
            copies[0].wait()
        value, grad = gelu_parts(dot(x, w1[:, cols]))
        value = value.astype(BF)
        hid[:, cols] = value
        if at == 0:
            copies[1].wait()
        part = dot(value, w2[cols, :])
        pre = (dot(dy, w2[cols, :], NT) * grad).astype(BF)
        du[:, cols] = pre
        part_dx = dot(pre, w1[:, cols], NT)
        total = part if total is None else total + part
        total_dx = part_dx if total_dx is None else total_dx + part_dx
    back[:, 0:768] = total.astype(BF)
    back[:, 768:1536] = total_dx.astype(BF)


def expert_backward(
    flag, dy, slope, in_mine, in_theirs, out_mine, out_theirs, dx, du, w1, w2, sems
):
    copies = load_weights(
        flag[0] == 1, (in_mine, out_mine), (in_theirs, out_theirs), (w1, w2), sems, (1, 0)
    )
    total = None
    for at, cols in chunks():
        if at == 0:
            copies[1].wait()
        pre = (dot(dy[...], w2[cols, :], NT) * slope[:, cols].astype(F32)).astype(BF)
        du[:, cols] = pre
        if at == 0:
            copies[0].wait()
        part = dot(pre, w1[:, cols], NT)
        total = part if total is None else total + part
    dx[...] = total.astype(BF)


def call_expert(kernel, flag, acts, weights, outs, flops, keeps):
    return call(
        kernel,
        (flag, *acts, *weights),
        [(out, BF) for out in outs],
        flops,
        4,
        [
            pltpu.VMEM((768, 1536), BF),
            pltpu.VMEM((1536, 768), BF),
            pltpu.SemaphoreType.DMA((2,)),
        ],
        (0,),
        keeps,
    )


def body(
    inputs, cotangent, segments, routes, slots, qkv_weight, out_weight, router_weight, gain_one,
    gain_two, bias_table, w_in, w_out,
):
    section = lax.axis_index("section")
    first = section == 0

    def pick(pair):
        return jnp.where(first, pair[0], pair[1])

    def pick_other(pair):
        return jnp.where(first, pair[1], pair[0])

    e, b_rows, diagonals, flip, toeplitz = (jnp.asarray(x, BF) for x in selections())
    flag = first.astype(jnp.int32).reshape(1)
    mine, theirs = call(
        pack_kernel,
        (flag, qkv_weight, out_weight, router_weight, gain_one, gain_two, bias_table),
        [((16, PACK), BF)] * 2,
        0,
    )
    theirs = swap(theirs)
    w_in_other, w_out_other = swap(w_in[0, 0]), swap(w_out[0, 0])
    flat = routes[0] * 8 + slots[0]
    flat_mine, flat_theirs = pick(flat), swap(pick_other(flat))

    copies_0, block_1 = call(
        copies_kernel, (flag, mine, theirs), [((64, 16, PACK), BF), ((16, PACK), BF)], 0
    )
    got_0 = a2a(copies_0).reshape(1024, PACK)
    got_1 = lax.all_gather(block_1, "dp", axis=0, tiled=True)
    idx_pair = (flat_mine, flat_theirs)
    idx_0, idx_1 = pick(idx_pair), pick_other(idx_pair)

    g1 = pick(cotangent)
    seg = pick(segments)
    places = np.arange(64)
    allowed = jnp.asarray(places[:, None] >= places[None, :]) & (seg[:, None] == seg[None, :])

    allowed = allowed.astype(F32)
    grad_rows = call(place_kernel, (flag, g1, idx_1.T), [((512, 768), BF)], 50000000)[0]
    ready = (grad_rows, w_in_other, w_out_other, pick(inputs), allowed, idx_0, idx_0.T)
    got_0, ready = lax.optimization_barrier((got_0, ready))
    grad_rows, w_in_other, w_out_other, x_in, allowed, idx_0, idx_0_t = ready
    weights = (w_in[0, 0], w_in_other, w_out[0, 0], w_out_other)
    dense_0 = (got_0, swap(got_0))
    grad_rows = a2a(grad_rows.reshape(64, 8, 768)).reshape(512, 768)

    h_0, qkv_0, p_0, left_0, mid_0, gate_0, gains_0, send_0 = call(
        functools.partial(forward_kernel, entering=True),
        (flag, x_in, *dense_0, e, b_rows, toeplitz, allowed, idx_0, idx_0_t),
        KEPT + [((512, 768), BF)],
        500000000,
        direct=(1, 2),
        order=(0, 3),
    )
    send_0, grad_rows = lax.optimization_barrier((send_0, grad_rows))
    x_0 = a2a(send_0.reshape(64, 8, 768)).reshape(512, 768)
    left_0_theirs = swap(left_0)
    y_0, hid_0, slope_0, x_0 = call_expert(
        expert_forward, flag, (x_0,), weights, [(512, 768), (512, 1536), (512, 1536)],
        2500000000, ((0, WIDE),),
    )
    got_1, y_0 = lax.optimization_barrier((got_1, y_0))
    dense_1 = (got_1, swap(got_1))
    back_0 = a2a(y_0.reshape(64, 8, 768)).reshape(512, 768)

    h_1, qkv_1, p_1, left_1, mid_1, gate_1, gains_1, send_1, back_0 = call(
        functools.partial(forward_kernel, entering=False),
        (flag, mid_0, gate_0, idx_0, back_0, *dense_1, e, b_rows, toeplitz, allowed,
         idx_1, idx_1.T),
        KEPT + [((512, 896), BF)],
        700000000,
        direct=(3, 5),
        order=(0, 1, 2, 6, 4),
        keeps=((3, WIDE),),
    )
    arrived = a2a(send_1.reshape(64, 8, 896)).reshape(512, 896)
    left_1_theirs = swap(left_1)
    back_1, hid_1, du_1, dy_1, x_1 = call_expert(
        expert_both, flag, (arrived, grad_rows), weights, [(512, 1536)] * 3 + [(512, 768)],
        5000000000, ((0, WIDE),),
    )
    back_1 = a2a(back_1.reshape(64, 8, 1536)).reshape(512, 1536)
    operands = [((16, 1024), BF), ((64, 1664), BF), ((64, 1664), BF)]
    ig_1, extra_1, own_1, other_1, out_1, send_0 = call(
        functools.partial(backward_kernel, leaving=False),
        (flag, g1, back_1, idx_1, gate_1, h_1, mid_1, qkv_1, p_1, *dense_1, e, gains_1,
         b_rows, diagonals, flip, gate_0, idx_0_t),
        [((64, 768), BF)] + operands + [((64, 768), BF), ((512, 768), BF)],
        1000000000,
        direct=(1,),
        order=(0, 2, 3, 5, 10, 11, 8, 9, 7, 6),
    )

    total_1, narrow_1 = dense_totals(
        totals_early, flag, (left_1, left_1_theirs, extra_1, own_1, other_1),
        [((64, 16, HALF), BF), ((64, 16, 128), BF)],
    )

    dy_0 = a2a(send_0.reshape(64, 8, 768)).reshape(512, 768)
    dy_0, total_1 = lax.optimization_barrier((dy_0, total_1))
    dx_0, du_0, dy_0 = call_expert(
        expert_backward, flag, (dy_0, slope_0), weights, [(512, 768), (512, 1536)],
        2500000000, ((0, WIDE),),
    )
    dx_rows = a2a(dx_0.reshape(64, 8, 768)).reshape(512, 768)
    dx_rows, total_1 = lax.optimization_barrier((dx_rows, total_1))
    total_1 = a2a(total_1)
    ig_0, extra_0, own_0, other_0 = call(
        functools.partial(backward_kernel, leaving=True),
        (flag, ig_1, back_0, dx_rows, idx_0, gate_0, h_0, mid_0, qkv_0, p_0, *dense_0, e,
         gains_0, b_rows, diagonals, flip),
        [((64, 768), BF)] + operands,
        1000000000,
        direct=(2,),
        order=(0, 3, 4, 1, 6, 11, 12, 9, 10, 8, 7),
    )
    (total_0,) = dense_totals(
        totals_late, flag, (left_0, left_0_theirs, extra_0, own_0, other_0),
        [((64, 16, PACK), BF)], (narrow_1,),
    )
    total_1, total_0 = lax.optimization_barrier((total_1, total_0))
    total_0 = a2a(total_0)

    acts = [(x_0, x_1), (du_0, du_1), (hid_0, hid_1), (dy_0, dy_1)]
    xs, dus, hids, dys = [
        jnp.concatenate([pick(pair), swap(pick_other(pair))], axis=0) for pair in acts
    ]
    grad_in = dot(xs, dus, TN)
    grad_out = dot(hids, dys, TN)

    total_0, grad_in, grad_out = lax.optimization_barrier((total_0, grad_in, grad_out))
    red_mine, red_theirs, tail = call(
        reduce_kernel, (flag, total_0, total_1),
        [((16, HALF), F32)] * 2 + [((16, 128), F32)], 0, direct=(0,),
    )
    dense = call(
        unpack_kernel,
        (flag, red_mine, swap(red_theirs), tail),
        [((12, 1, 2304), F32), ((12, 1, 768), F32), ((12, 1, 32), F32)]
        + [((1, 12), F32)] * 2
        + [((1, 6), F32)],
        0,
    )

    def by_micro(values):
        own, other = pick(values), swap(pick_other(values))
        return jnp.stack([pick((own, other)), pick((other, own))])[None]

    return (
        by_micro((h_1, out_1)),
        by_micro((ig_0, ig_1)),
        *(x.transpose(1, 0, 2) for x in dense[:3]),
        *dense[3:],
        grad_in[None, None],
        grad_out[None, None],
    )


def solution(mesh):
    placed = (
        P(None, "dp", None),
        P(None, "dp", None),
        P(None, "dp"),
        P("section", None, "dp", None),
        P("section", None, "dp", None),
        P("section", "dp", None),
        P("section", "dp", None),
        P("section", "dp", None),
        P("section", "dp"),
        P("section", "dp"),
        P("section", "dp"),
        P("section", "dp", None, None),
        P("section", "dp", None, None),
    )
    return jax.shard_map(
        body,
        mesh=mesh,
        in_specs=placed,
        out_specs=(
            P("section", None, "dp", None),
            P("section", None, "dp", None),
            P("section", "dp", None),
            P("section", "dp", None),
            P("section", "dp", None),
            P("section", "dp"),
            P("section", "dp"),
            P("section", "dp"),
            P("section", "dp", None, None),
            P("section", "dp", None, None),
        ),
        check_vma=False,
    )
```
